32 devices in a mesh: dp: 2 (over core), head: 4 (over z), ffn: 4 (over y, x).
Axes of the slice: x: 2, y: 2, z: 4, core: 2. Of those that a mesh axis runs over, the one named last changes fastest.
Arguments:
- tokens: bfloat16 [12, 2048, 1024], P('dp', 'ffn', 'head'), may hold values from -6 to 6
- first_values: bfloat16 [12, 2048, 1024], P('dp', 'ffn', 'head'), may hold values from -6 to 6
- segment_ids: int32 [12, 2048], P('dp'), may hold values from 0 to 7, as said below
- cotangent: bfloat16 [12, 2048, 1024], P('dp', 'ffn', 'head'), may hold values from -6 to 6
- qkv_weight: bfloat16 [1024, 3, 1024], P(('dp', 'ffn'), None, 'head'), may hold values from -0.1875 to 0.1875
- out_weight: bfloat16 [1024, 1024], P('head', ('dp', 'ffn')), may hold values from -0.75 to 0.75
- gate_up_weight: bfloat16 [1024, 2, 2816], P(('dp', 'ffn'), None, 'head'), may hold values from -0.1875 to 0.1875
- down_weight: bfloat16 [2816, 1024], P('head', ('dp', 'ffn')), may hold values from -0.109375 to 0.109375
- attn_gain: float32 [1024], P('head'), may hold values from 0.1 to 1.9
- mlp_gain: float32 [1024], P('head'), may hold values from 0.1 to 1.9
Outputs:
- out_tokens: bfloat16 [12, 2048, 1024], P('dp', 'ffn', 'head')
- grad_tokens: bfloat16 [12, 2048, 1024], P('dp', 'ffn', 'head')
- grad_first_values: bfloat16 [12, 2048, 1024], P('dp', 'ffn', 'head')
- grad_qkv_weight: float32 [1024, 3, 1024], P(('dp', 'ffn'), None, 'head')
- grad_out_weight: float32 [1024, 1024], P('head', ('dp', 'ffn'))
- grad_gate_up_weight: float32 [1024, 2, 2816], P(('dp', 'ffn'), None, 'head')
- grad_down_weight: float32 [2816, 1024], P('head', ('dp', 'ffn'))
- grad_attn_gain: float32 [1024], P('head')
- grad_mlp_gain: float32 [1024], P('head')
The draws below stay inside these ranges and needn't reach their ends.
Inputs may be any that keep to these rules, and one draw needn't show every extreme that they name: `segment_ids`: in each sequence the numbers start at 0 and never fall; of the 6 sequences of each index of dp, one drawn from the seed is a single document, and every other sequence reaches the largest number.
All inputs are finite; a program needn't handle non-finite values.
Results may differ from the reference program's by a relative error of at most 0.024.
Values may be sent and summed in bfloat16 or wider, within the bound.
No kernel may reach another device: no remote copies, remote signals or barrier semaphores. Data moves between devices by JAX's collectives and lax.ppermute only.
A program may use at most 320 MiB of HBM per device.

```python
import math
from functools import partial
import jax
import jax.numpy as jnp
from jax import lax

D = 1024
HEADS = 16
HD = 64
FF = 2816
LEN = 2048
SEQ_DP = 6
SEQS = 12


def draw_segment_ids(key, part):
    first_key = jax.random.fold_in(key, 11)
    second_key = jax.random.fold_in(key, 12)
    third_key = jax.random.fold_in(key, 13)
    rarity = min(128, max(LEN // 8, 2))
    boundary = jax.random.randint(first_key, (SEQS, LEN), 0, rarity)
    starts = jnp.where(boundary == 0, 1, 0).astype(jnp.int32)
    positions = jnp.arange(LEN, dtype=jnp.int32)[None, :]
    eighth = LEN // 8
    forced_offset = jax.random.randint(third_key, (SEQS, 7), 0, eighth)
    forced_place = (jnp.arange(1, 8, dtype=jnp.int32)[None, :] * eighth + forced_offset)[:, :, None]
    forced_hit = jnp.sum(jnp.where(positions[:, None, :] == forced_place, 1, 0), axis=1)
    starts = jnp.where(forced_hit > 0, 1, starts)
    starts = jnp.where(positions == 0, 0, starts)
    chosen = jax.random.randint(second_key, (SEQS // SEQ_DP, 1), 0, SEQ_DP)
    row_index = jnp.arange(SEQS, dtype=jnp.int32).reshape(SEQS // SEQ_DP, SEQ_DP)
    single = (row_index % SEQ_DP == chosen).reshape(SEQS, 1)
    starts = jnp.where(single, 0, starts)
    return jnp.minimum(jnp.cumsum(starts, axis=1), 7).astype(jnp.int32)


def shard_levels(rng, shape, split, smallest, top_value):
    def one(dim, blocks):
        draws = jax.random.uniform(jax.random.fold_in(jax.random.fold_in(rng, 6), dim), (blocks,), jnp.float32, smallest / len(split), top_value / len(split))
        return jnp.repeat(jnp.exp(draws), shape[dim] // blocks).reshape((-1,) + (1,) * (len(shape) - dim - 1))

    level = one(*split[0])
    for cut in split[1:]:
        level = level * one(*cut)
    return level


def noise(key, extent, width, bound, pieces=(), kind=jnp.bfloat16):
    result = width * jax.random.normal(key, extent, jnp.float32)
    if pieces:
        result = result * shard_levels(key, extent, pieces, -0.22, 0.18)
    return jnp.clip(result, -bound, bound).astype(kind)


def setup_inputs(seed: int = 0) -> dict:
    key_of = jax.random.split(jax.random.key(seed), 11)
    tokens = noise(key_of[0], (SEQS, LEN, D), 1.0, 6.0, ((0, 2), (1, 4), (2, 4)))
    first_values = noise(key_of[1], (SEQS, LEN, HEADS * HD), 1.0, 6.0, ((0, 2), (1, 4), (2, 4)))
    segment_ids = draw_segment_ids(jax.random.fold_in(key_of[10], 71), 0)
    cotangent = noise(key_of[3], (SEQS, LEN, D), 1.0, 6.0, ((0, 2), (1, 4), (2, 4)))
    qkv_weight = noise(key_of[4], (D, 3, HEADS * HD), D ** -0.5, 0.1875, ((0, 8), (2, 4)))
    out_weight = noise(key_of[5], (HEADS * HD, D), (HEADS * HD // 16) ** -0.5, 0.75, ((0, 4), (1, 8)))
    gate_up_weight = noise(key_of[6], (D, 2, FF), D ** -0.5, 0.1875, ((0, 8), (2, 4)))
    down_weight = noise(key_of[7], (FF, D), FF ** -0.5, 0.109375, ((0, 4), (1, 8)))
    attn_gain = jnp.clip(1.0 + 0.18 * jax.random.normal(key_of[8], (D,), jnp.float32), 0.1, 1.9)
    mlp_gain = jnp.clip(1.0 + 0.18 * jax.random.normal(key_of[9], (D,), jnp.float32), 0.1, 1.9)
    return {"tokens": tokens, "first_values": first_values, "segment_ids": segment_ids, "cotangent": cotangent, "qkv_weight": qkv_weight, "out_weight": out_weight, "gate_up_weight": gate_up_weight, "down_weight": down_weight, "attn_gain": attn_gain, "mlp_gain": mlp_gain}


@jax.custom_vjp
def low(v):
    return lax.optimization_barrier(v.astype(jnp.bfloat16)).astype(jnp.float32)

@jax.custom_vjp
def low_back(v):
    return v

def low_keep(v):
    return (low(v), None)

def low_pass(kept, grad):
    return (grad,)

def back_keep(v):
    return (v, None)

def back_low(kept, grad):
    return (low(grad),)
low.defvjp(low_keep, low_pass)
low_back.defvjp(back_keep, back_low)
EPSILON = 1e-06
MASKED = -1e+30

def rope_tables(positions, head_size):
    half_size = head_size // 2
    exponent = jnp.arange(half_size, dtype=jnp.float32) * (2.0 / head_size)
    frequency = jnp.exp(exponent * -jnp.log(jnp.float32(10000.0)))
    angles = positions.astype(jnp.float32)[:, None] * frequency[None, :]
    angles = jnp.concatenate([angles, angles], axis=1)
    return (jnp.cos(angles), jnp.sin(angles))

def rotate(vectors, cos_table, sin_table):
    half_size = vectors.shape[-1] // 2
    turned = jnp.concatenate([-vectors[..., half_size:], vectors[..., :half_size]], axis=-1)
    return vectors * cos_table + turned * sin_table

def normalize(values, gain_vector):
    factor = lax.rsqrt(lax.optimization_barrier(jnp.mean(values * values, axis=-1, keepdims=True)) + EPSILON)
    return values * factor * gain_vector

def layer(params, inputs):
    qkv_matrix, out_matrix, gate_matrix, down_matrix, attn_vector, mlp_vector = params
    seq_tokens, seq_values, seq_ids = inputs
    highest = lax.Precision.HIGHEST
    normed = low(normalize(seq_tokens, attn_vector))
    projected = low_back(jnp.dot(normed, qkv_matrix.reshape(D, 3 * HEADS * HD), precision=highest))
    projected = projected.reshape(LEN, 3, HEADS, HD)
    places = jnp.arange(LEN, dtype=jnp.int32)
    cos_table, sin_table = rope_tables(places, HD)
    cos_table = cos_table[:, None, :]
    sin_table = sin_table[:, None, :]
    queries = low(rotate(projected[:, 0], cos_table, sin_table))
    keys_rot = low(rotate(projected[:, 1], cos_table, sin_table))
    mixed_values = low(0.5 * projected[:, 2] + 0.5 * seq_values.reshape(LEN, HEADS, HD))
    allowed = (places[None, :] <= places[:, None]) & (seq_ids[None, :] == seq_ids[:, None])
    scores = jnp.einsum('qhd,khd->hqk', queries, keys_rot, precision=highest) * (1.0 / math.sqrt(HD))
    scores = low_back(scores)
    scores = jnp.where(allowed[None], scores, MASKED)
    weights = low(jax.nn.softmax(scores, axis=-1))
    attended = jnp.einsum('hqk,khd->qhd', weights, mixed_values, precision=highest)
    attended = low(low_back(attended.reshape(LEN, HEADS * HD)))
    branch = low_back(jnp.dot(attended, out_matrix, precision=highest))
    hidden = seq_tokens + branch
    normed_mlp = low(normalize(hidden, mlp_vector))
    gate_up = low_back(jnp.dot(normed_mlp, gate_matrix.reshape(D, 2 * FF), precision=highest))
    gate_up = gate_up.reshape(LEN, 2, FF)
    active = low(jax.nn.silu(gate_up[:, 0]) * gate_up[:, 1])
    return hidden + jnp.dot(active, down_matrix, precision=highest)

def reference(tokens, first_values, segment_ids, cotangent, qkv_weight, out_weight, gate_up_weight, down_weight, attn_gain, mlp_gain):
    params = (qkv_weight.astype(jnp.float32), out_weight.astype(jnp.float32), gate_up_weight.astype(jnp.float32), down_weight.astype(jnp.float32), attn_gain.astype(jnp.float32), mlp_gain.astype(jnp.float32))

    def forward(layer_params, all_tokens, all_values):
        per_sequence = jax.checkpoint(partial(layer, layer_params))
        return lax.map(per_sequence, (all_tokens, all_values, segment_ids))
    outputs, pullback = jax.vjp(forward, params, tokens.astype(jnp.float32), first_values.astype(jnp.float32))
    param_grads, token_grads, value_grads = pullback(cotangent.astype(jnp.float32))
    return (outputs.astype(jnp.bfloat16), token_grads.astype(jnp.bfloat16), value_grads.astype(jnp.bfloat16), param_grads[0], param_grads[1], param_grads[2], param_grads[3], param_grads[4], param_grads[5])
```

```python
import math

import jax
import jax.numpy as jnp
from jax import lax
from jax.experimental import pallas as pl
from jax.experimental.pallas import tpu as pltpu
from jax.sharding import PartitionSpec as P

HD = 64
MICRO = 4


EPSILON = 1e-06
MASKED = -1e30


def rope_tables(positions, head_size):
    half_size = head_size // 2
    exponent = jnp.arange(half_size, dtype=jnp.float32) * (2.0 / head_size)
    frequency = jnp.exp(exponent * -jnp.log(jnp.float32(10000.0)))
    angles = positions.astype(jnp.float32)[:, None] * frequency[None, :]
    angles = jnp.concatenate([angles, angles], axis=1)
    return (jnp.cos(angles), jnp.sin(angles))


def rotate(vectors, cos_table, sin_table):
    half_size = vectors.shape[-1] // 2
    turned = jnp.concatenate([-vectors[..., half_size:], vectors[..., :half_size]], axis=-1)
    return vectors * cos_table + turned * sin_table


def unrotate(gradient, cos_table, sin_table):
    half_size = gradient.shape[-1] // 2
    scaled = gradient * sin_table
    turned = jnp.concatenate([scaled[..., half_size:], -scaled[..., :half_size]], axis=-1)
    return gradient * cos_table + turned


def swiglu(gate_up):
    return jax.nn.silu(gate_up[:, 0]) * gate_up[:, 1]


def contract_rows(former, latter):
    return lax.dot_general(
        former, latter, (((0,), (0,)), ((), ())), preferred_element_type=jnp.float32
    )


def contract_last(former, latter):
    return lax.dot_general(
        former, latter, (((1,), (1,)), ((), ())), preferred_element_type=jnp.float32
    )


def gather_weights(qkv_weight, out_weight, gate_up_weight, down_weight):
    return (
        lax.all_gather(qkv_weight, ("dp", "ffn"), axis=0, tiled=True),
        lax.all_gather(out_weight, ("dp", "ffn"), axis=1, tiled=True),
        lax.all_gather(gate_up_weight, ("dp", "ffn"), axis=0, tiled=True),
        lax.all_gather(down_weight, ("dp", "ffn"), axis=1, tiled=True),
    )


def row_total(values):
    return lax.psum(values, "head")


def spread_rows(values):
    return lax.all_gather(values, "head", axis=1, tiled=True)


def spread_grads(values):
    return lax.all_gather(values, "head", axis=1, tiled=True)


def collect_rows(values):
    return lax.psum_scatter(
        values.astype(jnp.bfloat16), "head", scatter_dimension=1, tiled=True
    ).astype(jnp.float32)


def collect_grads(values):
    return lax.psum_scatter(
        values.astype(jnp.bfloat16), "head", scatter_dimension=1, tiled=True
    ).astype(jnp.float32)


def norm_forward(values, gain_vector, full_width):
    factor = lax.rsqrt(row_total(jnp.sum(values * values, axis=1)) / full_width + EPSILON)
    return (factor, values * factor[:, None] * gain_vector)


def norm_backward(values, factor, gain_vector, gradient, full_width):
    weighted = gradient * gain_vector
    row_inner = row_total(jnp.sum(weighted * values, axis=1))
    norm_grad = (
        factor[:, None] * weighted
        - values * (factor * factor * factor * row_inner / full_width)[:, None]
    )
    gain_grad = jnp.sum(gradient * values * factor[:, None], axis=0)
    return (norm_grad, gain_grad)


def masked_scores(queries, key_rows, query_places, key_places, query_ids, key_ids, score_scale):
    scores = (
        jnp.einsum("qhd,khd->hqk", queries, key_rows, preferred_element_type=jnp.float32)
        * score_scale
    )
    allowed = (key_places[None, :] <= query_places[:, None]) & (
        key_ids[None, :] == query_ids[:, None]
    )
    return jnp.where(allowed[None], scores, MASKED)


def attend_forward(
    queries, key_rows, value_rows, query_places, key_places, query_ids, key_ids, score_scale
):
    scores = masked_scores(
        queries, key_rows, query_places, key_places, query_ids, key_ids, score_scale
    )
    highest = jnp.max(scores, axis=2, keepdims=True)
    log_total = highest + jnp.log(jnp.sum(jnp.exp(scores - highest), axis=2, keepdims=True))
    weights = jnp.exp(scores - log_total).astype(jnp.bfloat16)
    attended = jnp.einsum("hqk,khd->qhd", weights, value_rows, preferred_element_type=jnp.float32)
    return (attended, log_total[:, :, 0])


def query_side(
    queries,
    key_rows,
    value_rows,
    grad_rows,
    log_total,
    query_places,
    key_places,
    query_ids,
    key_ids,
    score_scale,
):
    scores = masked_scores(
        queries, key_rows, query_places, key_places, query_ids, key_ids, score_scale
    )
    weights = jnp.exp(scores - log_total[:, :, None])
    weight_grad = jnp.einsum(
        "qhd,khd->hqk", grad_rows, value_rows, preferred_element_type=jnp.float32
    )
    row_inner = jnp.sum(weights * weight_grad, axis=2)
    score_grad = (weights * (weight_grad - row_inner[:, :, None])).astype(jnp.bfloat16)
    query_grad = (
        jnp.einsum("hqk,khd->qhd", score_grad, key_rows, preferred_element_type=jnp.float32)
        * score_scale
    )
    return (weights, score_grad, row_inner, query_grad)


def per_device(
    tokens,
    first_values,
    segment_ids,
    cotangent,
    qkv_weight,
    out_weight,
    gate_up_weight,
    down_weight,
    attn_gain,
    mlp_gain,
):
    seq_total = tokens.shape[0]
    local_len = tokens.shape[1]
    local_width = tokens.shape[2]
    full_width = local_width * lax.axis_size("head")
    seq_len = local_len * lax.axis_size("ffn")
    head_width = first_values.shape[2]
    head_local = head_width // HD
    hidden_local = down_weight.shape[0]
    score_scale = 1.0 / math.sqrt(HD)
    offset = lax.axis_index("ffn") * local_len
    own_places = offset + jnp.arange(local_len, dtype=jnp.int32)
    all_places = jnp.arange(seq_len, dtype=jnp.int32)
    cos_table, sin_table = rope_tables(own_places, HD)
    cos_table = cos_table[:, None, :]
    sin_table = sin_table[:, None, :]
    base_count = seq_total // MICRO
    remainder = seq_total % MICRO
    qkv_grads = jnp.zeros((full_width, 3, head_width), jnp.float32)
    out_grads = jnp.zeros((head_width, full_width), jnp.float32)
    gate_grads = jnp.zeros((full_width, 2, hidden_local), jnp.float32)
    down_grads = jnp.zeros((hidden_local, full_width), jnp.float32)
    attn_gain_grads = jnp.zeros((local_width,), jnp.float32)
    mlp_gain_grads = jnp.zeros((local_width,), jnp.float32)
    outputs = []
    token_grads = []
    value_grads = []
    seq_start = 0
    for micro_index in range(MICRO):
        seq_count = base_count + (1 if micro_index < remainder else 0)
        row_count = seq_count * local_len
        gathered = gather_weights(qkv_weight, out_weight, gate_up_weight, down_weight)
        qkv_matrix = gathered[0].reshape(full_width, 3 * head_width)
        out_matrix = gathered[1]
        gate_matrix = gathered[2].reshape(full_width, 2 * hidden_local)
        down_matrix = gathered[3]
        token_rows = (
            tokens[seq_start : seq_start + seq_count]
            .reshape(row_count, local_width)
            .astype(jnp.float32)
        )
        factor_one, normed_one = norm_forward(token_rows, attn_gain, full_width)
        normed_full = spread_rows(normed_one.astype(jnp.bfloat16))
        projected = jnp.dot(normed_full, qkv_matrix, preferred_element_type=jnp.float32)
        projected = projected.reshape(seq_count, local_len, 3, head_local, HD)
        queries = rotate(projected[:, :, 0], cos_table, sin_table).astype(jnp.bfloat16)
        key_local = rotate(projected[:, :, 1], cos_table, sin_table).astype(jnp.bfloat16)
        first_block = first_values[seq_start : seq_start + seq_count].reshape(
            seq_count, local_len, head_local, HD
        )
        value_local = (0.5 * projected[:, :, 2] + 0.5 * first_block.astype(jnp.float32)).astype(
            jnp.bfloat16
        )
        key_full, value_full = (
            lax.all_gather(
                key_local.reshape(seq_count, local_len, head_width), "ffn", axis=1, tiled=True
            ),
            lax.all_gather(
                value_local.reshape(seq_count, local_len, head_width), "ffn", axis=1, tiled=True
            ),
        )
        key_full = key_full.reshape(seq_count, seq_len, head_local, HD)
        value_full = value_full.reshape(seq_count, seq_len, head_local, HD)
        ids_full = segment_ids[seq_start : seq_start + seq_count]
        ids_own = lax.dynamic_slice_in_dim(ids_full, offset, local_len, axis=1)

        def forward_one(pieces):
            return attend_forward(
                pieces[0],
                pieces[1],
                pieces[2],
                own_places,
                all_places,
                pieces[3],
                pieces[4],
                score_scale,
            )

        attended, log_totals = lax.map(
            forward_one, (queries, key_full, value_full, ids_own, ids_full)
        )
        attended_low = attended.reshape(row_count, head_width).astype(jnp.bfloat16)
        branch = collect_rows(jnp.dot(attended_low, out_matrix, preferred_element_type=jnp.float32))
        hidden = token_rows + branch
        factor_two, normed_two = norm_forward(hidden, mlp_gain, full_width)
        normed_mlp = spread_rows(normed_two.astype(jnp.bfloat16))
        gate_up = jnp.dot(normed_mlp, gate_matrix, preferred_element_type=jnp.float32).reshape(
            row_count, 2, hidden_local
        )
        active, swiglu_back = jax.vjp(swiglu, gate_up)
        active_low = active.astype(jnp.bfloat16)
        mlp_branch = collect_rows(
            jnp.dot(active_low, down_matrix, preferred_element_type=jnp.float32)
        )
        outputs.append(
            (hidden + mlp_branch).astype(jnp.bfloat16).reshape(seq_count, local_len, local_width)
        )
        grad_out = cotangent[seq_start : seq_start + seq_count].reshape(row_count, local_width)
        grad_full = spread_grads(grad_out)
        active_grad = contract_last(grad_full, down_matrix)
        down_grads = down_grads + contract_rows(active_low, grad_full)
        gate_grad = (
            swiglu_back(active_grad)[0].astype(jnp.bfloat16).reshape(row_count, 2 * hidden_local)
        )
        gate_grads = gate_grads + contract_rows(normed_mlp, gate_grad).reshape(
            full_width, 2, hidden_local
        )
        normed_grad = collect_grads(contract_last(gate_grad, gate_matrix))
        back_two, gain_two = norm_backward(hidden, factor_two, mlp_gain, normed_grad, full_width)
        mlp_gain_grads = mlp_gain_grads + gain_two
        hidden_grad = grad_out.astype(jnp.float32) + back_two
        hidden_full = spread_grads(hidden_grad.astype(jnp.bfloat16))
        attended_grad = contract_last(hidden_full, out_matrix).astype(jnp.bfloat16)
        out_grads = out_grads + contract_rows(attended_low, hidden_full)
        grad_blocks = attended_grad.reshape(seq_count, local_len, head_local, HD)

        def backward_one(pieces):
            (
                queries_one,
                key_one,
                value_one,
                grad_one,
                total_one,
                own_ids,
                full_ids,
                own_key,
                own_value,
            ) = pieces
            weights, score_grad, row_inner, query_grad = query_side(
                queries_one,
                key_one,
                value_one,
                grad_one,
                total_one,
                own_places,
                all_places,
                own_ids,
                full_ids,
                score_scale,
            )
            key_grad = (
                jnp.einsum(
                    "hqk,qhd->khd", score_grad, queries_one, preferred_element_type=jnp.float32
                )
                * score_scale
            )
            value_grad = jnp.einsum(
                "hqk,qhd->khd",
                weights.astype(jnp.bfloat16),
                grad_one,
                preferred_element_type=jnp.float32,
            )
            key_value = jnp.stack([key_grad, value_grad], axis=1).reshape(seq_len, 2, head_width)
            return (
                query_grad,
                lax.psum_scatter(
                    key_value.astype(jnp.bfloat16), "ffn", scatter_dimension=0, tiled=True
                ).astype(jnp.float32),
            )

        query_grads, key_value_grads = lax.map(
            backward_one,
            (
                queries,
                key_full,
                value_full,
                grad_blocks,
                log_totals,
                ids_own,
                ids_full,
                key_local,
                value_local,
            ),
        )
        key_rot_grad = key_value_grads[:, :, 0].reshape(seq_count, local_len, head_local, HD)
        value_mix_grad = key_value_grads[:, :, 1].reshape(seq_count, local_len, head_local, HD)
        value_grads.append(
            (0.5 * value_mix_grad).astype(jnp.bfloat16).reshape(seq_count, local_len, head_width)
        )
        projected_grad = (
            jnp.stack(
                [
                    unrotate(query_grads, cos_table, sin_table),
                    unrotate(key_rot_grad, cos_table, sin_table),
                    0.5 * value_mix_grad,
                ],
                axis=2,
            )
            .astype(jnp.bfloat16)
            .reshape(row_count, 3 * head_width)
        )
        qkv_grads = qkv_grads + contract_rows(normed_full, projected_grad).reshape(
            full_width, 3, head_width
        )
        normed_grad_one = collect_grads(contract_last(projected_grad, qkv_matrix))
        back_one, gain_one = norm_backward(
            token_rows, factor_one, attn_gain, normed_grad_one, full_width
        )
        attn_gain_grads = attn_gain_grads + gain_one
        token_grads.append(
            (hidden_grad + back_one).astype(jnp.bfloat16).reshape(seq_count, local_len, local_width)
        )
        seq_start = seq_start + seq_count
    weight_sums = (
        lax.psum_scatter(
            qkv_grads.astype(jnp.bfloat16), ("dp", "ffn"), scatter_dimension=0, tiled=True
        ).astype(jnp.float32),
        lax.psum_scatter(
            out_grads.astype(jnp.bfloat16), ("dp", "ffn"), scatter_dimension=1, tiled=True
        ).astype(jnp.float32),
        lax.psum_scatter(
            gate_grads.astype(jnp.bfloat16), ("dp", "ffn"), scatter_dimension=0, tiled=True
        ).astype(jnp.float32),
        lax.psum_scatter(
            down_grads.astype(jnp.bfloat16), ("dp", "ffn"), scatter_dimension=1, tiled=True
        ).astype(jnp.float32),
    )
    gain_sums = lax.psum((attn_gain_grads, mlp_gain_grads), ("dp", "ffn"))
    return (
        jnp.concatenate(outputs, axis=0),
        jnp.concatenate(token_grads, axis=0),
        jnp.concatenate(value_grads, axis=0),
        weight_sums[0],
        weight_sums[1],
        weight_sums[2],
        weight_sums[3],
        gain_sums[0],
        gain_sums[1],
    )


BF16 = jnp.bfloat16
F32 = jnp.float32
BQ = 256
BK = 512
MASKED_SCORE = -1e30


def matmul(former, latter):
    return lax.dot_general(former, latter, (((1,), (0,)), ((), ())), preferred_element_type=F32)


def compiler_params(mib):
    return pltpu.CompilerParams(vmem_limit_bytes=mib * 1024 * 1024)


def exchange(blocks, axes, count):
    me = lax.axis_index(axes)
    out = blocks
    for step in range(1, count):
        send = lax.dynamic_index_in_dim(blocks, me ^ step, 0, keepdims=False)
        got = lax.ppermute(send, axes, [(j, j ^ step) for j in range(count)])
        out = lax.dynamic_update_index_in_dim(out, got, me ^ step, 0)
    return out


def swap(values):
    return lax.ppermute(values, "dp", [(0, 1), (1, 0)])


def halves(turned_by, lanes):
    return (lax.broadcasted_iota(jnp.int32, (1, lanes), 1) % HD) < turned_by


def swap_halves(values):
    low = (lax.broadcasted_iota(jnp.int32, values.shape, 1) % HD) < HD // 2
    lanes = values.shape[1]
    return jnp.where(
        low, pltpu.roll(values, lanes - HD // 2, 1), pltpu.roll(values, HD // 2, 1)
    )


def norm_kernel(main_ref, shared_ref, gain_ref, main_out, shared_out):
    width = main_ref.shape[2]
    blocks = main_ref.shape[0]
    for ref, out in ((main_ref, main_out), (shared_ref, shared_out)):
        rows = ref.shape[1]
        for start in range(0, rows, 256):
            part = pl.ds(start, 256)
            values = [ref[b, part, :].astype(F32) for b in range(blocks)]
            total = sum(jnp.sum(v * v, axis=1, keepdims=True) for v in values)
            factor = lax.rsqrt(total / (width * blocks) + EPSILON)
            for b in range(blocks):
                cols = pl.ds(b * width, width)
                out[part, cols] = (values[b] * factor * gain_ref[:, cols]).astype(BF16)


def head_masks():
    lane = lax.broadcasted_iota(jnp.int32, (1, 2 * HD), 1)
    first = jnp.where(lane < HD, 1.0, 0.0).astype(BF16)
    return first, (1.0 - first.astype(F32)).astype(BF16)


def attend_kernel(
    low_ref, n_ref, w_ref, fv_ref, start_ref, cos_ref, sin_ref, q_ref, k_ref, v_ref, o_ref, lse_ref
):
    length = n_ref.shape[0]
    lanes = 2 * HD
    for begin in range(0, length, 512):
        rows = pl.ds(begin, 512)
        made = matmul(n_ref[rows, :], w_ref[...])
        cos, sin = cos_ref[rows, :], sin_ref[rows, :]
        q = made[:, :lanes]
        k = made[:, lanes : 2 * lanes]
        q_ref[rows, :] = ((q * cos + swap_halves(q) * sin) * (1.0 / math.sqrt(HD))).astype(BF16)
        k_ref[rows, :] = (k * cos + swap_halves(k) * sin).astype(BF16)
        v_ref[rows, :] = (0.5 * made[:, 2 * lanes :] + 0.5 * fv_ref[rows, :].astype(F32)).astype(
            BF16
        )
    mask_a, mask_b = head_masks()
    lane = lax.broadcasted_iota(jnp.int32, (BQ, lanes), 1)
    for i in range(length // BQ):
        rows = pl.ds(i * BQ, BQ)
        q = q_ref[rows, :]
        both = jnp.concatenate([q * mask_a, q * mask_b], axis=0)
        start = start_ref[rows, :]
        start = jnp.concatenate([start, start], axis=0)
        place = i * BQ + lax.broadcasted_iota(jnp.int32, (BQ, 1), 0)
        place = jnp.concatenate([place, place], axis=0)

        def step(j, carry):
            top, total, acc = carry
            keys = pl.ds(pl.multiple_of(j * BK, BK), BK)
            s = contract_last(both, k_ref[keys, :])
            key = j * BK + lax.broadcasted_iota(jnp.int32, s.shape, 1)
            s = jnp.where((key >= start) & (key <= place), s, MASKED_SCORE)
            new_top = jnp.maximum(top, jnp.max(s, axis=1, keepdims=True))
            p = jnp.exp(s - new_top)
            scale = jnp.exp(top - new_top)
            total = total * scale + jnp.sum(p, axis=1, keepdims=True)
            acc = acc * scale + matmul(p.astype(BF16), v_ref[keys, :])
            return new_top, total, acc

        top, total, acc = lax.fori_loop(
            low_ref[i],
            (i * BQ) // BK + 1,
            step,
            (
                jnp.full((2 * BQ, 1), MASKED_SCORE, F32),
                jnp.zeros((2 * BQ, 1), F32),
                jnp.zeros((2 * BQ, lanes), F32),
            ),
        )
        acc = acc / total
        lse = top + jnp.log(total)
        o_ref[rows, :] = jnp.where(lane < HD, acc[:BQ], acc[BQ:]).astype(BF16)
        lse_ref[rows, :] = jnp.where(
            lane < HD, jnp.broadcast_to(lse[:BQ], (BQ, lanes)), jnp.broadcast_to(lse[BQ:], (BQ, lanes))
        )


def attend(low, normed, weight, first, start_col, cos, sin):
    length = normed.shape[0]
    small = jax.ShapeDtypeStruct((length, 2 * HD), BF16)
    vmem = pl.BlockSpec(memory_space=pltpu.VMEM)
    return pl.pallas_call(
        attend_kernel,
        out_shape=(small, small, small, small, jax.ShapeDtypeStruct((length, 2 * HD), F32)),
        in_specs=[pl.BlockSpec(memory_space=pltpu.SMEM)] + [vmem] * 6,
        out_specs=(vmem,) * 5,
        compiler_params=compiler_params(48),
    )(low, normed, weight, first, start_col, cos, sin)


def attend_back_kernel(
    low_ref,
    n_ref,
    w_ref,
    q_ref,
    k_ref,
    v_ref,
    o_ref,
    lse_ref,
    do_ref,
    start_ref,
    cos_ref,
    sin_ref,
    dn_ref,
    gw_ref,
    gfv_ref,
    dq_ref,
    dk_ref,
    dv_ref,
    dp_ref,
):
    length = n_ref.shape[0]
    lanes = 2 * HD
    dk_ref[...] = jnp.zeros_like(dk_ref)
    dv_ref[...] = jnp.zeros_like(dv_ref)
    mask_a, mask_b = head_masks()
    lane = lax.broadcasted_iota(jnp.int32, (BQ, lanes), 1)
    for i in range(length // BQ):
        rows = pl.ds(i * BQ, BQ)
        q, do = q_ref[rows, :], do_ref[rows, :]
        q2 = jnp.concatenate([q * mask_a, q * mask_b], axis=0)
        do2 = jnp.concatenate([do * mask_a, do * mask_b], axis=0)
        lse = jnp.transpose(lse_ref[rows, :])
        lse = jnp.concatenate([lse[0:1, :], lse[HD : HD + 1, :]], axis=1)
        inner = jnp.transpose(do.astype(F32) * o_ref[rows, :].astype(F32))
        inner = jnp.concatenate(
            [
                jnp.sum(inner[:HD], axis=0, keepdims=True),
                jnp.sum(inner[HD:], axis=0, keepdims=True),
            ],
            axis=1,
        )
        start = start_ref[:, rows]
        start = jnp.concatenate([start, start], axis=1)
        place = i * BQ + lax.broadcasted_iota(jnp.int32, (1, BQ), 1)
        place = jnp.concatenate([place, place], axis=1)

        def step(j, acc):
            keys = pl.ds(pl.multiple_of(j * BK, BK), BK)
            k, v = k_ref[keys, :], v_ref[keys, :]
            s = contract_last(k, q2)
            key = j * BK + lax.broadcasted_iota(jnp.int32, s.shape, 0)
            s = jnp.where((key >= start) & (key <= place), s, MASKED_SCORE)
            p = jnp.exp(s - lse)
            dp = contract_last(v, do2)
            ds = (p * (dp - inner)).astype(BF16)
            dv_ref[keys, :] += matmul(p.astype(BF16), do2)
            dk_ref[keys, :] += matmul(ds, q2)
            return acc + contract_rows(ds, k)

        acc = lax.fori_loop(
            low_ref[i], (i * BQ) // BK + 1, step, jnp.zeros((2 * BQ, lanes), F32)
        )
        dq_ref[rows, :] = jnp.where(lane < HD, acc[:BQ], acc[BQ:]) * (1.0 / math.sqrt(HD))
    for begin in range(0, length, 512):
        rows = pl.ds(begin, 512)
        cos, sin = cos_ref[rows, :], sin_ref[rows, :]
        dq, dk = dq_ref[rows, :], dk_ref[rows, :]
        dv = (0.5 * dv_ref[rows, :]).astype(BF16)
        gfv_ref[rows, :] = dv
        dp_ref[rows, 0:lanes] = (dq * cos - swap_halves(dq) * sin).astype(BF16)
        dp_ref[rows, lanes : 2 * lanes] = (dk * cos - swap_halves(dk) * sin).astype(BF16)
        dp_ref[rows, 2 * lanes :] = dv
        dn_ref[rows, :] = contract_last(dp_ref[rows, :], w_ref[...]).astype(BF16)
    for begin in range(0, n_ref.shape[1], 256):
        cols = pl.ds(begin, 256)
        gw_ref[:, cols] = contract_rows(dp_ref[...], n_ref[:, cols])


def attend_back(low, normed, weight, kept, grad, start_row, cos, sin):
    length, width = normed.shape
    lanes = 2 * HD
    vmem = pl.BlockSpec(memory_space=pltpu.VMEM)
    return pl.pallas_call(
        attend_back_kernel,
        out_shape=(
            jax.ShapeDtypeStruct((length, width), BF16),
            jax.ShapeDtypeStruct((3 * lanes, width), F32),
            jax.ShapeDtypeStruct((length, lanes), BF16),
        ),
        in_specs=[pl.BlockSpec(memory_space=pltpu.SMEM)] + [vmem] * 11,
        out_specs=(vmem,) * 3,
        scratch_shapes=[
            pltpu.VMEM((length, lanes), F32),
            pltpu.VMEM((length, lanes), F32),
            pltpu.VMEM((length, lanes), F32),
            pltpu.VMEM((length, 3 * lanes), BF16),
        ],
        compiler_params=compiler_params(56),
    )(low, normed, weight, *kept, grad, start_row, cos, sin)


def fill_out_weight(wall_ref, ow_ref):
    groups, depth, high, wide = wall_ref.shape
    for g in range(groups):
        for z in range(depth):
            ow_ref[z * high : (z + 1) * high, g * wide : (g + 1) * wide] = wall_ref[g, z]


def pair_column(index, ffn_size):
    return (index % ffn_size) * 2 + index // ffn_size


def hidden_kernel(
    om_ref, os_ref, xm_ref, xs_ref, cm_ref, cs_ref, wall_ref, gain_ref,
    h_ref, n_ref, ob_ref, dy_ref, ow_ref,
):
    fill_out_weight(wall_ref, ow_ref)
    groups, lanes = om_ref.shape[0], om_ref.shape[2]
    blocks, width = xm_ref.shape[0], xm_ref.shape[2]
    base = 0
    for o, x, c in ((om_ref, xm_ref, cm_ref), (os_ref, xs_ref, cs_ref)):
        rows = x.shape[1]
        for begin in range(0, rows, 256):
            part = pl.ds(begin, 256)
            here = pl.ds(base + begin, 256)
            for g in range(groups):
                column = pair_column(g, groups // 2) * lanes
                ob_ref[here, column : column + lanes] = o[g, part, :]
            for b in range(blocks):
                dy_ref[here, b * width : (b + 1) * width] = c[b, part, :]
            branch = matmul(ob_ref[here, :], ow_ref[...])
            total = jnp.zeros((256, 1), F32)
            for b in range(blocks):
                cols = slice(b * width, (b + 1) * width)
                h = x[b, part, :].astype(F32) + branch[:, cols]
                h_ref[here, cols] = h
                total = total + jnp.sum(h * h, axis=1, keepdims=True)
            factor = lax.rsqrt(total / (width * blocks) + EPSILON)
            n_ref[here, :] = (h_ref[here, :] * factor * gain_ref[...]).astype(BF16)
        base += rows


def mlp_kernel(
    n_ref, dy_ref, wall_ref, y_ref, dn_ref, grad_ref, g_ref, d_ref, nt_ref, act_ref, dgu_ref
):
    groups, rows_in, lanes = wall_ref.shape[0], wall_ref.shape[2], wall_ref.shape[3]
    rows, width = n_ref.shape
    padded = d_ref.shape[0]
    deep = width // groups
    tiles = 2 * padded // lanes
    up_to = rows_in - (tiles * deep)
    skip = grad_ref.shape[2] - tiles * deep
    hidden = skip
    first = up_to - hidden

    @pl.when(pl.program_id(0) == 0)
    def _():
        y_ref[...] = jnp.zeros_like(y_ref)
        dn_ref[...] = jnp.zeros_like(dn_ref)
        nt_ref[...] = jnp.transpose(n_ref[...])
        d_ref[hidden:, :] = jnp.zeros((padded - hidden, width), BF16)

    for g in range(groups):
        for t in range(tiles):
            at = first + t * deep
            g_ref[g * deep : (g + 1) * deep, t * lanes : (t + 1) * lanes] = wall_ref[
                g, 0, at : at + deep, :
            ]
        at = first + tiles * deep
        d_ref[0:hidden, g * lanes : (g + 1) * lanes] = wall_ref[g, 0, at : at + hidden, :]
    for begin in range(0, rows, 256):
        part = pl.ds(begin, 256)
        gu = matmul(n_ref[part, :], g_ref[...])
        gate, up = gu[:, :padded], gu[:, padded:]
        sig = 1.0 / (1.0 + jnp.exp(-gate))
        silu = gate * sig
        act_ref[part, :] = (silu * up).astype(BF16)
        dact = contract_last(dy_ref[part, :], d_ref[...])
        dgu_ref[part, :padded] = (dact * up * sig * (1.0 + gate * (1.0 - sig))).astype(BF16)
        dgu_ref[part, padded:] = (dact * silu).astype(BF16)
        y_ref[part, :] += matmul(act_ref[part, :], d_ref[...])
        dn_ref[part, :] += contract_last(dgu_ref[part, :], g_ref[...])
    for begin in range(0, 2 * padded, 512):
        made = matmul(nt_ref[...], dgu_ref[:, begin : begin + 512]).astype(BF16)
        for g in range(groups):
            for t in range(512 // lanes):
                at = (begin // lanes + t) * deep
                grad_ref[g, 0, at : at + deep, :] = made[
                    g * deep : (g + 1) * deep, t * lanes : (t + 1) * lanes
                ]
    for begin in range(0, width, 512):
        made = contract_rows(act_ref[...], dy_ref[:, begin : begin + 512]).astype(BF16)
        for t in range(512 // lanes):
            grad_ref[begin // lanes + t, 0, tiles * deep :, :] = made[
                :hidden, t * lanes : (t + 1) * lanes
            ]


def hidden_back_kernel(
    h_ref, y_ref, dn_ref, dy_ref, ob_ref, wall_ref, gain_ref,
    outm_ref, outs_ref, dh_ref, dom_ref, dos_ref, gout_ref, ggain_ref, ow_ref, low_ref,
):
    fill_out_weight(wall_ref, ow_ref)
    groups, lanes = dom_ref.shape[0], dom_ref.shape[2]
    blocks, width = outm_ref.shape[0], outm_ref.shape[2]
    full = width * blocks
    gain = gain_ref[...]
    ggain = jnp.zeros((1, full), F32)
    base = 0
    for out, dob in ((outm_ref, dom_ref), (outs_ref, dos_ref)):
        rows = out.shape[1]
        for begin in range(0, rows, 256):
            part = pl.ds(begin, 256)
            here = pl.ds(base + begin, 256)
            h = h_ref[here, :]
            factor = lax.rsqrt(jnp.sum(h * h, axis=1, keepdims=True) / full + EPSILON)
            dn = dn_ref[here, :]
            result = (h + y_ref[here, :]).astype(BF16)
            for b in range(blocks):
                out[b, part, :] = result[:, b * width : (b + 1) * width]
            weighted = dn * gain
            ggain = ggain + jnp.sum(dn * (h * factor), axis=0, keepdims=True)
            row_inner = jnp.sum(weighted * h, axis=1, keepdims=True)
            dh = (
                dy_ref[here, :].astype(F32)
                + factor * weighted
                - h * (factor * factor * factor * row_inner / full)
            )
            dh_ref[here, :] = dh
            low_ref[here, :] = dh.astype(BF16)
            made = contract_last(low_ref[here, :], ow_ref[...]).astype(BF16)
            for g in range(groups):
                column = pair_column(g, groups // 2) * lanes
                dob[g, part, :] = made[:, column : column + lanes]
        base += rows
    ggain_ref[...] = ggain
    high, wide = gout_ref.shape[2], gout_ref.shape[3]
    for z in range(gout_ref.shape[1]):
        made = contract_rows(ob_ref[:, z * high : (z + 1) * high], low_ref[...]).astype(BF16)
        for g in range(groups):
            gout_ref[g, z] = made[:, g * wide : (g + 1) * wide]


def last_kernel(
    xm_ref, xs_ref, dh_ref, am_ref, bm_ref, as_ref, bs_ref, gain_ref,
    outm_ref, outs_ref, ggain_ref,
):
    blocks, width = xm_ref.shape[0], xm_ref.shape[2]
    full = width * blocks
    ggain_ref[...] = jnp.zeros_like(ggain_ref)
    base = 0
    for x, out, own, others in (
        (xm_ref, outm_ref, am_ref, bm_ref),
        (xs_ref, outs_ref, as_ref, bs_ref),
    ):
        rows = x.shape[1]
        for begin in range(0, rows, 256):
            part = pl.ds(begin, 256)
            here = pl.ds(base + begin, 256)
            dn = own[part, :].astype(F32)
            for other in range(others.shape[0]):
                dn = dn + others[other, part, :].astype(F32)
            weighted = dn * gain_ref[...]
            total = jnp.zeros((256, 1), F32)
            inner = jnp.zeros((256, 1), F32)
            for b in range(blocks):
                cols = slice(b * width, (b + 1) * width)
                value = x[b, part, :].astype(F32)
                total = total + jnp.sum(value * value, axis=1, keepdims=True)
                inner = inner + jnp.sum(weighted[:, cols] * value, axis=1, keepdims=True)
            factor = lax.rsqrt(total / full + EPSILON)
            slope = factor * factor * factor * inner / full
            for b in range(blocks):
                cols = slice(b * width, (b + 1) * width)
                value = x[b, part, :].astype(F32)
                ggain_ref[:, cols] += jnp.sum(dn[:, cols] * value * factor, axis=0, keepdims=True)
                out[b, part, :] = (
                    dh_ref[here, cols] + factor * weighted[:, cols] - value * slope
                ).astype(BF16)
        base += rows


def by_layers():
    def run(
        tokens,
        first_values,
        segment_ids,
        cotangent,
        qkv_weight,
        out_weight,
        gate_up_weight,
        down_weight,
        attn_gain,
        mlp_gain,
    ):
        dp, z, f = (lax.axis_index(a) for a in ("dp", "head", "ffn"))
        depth, side = lax.axis_size("head"), lax.axis_size("ffn")
        group = 2 * side
        length, width = tokens.shape[1], tokens.shape[2]
        half = length // 2
        full_width = width * depth
        seq_len = length * side
        lanes = 2 * HD
        hidden = down_weight.shape[0]
        padded = -(-hidden // lanes) * lanes
        layer = ("dp", "ffn")
        vmem = pl.BlockSpec(memory_space=pltpu.VMEM)

        def to_layers(values):
            keep = lax.dynamic_slice(values, (depth, dp * half, 0), (2, half, width))
            give = lax.dynamic_slice(values, (depth, (1 - dp) * half, 0), (2, half, width))
            got = swap(give)
            early = jnp.where(dp == 0, keep, got)
            late = jnp.where(dp == 0, got, keep)
            shared = jnp.stack([early[0], late[0], early[1], late[1]])
            return (
                exchange(values[:depth], "head", depth),
                exchange(shared, "head", depth),
            )

        def from_layers(main, shared):
            main = exchange(main, "head", depth)
            shared = exchange(shared, "head", depth)
            keep = jnp.where(dp == 0, shared[0::2], shared[1::2])
            got = swap(jnp.where(dp == 0, shared[1::2], shared[0::2]))
            early = jnp.where(dp == 0, keep, got)
            late = jnp.where(dp == 0, got, keep)
            return jnp.concatenate([main, jnp.concatenate([early, late], axis=1)], axis=0)

        def tiles(values):
            values = jnp.pad(values, ((0, 0), (0, padded - hidden)))
            return values.reshape(-1, padded // lanes, lanes).transpose(1, 0, 2).reshape(-1, lanes)

        wall = jnp.concatenate(
            [out_weight, tiles(gate_up_weight[:, 0]), tiles(gate_up_weight[:, 1]), down_weight],
            axis=0,
        )
        wall = lax.all_gather(wall, ("dp", "ffn", "head"), axis=0, tiled=False)
        wall = wall.reshape(group, depth, wall.shape[1], lanes)
        out_rows = out_weight.shape[0]

        deep = qkv_weight.shape[0]
        part = qkv_weight.reshape(deep, 3, 2, lanes).transpose(2, 1, 0, 3)
        part = exchange(jnp.broadcast_to(part[None], (depth,) + part.shape), "head", depth)
        part = part.transpose(1, 0, 2, 3, 4).reshape(group, 3, deep, lanes)
        part = exchange(part, layer, group)
        weight = part.transpose(0, 2, 1, 3).reshape(group * deep, 3 * lanes)
        gains = jnp.stack([attn_gain, mlp_gain])
        gains = exchange(jnp.broadcast_to(gains[None], (depth,) + gains.shape), "head", depth)
        gains = gains.transpose(1, 0, 2).reshape(2, 1, full_width)

        other_ids = swap(segment_ids)
        pick = depth + z // 2
        ids = [
            lax.dynamic_index_in_dim(segment_ids, z, 0, keepdims=False),
            lax.dynamic_index_in_dim(other_ids, z, 0, keepdims=False),
            jnp.where(
                z % 2 == dp,
                lax.dynamic_index_in_dim(segment_ids, pick, 0, keepdims=False),
                lax.dynamic_index_in_dim(other_ids, pick, 0, keepdims=False),
            ),
        ]
        ids = jnp.stack(ids)
        starts = jnp.sum((ids[:, None, :] < ids[:, :, None]).astype(jnp.int32), axis=2)
        lows = starts[:, ::BQ] // BK

        places = jnp.arange(seq_len, dtype=jnp.int32)
        cos, sin = rope_tables(places, HD)
        cos = jnp.concatenate([cos, cos], axis=1)
        sin = jnp.concatenate([-sin[:, : HD // 2], sin[:, HD // 2 :]], axis=1)
        sin = jnp.concatenate([sin, sin], axis=1)

        xm, xs = to_layers(tokens)
        nm, ns = pl.pallas_call(
            norm_kernel,
            out_shape=(
                jax.ShapeDtypeStruct((length, full_width), BF16),
                jax.ShapeDtypeStruct((half, full_width), BF16),
            ),
            in_specs=[vmem] * 3,
            out_specs=(vmem,) * 2,
            compiler_params=compiler_params(32),
        )(xm, xs, gains[0])

        def spread(values):
            blocks = jnp.broadcast_to(values[None], (side,) + values.shape)
            own = exchange(blocks, "ffn", side)
            return own, swap(own)

        own, other = spread(nm)
        normed = [own.reshape(seq_len, full_width), other.reshape(seq_len, full_width)]
        own, other = spread(ns)
        mixed = jnp.stack(
            [jnp.where(dp == 0, own, other), jnp.where(dp == 0, other, own)], axis=1
        )
        normed.append(mixed.reshape(seq_len, full_width))

        fm, fs = to_layers(first_values)

        def to_pairs(values):
            rows = values.shape[1]
            values = values.reshape(depth, rows, 2, lanes).transpose(2, 0, 1, 3)
            return exchange(values.reshape(group, rows, lanes), layer, group)

        def positions(main, shared):
            main = main.reshape(2, seq_len, lanes)
            shared = shared.reshape(2, side, half, lanes).transpose(1, 0, 2, 3)
            return [
                lax.dynamic_index_in_dim(main, dp, 0, keepdims=False),
                lax.dynamic_index_in_dim(main, 1 - dp, 0, keepdims=False),
                shared.reshape(seq_len, lanes),
            ]

        def owners(values):
            mine = values[0].reshape(1, side, length, lanes)
            theirs = values[1].reshape(1, side, length, lanes)
            main = jnp.where(
                dp == 0,
                jnp.concatenate([mine, theirs], axis=0),
                jnp.concatenate([theirs, mine], axis=0),
            ).reshape(group, length, lanes)
            shared = values[2].reshape(side, 2, half, lanes).transpose(1, 0, 2, 3)
            return (
                exchange(main, layer, group),
                exchange(shared.reshape(group, half, lanes), layer, group),
            )

        firsts = positions(to_pairs(fm), to_pairs(fs))
        kept = [
            attend(lows[i], normed[i], weight, firsts[i], starts[i][:, None], cos, sin)
            for i in range(3)
        ]
        om, os_ = owners([k[3] for k in kept])
        cm, cs = to_layers(cotangent)

        rows = length + half
        whole = jax.ShapeDtypeStruct((rows, full_width), F32)
        whole_low = jax.ShapeDtypeStruct((rows, full_width), BF16)
        out_spec = pl.BlockSpec((group, depth, out_rows, lanes), lambda i: (0, 0, 0, 0))

        def fixed(shape):
            return pl.BlockSpec(
                shape, lambda i: (0,) * len(shape), pipeline_mode=pl.Buffered(1)
            )

        ow_scratch = pltpu.VMEM((out_rows * depth, group * lanes), BF16)
        h, n2, ob, dy = pl.pallas_call(
            hidden_kernel,
            grid=(1,),
            out_shape=(whole, whole_low, whole_low, whole_low),
            in_specs=[fixed(a.shape) for a in (om, os_, xm, xs, cm, cs)]
            + [out_spec, fixed((1, full_width))],
            out_specs=tuple(fixed((rows, full_width)) for _ in range(4)),
            scratch_shapes=[ow_scratch],
            compiler_params=compiler_params(56),
        )(om, os_, xm, xs, cm, cs, wall, gains[1])

        high = wall.shape[2]
        grad_rows = high - out_rows
        y, dn2, grads = pl.pallas_call(
            mlp_kernel,
            grid=(depth,),
            out_shape=(
                whole,
                whole,
                jax.ShapeDtypeStruct((group, depth, grad_rows, lanes), BF16),
            ),
            in_specs=[
                fixed((rows, full_width)),
                fixed((rows, full_width)),
                pl.BlockSpec((group, 1, high, lanes), lambda i: (0, i, 0, 0)),
            ],
            out_specs=(
                fixed((rows, full_width)),
                fixed((rows, full_width)),
                pl.BlockSpec((group, 1, grad_rows, lanes), lambda i: (0, i, 0, 0)),
            ),
            scratch_shapes=[
                pltpu.VMEM((full_width, 2 * padded), BF16),
                pltpu.VMEM((padded, full_width), BF16),
                pltpu.VMEM((full_width, rows), BF16),
                pltpu.VMEM((rows, padded), BF16),
                pltpu.VMEM((rows, 2 * padded), BF16),
            ],
            compiler_params=compiler_params(60),
        )(n2, dy, wall)

        grads = grads.reshape(group * depth * grad_rows, lanes)
        grads = lax.psum_scatter(grads, layer, scatter_dimension=0, tiled=True)
        grads = lax.psum_scatter(grads, "head", scatter_dimension=0, tiled=True)

        outm, outs, dh, dom, dos, gout, gain_two = pl.pallas_call(
            hidden_back_kernel,
            grid=(1,),
            out_shape=(
                jax.ShapeDtypeStruct(xm.shape, BF16),
                jax.ShapeDtypeStruct(xs.shape, BF16),
                whole,
                jax.ShapeDtypeStruct(om.shape, BF16),
                jax.ShapeDtypeStruct(os_.shape, BF16),
                jax.ShapeDtypeStruct((group, depth, out_rows, lanes), BF16),
                jax.ShapeDtypeStruct((1, full_width), F32),
            ),
            in_specs=[fixed((rows, full_width))] * 5 + [out_spec, fixed((1, full_width))],
            out_specs=tuple(
                fixed(s)
                for s in (
                    xm.shape,
                    xs.shape,
                    (rows, full_width),
                    om.shape,
                    os_.shape,
                    (group, depth, out_rows, lanes),
                    (1, full_width),
                )
            ),
            scratch_shapes=[ow_scratch, pltpu.VMEM((rows, full_width), BF16)],
            compiler_params=compiler_params(60),
        )(h, y, dn2, dy, ob, wall, gains[1])
        out_tokens = from_layers(outm, outs)

        douts = positions(exchange(dom, layer, group), exchange(dos, layer, group))
        back = [
            attend_back(
                lows[i], normed[i], weight, kept[i], douts[i], starts[i][None], cos, sin
            )
            for i in range(3)
        ]

        gout = exchange(gout, layer, group)
        gout = jnp.sum(gout.astype(F32), axis=0).astype(BF16)
        grad_out = jnp.sum(exchange(gout, "head", depth).astype(F32), axis=0)

        gvm, gvs = owners([b[2] for b in back])

        def to_columns(values):
            rows = values.shape[1]
            values = values.reshape(2, side, rows, lanes).transpose(1, 2, 0, 3)
            return values.reshape(depth, rows, width)

        value_grads = from_layers(to_columns(gvm), to_columns(gvs))

        def summed(mine, theirs):
            chip = (mine.astype(F32) + theirs.astype(F32)).astype(BF16)
            own = lax.dynamic_index_in_dim(chip, f, 0, keepdims=False)
            got = []
            for step in range(1, side):
                send = lax.dynamic_index_in_dim(chip, f ^ step, 0, keepdims=False)
                got.append(lax.ppermute(send, "ffn", [(j, j ^ step) for j in range(side)]))
            return own, jnp.stack(got)

        dn = [b[0] for b in back]
        main_parts = summed(
            dn[0].reshape(side, length, full_width),
            swap(dn[1].reshape(side, length, full_width)),
        )
        shared = dn[2].reshape(side, 2, half, full_width)
        shared_parts = summed(
            lax.dynamic_index_in_dim(shared, dp, 1, keepdims=False),
            swap(lax.dynamic_index_in_dim(shared, 1 - dp, 1, keepdims=False)),
        )
        tokm, toks, gain_one = pl.pallas_call(
            last_kernel,
            out_shape=(
                jax.ShapeDtypeStruct(xm.shape, BF16),
                jax.ShapeDtypeStruct(xs.shape, BF16),
                jax.ShapeDtypeStruct((1, full_width), F32),
            ),
            in_specs=[vmem] * 8,
            out_specs=(vmem,) * 3,
            compiler_params=compiler_params(56),
        )(xm, xs, dh, *main_parts, *shared_parts, gains[0])
        token_grads = from_layers(tokm, toks)

        grad_w = (back[0][1] + back[1][1] + back[2][1]).astype(BF16)
        grad_w = grad_w.reshape(3, lanes, group, deep).transpose(2, 0, 3, 1)
        grad_w = exchange(grad_w, layer, group)
        grad_w = grad_w.reshape(2, side, 3, deep, lanes).transpose(1, 3, 2, 0, 4)
        grad_w = grad_w.reshape(depth, deep, 3, width)
        grad_qkv = jnp.sum(exchange(grad_w, "head", depth).astype(F32), axis=0)

        gain_sums = lax.psum(jnp.concatenate([gain_one, gain_two]), ("dp", "ffn", "head"))
        gain_sums = lax.dynamic_slice_in_dim(gain_sums, z * width, width, axis=1)

        grads = grads.astype(F32)
        count = padded // lanes * deep

        def untile(values):
            values = values.reshape(padded // lanes, deep, lanes).transpose(1, 0, 2)
            return values.reshape(deep, padded)[:, :hidden]

        grad_gate = jnp.stack([untile(grads[:count]), untile(grads[count : 2 * count])], axis=1)
        return (
            out_tokens,
            token_grads,
            value_grads,
            grad_qkv,
            grad_out,
            grad_gate,
            grads[2 * count :],
            gain_sums[0],
            gain_sums[1],
        )

    return run


def fits_layers(mesh, seqs, seq_len, full_width, heads):
    sizes = dict(mesh.shape)
    return (
        sizes["dp"] == 2
        and sizes["head"] == 4
        and sizes["ffn"] == 4
        and seqs == 12
        and seq_len % (512 * 4) == 0
        and full_width == 1024
        and heads == 16
    )


def solution(mesh):
    in_specs = (
        P("dp", "ffn", "head"),
        P("dp", "ffn", "head"),
        P("dp", None),
        P("dp", "ffn", "head"),
        P(("dp", "ffn"), None, "head"),
        P("head", ("dp", "ffn")),
        P(("dp", "ffn"), None, "head"),
        P("head", ("dp", "ffn")),
        P("head"),
        P("head"),
    )
    out_specs = (
        P("dp", "ffn", "head"),
        P("dp", "ffn", "head"),
        P("dp", "ffn", "head"),
        P(("dp", "ffn"), None, "head"),
        P("head", ("dp", "ffn")),
        P(("dp", "ffn"), None, "head"),
        P("head", ("dp", "ffn")),
        P("head"),
        P("head"),
    )

    def program(*args):
        seqs, seq_len, full_width = args[0].shape
        heads = args[5].shape[0] // HD
        fast = fits_layers(mesh, seqs, seq_len, full_width, heads)
        body = by_layers() if fast else per_device
        return jax.shard_map(
            body, mesh=mesh, in_specs=in_specs, out_specs=out_specs, check_vma=False
        )(*args)

    return program
```

```python
import functools
import math

import jax
import jax.numpy as jnp
from jax import lax
from jax.experimental import pallas as pl
from jax.experimental.pallas import tpu as pltpu
from jax.sharding import PartitionSpec as P

HD = 64
MICRO = 4


EPSILON = 1e-06
MASKED = -1e30


def rope_tables(positions, head_size):
    half_size = head_size // 2
    exponent = jnp.arange(half_size, dtype=jnp.float32) * (2.0 / head_size)
    frequency = jnp.exp(exponent * -jnp.log(jnp.float32(10000.0)))
    angles = positions.astype(jnp.float32)[:, None] * frequency[None, :]
    angles = jnp.concatenate([angles, angles], axis=1)
    return (jnp.cos(angles), jnp.sin(angles))


def rotate(vectors, cos_table, sin_table):
    half_size = vectors.shape[-1] // 2
    turned = jnp.concatenate([-vectors[..., half_size:], vectors[..., :half_size]], axis=-1)
    return vectors * cos_table + turned * sin_table


def unrotate(gradient, cos_table, sin_table):
    half_size = gradient.shape[-1] // 2
    scaled = gradient * sin_table
    turned = jnp.concatenate([scaled[..., half_size:], -scaled[..., :half_size]], axis=-1)
    return gradient * cos_table + turned


def swiglu(gate_up):
    return jax.nn.silu(gate_up[:, 0]) * gate_up[:, 1]


def contract_rows(former, latter):
    return lax.dot_general(
        former, latter, (((0,), (0,)), ((), ())), preferred_element_type=jnp.float32
    )


def contract_last(former, latter):
    return lax.dot_general(
        former, latter, (((1,), (1,)), ((), ())), preferred_element_type=jnp.float32
    )


def gather_weights(qkv_weight, out_weight, gate_up_weight, down_weight):
    return (
        lax.all_gather(qkv_weight, ("dp", "ffn"), axis=0, tiled=True),
        lax.all_gather(out_weight, ("dp", "ffn"), axis=1, tiled=True),
        lax.all_gather(gate_up_weight, ("dp", "ffn"), axis=0, tiled=True),
        lax.all_gather(down_weight, ("dp", "ffn"), axis=1, tiled=True),
    )


def row_total(values):
    return lax.psum(values, "head")


def spread_rows(values):
    return lax.all_gather(values, "head", axis=1, tiled=True)


def spread_grads(values):
    return lax.all_gather(values, "head", axis=1, tiled=True)


def collect_rows(values):
    return lax.psum_scatter(
        values.astype(jnp.bfloat16), "head", scatter_dimension=1, tiled=True
    ).astype(jnp.float32)


def collect_grads(values):
    return lax.psum_scatter(
        values.astype(jnp.bfloat16), "head", scatter_dimension=1, tiled=True
    ).astype(jnp.float32)


def norm_forward(values, gain_vector, full_width):
    factor = lax.rsqrt(row_total(jnp.sum(values * values, axis=1)) / full_width + EPSILON)
    return (factor, values * factor[:, None] * gain_vector)


def norm_backward(values, factor, gain_vector, gradient, full_width):
    weighted = gradient * gain_vector
    row_inner = row_total(jnp.sum(weighted * values, axis=1))
    norm_grad = (
        factor[:, None] * weighted
        - values * (factor * factor * factor * row_inner / full_width)[:, None]
    )
    gain_grad = jnp.sum(gradient * values * factor[:, None], axis=0)
    return (norm_grad, gain_grad)


def masked_scores(queries, key_rows, query_places, key_places, query_ids, key_ids, score_scale):
    scores = (
        jnp.einsum("qhd,khd->hqk", queries, key_rows, preferred_element_type=jnp.float32)
        * score_scale
    )
    allowed = (key_places[None, :] <= query_places[:, None]) & (
        key_ids[None, :] == query_ids[:, None]
    )
    return jnp.where(allowed[None], scores, MASKED)


def attend_forward(
    queries, key_rows, value_rows, query_places, key_places, query_ids, key_ids, score_scale
):
    scores = masked_scores(
        queries, key_rows, query_places, key_places, query_ids, key_ids, score_scale
    )
    highest = jnp.max(scores, axis=2, keepdims=True)
    log_total = highest + jnp.log(jnp.sum(jnp.exp(scores - highest), axis=2, keepdims=True))
    weights = jnp.exp(scores - log_total).astype(jnp.bfloat16)
    attended = jnp.einsum("hqk,khd->qhd", weights, value_rows, preferred_element_type=jnp.float32)
    return (attended, log_total[:, :, 0])


def query_side(
    queries,
    key_rows,
    value_rows,
    grad_rows,
    log_total,
    query_places,
    key_places,
    query_ids,
    key_ids,
    score_scale,
):
    scores = masked_scores(
        queries, key_rows, query_places, key_places, query_ids, key_ids, score_scale
    )
    weights = jnp.exp(scores - log_total[:, :, None])
    weight_grad = jnp.einsum(
        "qhd,khd->hqk", grad_rows, value_rows, preferred_element_type=jnp.float32
    )
    row_inner = jnp.sum(weights * weight_grad, axis=2)
    score_grad = (weights * (weight_grad - row_inner[:, :, None])).astype(jnp.bfloat16)
    query_grad = (
        jnp.einsum("hqk,khd->qhd", score_grad, key_rows, preferred_element_type=jnp.float32)
        * score_scale
    )
    return (weights, score_grad, row_inner, query_grad)


def per_device(
    tokens,
    first_values,
    segment_ids,
    cotangent,
    qkv_weight,
    out_weight,
    gate_up_weight,
    down_weight,
    attn_gain,
    mlp_gain,
):
    seq_total = tokens.shape[0]
    local_len = tokens.shape[1]
    local_width = tokens.shape[2]
    full_width = local_width * lax.axis_size("head")
    seq_len = local_len * lax.axis_size("ffn")
    head_width = first_values.shape[2]
    head_local = head_width // HD
    hidden_local = down_weight.shape[0]
    score_scale = 1.0 / math.sqrt(HD)
    offset = lax.axis_index("ffn") * local_len
    own_places = offset + jnp.arange(local_len, dtype=jnp.int32)
    all_places = jnp.arange(seq_len, dtype=jnp.int32)
    cos_table, sin_table = rope_tables(own_places, HD)
    cos_table = cos_table[:, None, :]
    sin_table = sin_table[:, None, :]
    base_count = seq_total // MICRO
    remainder = seq_total % MICRO
    qkv_grads = jnp.zeros((full_width, 3, head_width), jnp.float32)
    out_grads = jnp.zeros((head_width, full_width), jnp.float32)
    gate_grads = jnp.zeros((full_width, 2, hidden_local), jnp.float32)
    down_grads = jnp.zeros((hidden_local, full_width), jnp.float32)
    attn_gain_grads = jnp.zeros((local_width,), jnp.float32)
    mlp_gain_grads = jnp.zeros((local_width,), jnp.float32)
    outputs = []
    token_grads = []
    value_grads = []
    seq_start = 0
    for micro_index in range(MICRO):
        seq_count = base_count + (1 if micro_index < remainder else 0)
        row_count = seq_count * local_len
        gathered = gather_weights(qkv_weight, out_weight, gate_up_weight, down_weight)
        qkv_matrix = gathered[0].reshape(full_width, 3 * head_width)
        out_matrix = gathered[1]
        gate_matrix = gathered[2].reshape(full_width, 2 * hidden_local)
        down_matrix = gathered[3]
        token_rows = (
            tokens[seq_start : seq_start + seq_count]
            .reshape(row_count, local_width)
            .astype(jnp.float32)
        )
        factor_one, normed_one = norm_forward(token_rows, attn_gain, full_width)
        normed_full = spread_rows(normed_one.astype(jnp.bfloat16))
        projected = jnp.dot(normed_full, qkv_matrix, preferred_element_type=jnp.float32)
        projected = projected.reshape(seq_count, local_len, 3, head_local, HD)
        queries = rotate(projected[:, :, 0], cos_table, sin_table).astype(jnp.bfloat16)
        key_local = rotate(projected[:, :, 1], cos_table, sin_table).astype(jnp.bfloat16)
        first_block = first_values[seq_start : seq_start + seq_count].reshape(
            seq_count, local_len, head_local, HD
        )
        value_local = (0.5 * projected[:, :, 2] + 0.5 * first_block.astype(jnp.float32)).astype(
            jnp.bfloat16
        )
        key_full, value_full = (
            lax.all_gather(
                key_local.reshape(seq_count, local_len, head_width), "ffn", axis=1, tiled=True
            ),
            lax.all_gather(
                value_local.reshape(seq_count, local_len, head_width), "ffn", axis=1, tiled=True
            ),
        )
        key_full = key_full.reshape(seq_count, seq_len, head_local, HD)
        value_full = value_full.reshape(seq_count, seq_len, head_local, HD)
        ids_full = segment_ids[seq_start : seq_start + seq_count]
        ids_own = lax.dynamic_slice_in_dim(ids_full, offset, local_len, axis=1)

        def forward_one(pieces):
            return attend_forward(
                pieces[0],
                pieces[1],
                pieces[2],
                own_places,
                all_places,
                pieces[3],
                pieces[4],
                score_scale,
            )

        attended, log_totals = lax.map(
            forward_one, (queries, key_full, value_full, ids_own, ids_full)
        )
        attended_low = attended.reshape(row_count, head_width).astype(jnp.bfloat16)
        branch = collect_rows(jnp.dot(attended_low, out_matrix, preferred_element_type=jnp.float32))
        hidden = token_rows + branch
        factor_two, normed_two = norm_forward(hidden, mlp_gain, full_width)
        normed_mlp = spread_rows(normed_two.astype(jnp.bfloat16))
        gate_up = jnp.dot(normed_mlp, gate_matrix, preferred_element_type=jnp.float32).reshape(
            row_count, 2, hidden_local
        )
        active, swiglu_back = jax.vjp(swiglu, gate_up)
        active_low = active.astype(jnp.bfloat16)
        mlp_branch = collect_rows(
            jnp.dot(active_low, down_matrix, preferred_element_type=jnp.float32)
        )
        outputs.append(
            (hidden + mlp_branch).astype(jnp.bfloat16).reshape(seq_count, local_len, local_width)
        )
        grad_out = cotangent[seq_start : seq_start + seq_count].reshape(row_count, local_width)
        grad_full = spread_grads(grad_out)
        active_grad = contract_last(grad_full, down_matrix)
        down_grads = down_grads + contract_rows(active_low, grad_full)
        gate_grad = (
            swiglu_back(active_grad)[0].astype(jnp.bfloat16).reshape(row_count, 2 * hidden_local)
        )
        gate_grads = gate_grads + contract_rows(normed_mlp, gate_grad).reshape(
            full_width, 2, hidden_local
        )
        normed_grad = collect_grads(contract_last(gate_grad, gate_matrix))
        back_two, gain_two = norm_backward(hidden, factor_two, mlp_gain, normed_grad, full_width)
        mlp_gain_grads = mlp_gain_grads + gain_two
        hidden_grad = grad_out.astype(jnp.float32) + back_two
        hidden_full = spread_grads(hidden_grad.astype(jnp.bfloat16))
        attended_grad = contract_last(hidden_full, out_matrix).astype(jnp.bfloat16)
        out_grads = out_grads + contract_rows(attended_low, hidden_full)
        grad_blocks = attended_grad.reshape(seq_count, local_len, head_local, HD)

        def backward_one(pieces):
            (
                queries_one,
                key_one,
                value_one,
                grad_one,
                total_one,
                own_ids,
                full_ids,
                own_key,
                own_value,
            ) = pieces
            weights, score_grad, row_inner, query_grad = query_side(
                queries_one,
                key_one,
                value_one,
                grad_one,
                total_one,
                own_places,
                all_places,
                own_ids,
                full_ids,
                score_scale,
            )
            key_grad = (
                jnp.einsum(
                    "hqk,qhd->khd", score_grad, queries_one, preferred_element_type=jnp.float32
                )
                * score_scale
            )
            value_grad = jnp.einsum(
                "hqk,qhd->khd",
                weights.astype(jnp.bfloat16),
                grad_one,
                preferred_element_type=jnp.float32,
            )
            key_value = jnp.stack([key_grad, value_grad], axis=1).reshape(seq_len, 2, head_width)
            return (
                query_grad,
                lax.psum_scatter(
                    key_value.astype(jnp.bfloat16), "ffn", scatter_dimension=0, tiled=True
                ).astype(jnp.float32),
            )

        query_grads, key_value_grads = lax.map(
            backward_one,
            (
                queries,
                key_full,
                value_full,
                grad_blocks,
                log_totals,
                ids_own,
                ids_full,
                key_local,
                value_local,
            ),
        )
        key_rot_grad = key_value_grads[:, :, 0].reshape(seq_count, local_len, head_local, HD)
        value_mix_grad = key_value_grads[:, :, 1].reshape(seq_count, local_len, head_local, HD)
        value_grads.append(
            (0.5 * value_mix_grad).astype(jnp.bfloat16).reshape(seq_count, local_len, head_width)
        )
        projected_grad = (
            jnp.stack(
                [
                    unrotate(query_grads, cos_table, sin_table),
                    unrotate(key_rot_grad, cos_table, sin_table),
                    0.5 * value_mix_grad,
                ],
                axis=2,
            )
            .astype(jnp.bfloat16)
            .reshape(row_count, 3 * head_width)
        )
        qkv_grads = qkv_grads + contract_rows(normed_full, projected_grad).reshape(
            full_width, 3, head_width
        )
        normed_grad_one = collect_grads(contract_last(projected_grad, qkv_matrix))
        back_one, gain_one = norm_backward(
            token_rows, factor_one, attn_gain, normed_grad_one, full_width
        )
        attn_gain_grads = attn_gain_grads + gain_one
        token_grads.append(
            (hidden_grad + back_one).astype(jnp.bfloat16).reshape(seq_count, local_len, local_width)
        )
        seq_start = seq_start + seq_count
    weight_sums = (
        lax.psum_scatter(
            qkv_grads.astype(jnp.bfloat16), ("dp", "ffn"), scatter_dimension=0, tiled=True
        ).astype(jnp.float32),
        lax.psum_scatter(
            out_grads.astype(jnp.bfloat16), ("dp", "ffn"), scatter_dimension=1, tiled=True
        ).astype(jnp.float32),
        lax.psum_scatter(
            gate_grads.astype(jnp.bfloat16), ("dp", "ffn"), scatter_dimension=0, tiled=True
        ).astype(jnp.float32),
        lax.psum_scatter(
            down_grads.astype(jnp.bfloat16), ("dp", "ffn"), scatter_dimension=1, tiled=True
        ).astype(jnp.float32),
    )
    gain_sums = lax.psum((attn_gain_grads, mlp_gain_grads), ("dp", "ffn"))
    return (
        jnp.concatenate(outputs, axis=0),
        jnp.concatenate(token_grads, axis=0),
        jnp.concatenate(value_grads, axis=0),
        weight_sums[0],
        weight_sums[1],
        weight_sums[2],
        weight_sums[3],
        gain_sums[0],
        gain_sums[1],
    )


BF16 = jnp.bfloat16
F32 = jnp.float32
BQ = 512
BK = 512
MASKED_SCORE = -1e30


def matmul(former, latter):
    return lax.dot_general(former, latter, (((1,), (0,)), ((), ())), preferred_element_type=F32)


def compiler_params(mib):
    return pltpu.CompilerParams(vmem_limit_bytes=mib * 1024 * 1024)


def exchange(blocks, axes):
    return lax.all_to_all(blocks, axes, 0, 0, tiled=True)


def send_line(blocks, axis="head"):
    count = blocks.shape[0]
    me = lax.axis_index(axis)
    got = []
    for step in range(1, count):
        send = lax.dynamic_index_in_dim(blocks, me ^ step, 0, keepdims=False)
        got.append(lax.ppermute(send, axis, [(j, j ^ step) for j in range(count)]))
    return blocks, got


def join_line(blocks, got, axis="head"):
    me = lax.axis_index(axis)
    got = after(*got)
    for step, piece in enumerate(got):
        blocks = lax.dynamic_update_index_in_dim(blocks, piece, me ^ (step + 1), 0)
    return blocks


def exchange_line(blocks, axis="head"):
    return join_line(*send_line(blocks, axis), axis)


def after(values, *earlier):
    return lax.optimization_barrier((values, *earlier))


def send_across(blocks):
    count = blocks.shape[0]
    me = lax.axis_index("ffn")
    got = []
    for step in range(count):
        pairs = []
        for j in range(count * count):
            h, f = divmod(j, count)
            pairs.append((j, (f ^ step) * count + h))
        send = lax.dynamic_index_in_dim(blocks, me ^ step, 0, keepdims=False)
        got.append(lax.ppermute(send, ("head", "ffn"), pairs))
    return got


def join_across(got):
    here = lax.axis_index("head")
    a, b, c, d = after(*got)
    return jnp.where(
        here % 2 == 0,
        jnp.where(here < 2, jnp.stack([a, b, c, d]), jnp.stack([c, d, a, b])),
        jnp.where(here < 2, jnp.stack([b, a, d, c]), jnp.stack([d, c, b, a])),
    )


def swap(values):
    return lax.ppermute(values, "dp", [(0, 1), (1, 0)])


def swap_halves(values):
    low = (lax.broadcasted_iota(jnp.int32, values.shape, 1) % HD) < HD // 2
    lanes = values.shape[1]
    return jnp.where(
        low, pltpu.roll(values, lanes - HD // 2, 1), pltpu.roll(values, HD // 2, 1)
    )


def norm_kernel(x_ref, gain_ref, main_ref, shared_ref):
    blocks, rows, width = x_ref.shape
    for start in range(0, rows, 256):
        part = pl.ds(start, 256)
        values = [x_ref[b, part, :].astype(F32) for b in range(blocks)]
        total = sum(jnp.sum(v * v, axis=1, keepdims=True) for v in values)
        factor = lax.rsqrt(total / (width * blocks) + EPSILON)
        out_ref, base = main_ref, 0
        if start >= main_ref.shape[1]:
            out_ref, base = shared_ref, main_ref.shape[1]
        for b in range(blocks):
            cols = pl.ds(b * width, width)
            normed = (values[b] * factor * gain_ref[:, cols]).astype(BF16)
            for copy in range(out_ref.shape[0]):
                out_ref[copy, start - base : start - base + 256, cols] = normed


def normalized(x, gain, copies, length):
    shapes = [(copies, r, gain.shape[1]) for r in (length, x.shape[1] - length)]
    return pl.pallas_call(
        norm_kernel,
        grid=(1,),
        out_shape=tuple(jax.ShapeDtypeStruct(s, BF16) for s in shapes),
        in_specs=[once(x.shape), once(gain.shape)],
        out_specs=tuple(once(s) for s in shapes),
        compiler_params=compiler_params(48),
    )(x, gain)


def head_masks():
    lane = lax.broadcasted_iota(jnp.int32, (1, 2 * HD), 1)
    first = jnp.where(lane < HD, 1.0, 0.0).astype(BF16)
    return first, (1.0 - first.astype(F32)).astype(BF16)


def row_chunks(refs, side_ref):
    rows = refs[0].shape[1]
    chunks = []
    for number, ref in enumerate(refs):
        for block in range(ref.shape[0]):
            at = block * rows * len(refs)
            if len(refs) == 2:
                half = side_ref[0] if number == 0 else 1 - side_ref[0]
                at = pl.multiple_of(at + half * rows, rows)
            chunks.append((number, block, pl.ds(at, rows)))
    return chunks


def attend_kernel(count, side_ref, low_ref, *refs):
    n_refs, fv_refs = refs[:count], refs[count : 2 * count]
    w_ref, start_ref, cos_ref, sin_ref, q_ref, k_ref, v_ref, o_ref, lse_ref = refs[2 * count :]
    length = q_ref.shape[0]
    lanes = 2 * HD
    for number, block, rows in row_chunks(n_refs, side_ref):
        made = matmul(n_refs[number][block], w_ref[...])
        cos, sin = cos_ref[rows, :], sin_ref[rows, :]
        q = made[:, :lanes]
        k = made[:, lanes : 2 * lanes]
        q_ref[rows, :] = ((q * cos + swap_halves(q) * sin) * (1.0 / math.sqrt(HD))).astype(BF16)
        k_ref[rows, :] = (k * cos + swap_halves(k) * sin).astype(BF16)
        first = fv_refs[number][block].astype(F32)
        v_ref[rows, :] = (0.5 * made[:, 2 * lanes :] + 0.5 * first).astype(BF16)
    mask_a, mask_b = head_masks()
    lane = lax.broadcasted_iota(jnp.int32, (BQ, lanes), 1)
    for i in range(length // BQ):
        rows = pl.ds(i * BQ, BQ)
        q = q_ref[rows, :]
        both = jnp.concatenate([q * mask_a, q * mask_b], axis=0)
        start = start_ref[rows, :]
        start = jnp.concatenate([start, start], axis=0)
        place = i * BQ + lax.broadcasted_iota(jnp.int32, (BQ, 1), 0)
        place = jnp.concatenate([place, place], axis=0)

        def step(j, carry):
            top, total, acc = carry
            keys = pl.ds(pl.multiple_of(j * BK, BK), BK)
            s = contract_last(both, k_ref[keys, :])
            key = j * BK + lax.broadcasted_iota(jnp.int32, s.shape, 1)
            s = jnp.where((key >= start) & (key <= place), s, MASKED_SCORE)
            new_top = jnp.maximum(top, jnp.max(s, axis=1, keepdims=True))
            p = jnp.exp(s - new_top)
            scale = jnp.exp(top - new_top)
            total = total * scale + jnp.sum(p, axis=1, keepdims=True)
            acc = acc * scale + matmul(p.astype(BF16), v_ref[keys, :])
            return new_top, total, acc

        top, total, acc = lax.fori_loop(
            low_ref[i],
            (i * BQ + BQ - 1) // BK + 1,
            step,
            (
                jnp.full((2 * BQ, 1), MASKED_SCORE, F32),
                jnp.zeros((2 * BQ, 1), F32),
                jnp.zeros((2 * BQ, lanes), F32),
            ),
        )
        acc = acc / total
        lse = top + jnp.log(total)
        o_ref[rows, :] = jnp.where(lane < HD, acc[:BQ], acc[BQ:]).astype(BF16)
        lse_ref[rows, :] = jnp.where(
            lane < HD, jnp.broadcast_to(lse[:BQ], (BQ, lanes)), jnp.broadcast_to(lse[BQ:], (BQ, lanes))
        )


def once(shape, index=None):
    index = (0,) * len(shape) if index is None else index
    return pl.BlockSpec(shape, lambda i: index, pipeline_mode=pl.Buffered(1))


def attend(side, low, normed, weight, firsts, begin, start_col, cos, sin):
    count = len(normed)
    blocks, rows, _ = normed[0].shape
    length = start_col.shape[0]
    lanes = 2 * HD
    small = jax.ShapeDtypeStruct((length, lanes), BF16)
    scalar = pl.BlockSpec(memory_space=pltpu.SMEM)
    return pl.pallas_call(
        functools.partial(attend_kernel, count),
        grid=(1,),
        out_shape=(small, small, small, small, jax.ShapeDtypeStruct((length, lanes), F32)),
        in_specs=[scalar, scalar]
        + [once(n.shape) for n in normed]
        + [once((blocks, rows, lanes), (0, begin // rows, 0))] * count
        + [once(a.shape) for a in (weight, start_col, cos, sin)],
        out_specs=(once((length, lanes)),) * 5,
        compiler_params=compiler_params(48),
    )(side, low, *normed, *firsts, weight, start_col, cos, sin)


def attend_back_kernel(count, side_ref, low_ref, *refs):
    n_refs, do_refs = refs[:count], refs[count : 2 * count]
    w_ref, q_ref, k_ref, v_ref, o_ref, lse_ref, start_ref, cos_ref, sin_ref = refs[
        2 * count : 2 * count + 9
    ]
    dn_refs = refs[2 * count + 9 : 3 * count + 9]
    gw_ref, gfv_ref, dq_ref, dk_ref, dv_ref, dp_ref, do_ref = refs[3 * count + 9 :]
    length = q_ref.shape[0]
    lanes = 2 * HD
    chunks = row_chunks(n_refs, side_ref)
    for number, block, rows in chunks:
        do_ref[rows, :] = do_refs[number][block]
    dk_ref[...] = jnp.zeros_like(dk_ref)
    dv_ref[...] = jnp.zeros_like(dv_ref)
    mask_a, mask_b = head_masks()
    lane = lax.broadcasted_iota(jnp.int32, (BQ, lanes), 1)
    for i in range(length // BQ):
        rows = pl.ds(i * BQ, BQ)
        q, do = q_ref[rows, :], do_ref[rows, :]
        q2 = jnp.concatenate([q * mask_a, q * mask_b], axis=0)
        do2 = jnp.concatenate([do * mask_a, do * mask_b], axis=0)
        lse = jnp.transpose(lse_ref[rows, :])
        lse = jnp.concatenate([lse[0:1, :], lse[HD : HD + 1, :]], axis=1)
        inner = jnp.transpose(do.astype(F32) * o_ref[rows, :].astype(F32))
        inner = jnp.concatenate(
            [
                jnp.sum(inner[:HD], axis=0, keepdims=True),
                jnp.sum(inner[HD:], axis=0, keepdims=True),
            ],
            axis=1,
        )
        start = start_ref[:, rows]
        start = jnp.concatenate([start, start], axis=1)
        place = i * BQ + lax.broadcasted_iota(jnp.int32, (1, BQ), 1)
        place = jnp.concatenate([place, place], axis=1)

        def step(j, acc):
            keys = pl.ds(pl.multiple_of(j * BK, BK), BK)
            k, v = k_ref[keys, :], v_ref[keys, :]
            s = contract_last(k, q2)
            key = j * BK + lax.broadcasted_iota(jnp.int32, s.shape, 0)
            s = jnp.where((key >= start) & (key <= place), s, MASKED_SCORE)
            p = jnp.exp(s - lse)
            dp = contract_last(v, do2)
            ds = (p * (dp - inner)).astype(BF16)
            dv_ref[keys, :] += matmul(p.astype(BF16), do2)
            dk_ref[keys, :] += matmul(ds, q2)
            return acc + contract_rows(ds, k)

        acc = lax.fori_loop(
            low_ref[i], (i * BQ + BQ - 1) // BK + 1, step, jnp.zeros((2 * BQ, lanes), F32)
        )
        dq_ref[rows, :] = jnp.where(lane < HD, acc[:BQ], acc[BQ:]) * (1.0 / math.sqrt(HD))
    for begin in range(0, length, 512):
        rows = pl.ds(begin, 512)
        cos, sin = cos_ref[rows, :], sin_ref[rows, :]
        dq, dk = dq_ref[rows, :], dk_ref[rows, :]
        dv = (0.5 * dv_ref[rows, :]).astype(BF16)
        gfv_ref[rows, :] = dv
        dp_ref[rows, 0:lanes] = (dq * cos - swap_halves(dq) * sin).astype(BF16)
        dp_ref[rows, lanes : 2 * lanes] = (dk * cos - swap_halves(dk) * sin).astype(BF16)
        dp_ref[rows, 2 * lanes :] = dv
    for number, block, rows in chunks:
        part = dp_ref[rows, :]
        dn_refs[number][block] = contract_last(part, w_ref[...]).astype(BF16)
        made = contract_rows(part, n_refs[number][block])
        if number + block == 0:
            gw_ref[...] = made
        else:
            gw_ref[...] += made


def attend_back(side, low, normed, weight, kept, grads, begin, start_row, cos, sin):
    count = len(normed)
    blocks, rows, width = normed[0].shape
    length = start_row.shape[1]
    lanes = 2 * HD
    scalar = pl.BlockSpec(memory_space=pltpu.SMEM)
    return pl.pallas_call(
        functools.partial(attend_back_kernel, count),
        grid=(1,),
        out_shape=tuple(jax.ShapeDtypeStruct(n.shape, BF16) for n in normed)
        + (
            jax.ShapeDtypeStruct((3 * lanes, width), F32),
            jax.ShapeDtypeStruct((length, lanes), BF16),
        ),
        in_specs=[scalar, scalar]
        + [once(n.shape) for n in normed]
        + [once((blocks, rows, lanes), (0, begin // rows, 0))] * count
        + [once(a.shape) for a in (weight, *kept, start_row, cos, sin)],
        out_specs=tuple(once(n.shape) for n in normed)
        + (once((3 * lanes, width)), once((length, lanes))),
        scratch_shapes=[
            pltpu.VMEM((length, lanes), F32),
            pltpu.VMEM((length, lanes), F32),
            pltpu.VMEM((length, lanes), F32),
            pltpu.VMEM((length, 3 * lanes), BF16),
            pltpu.VMEM((length, lanes), BF16),
        ],
        compiler_params=compiler_params(56),
    )(side, low, *normed, *grads, weight, *kept, start_row, cos, sin)


def fill_out_weight(wall_ref, ow_ref):
    groups, depth, high, wide = wall_ref.shape
    for g in range(groups):
        for z in range(depth):
            ow_ref[z * high : (z + 1) * high, g * wide : (g + 1) * wide] = wall_ref[g, z]


def hidden_kernel(
    om_ref, os_ref, x_ref, wall_ref, gain_ref,
    h_ref, n_ref, ob_ref, ow_ref,
):
    fill_out_weight(wall_ref, ow_ref)
    blocks, width = x_ref.shape[0], x_ref.shape[2]
    base = 0
    for o in (om_ref, os_ref):
        rows = o.shape[1]
        for begin in range(0, rows, 256):
            part = pl.ds(begin, 256)
            here = pl.ds(base + begin, 256)
            for b in range(blocks):
                ob_ref[here, b * width : (b + 1) * width] = o[b, part, :]
            branch = matmul(ob_ref[here, :], ow_ref[...])
            total = jnp.zeros((256, 1), F32)
            for b in range(blocks):
                cols = slice(b * width, (b + 1) * width)
                h = x_ref[b, here, :].astype(F32) + branch[:, cols]
                h_ref[here, cols] = h
                total = total + jnp.sum(h * h, axis=1, keepdims=True)
            factor = lax.rsqrt(total / (width * blocks) + EPSILON)
            n_ref[here, :] = (h_ref[here, :] * factor * gain_ref[...]).astype(BF16)
        base += rows


def mlp_kernel(
    begin_tile, hidden, first, down_first,
    n_ref, c_ref, wall_ref, y_ref, dn_ref, grad_ref,
    g_ref, d_ref, nt_ref, act_ref, dgu_ref, dy_ref,
):
    groups, lanes = wall_ref.shape[0], wall_ref.shape[3]
    rows, width = n_ref.shape
    padded = d_ref.shape[0]
    deep = width // groups
    tiles = 2 * padded // lanes
    all_tiles = (down_first - first) // deep // 2

    @pl.when(pl.program_id(0) == 0)
    def _():
        y_ref[...] = jnp.zeros_like(y_ref)
        dn_ref[...] = jnp.zeros_like(dn_ref)
        nt_ref[...] = jnp.transpose(n_ref[...])
        for b in range(c_ref.shape[0]):
            part = c_ref.shape[2]
            dy_ref[:, b * part : (b + 1) * part] = c_ref[b]
        if padded > hidden:
            d_ref[hidden:, :] = jnp.zeros((padded - hidden, width), BF16)

    for g in range(groups):
        for t in range(tiles):
            column = begin_tile + t
            if t >= tiles // 2:
                column += all_tiles - tiles // 2
            at = first + column * deep
            g_ref[g * deep : (g + 1) * deep, t * lanes : (t + 1) * lanes] = wall_ref[
                g, 0, at : at + deep, :
            ]
        at = down_first + begin_tile * lanes
        d_ref[0:hidden, g * lanes : (g + 1) * lanes] = wall_ref[g, 0, at : at + hidden, :]
    for begin in range(0, rows, 256):
        part = pl.ds(begin, 256)
        gu = matmul(n_ref[part, :], g_ref[...])
        gate, up = gu[:, :padded], gu[:, padded:]
        sig = 1.0 / (1.0 + jnp.exp(-gate))
        silu = gate * sig
        act_ref[part, :] = (silu * up).astype(BF16)
        dact = contract_last(dy_ref[part, :], d_ref[...])
        dgu_ref[part, :padded] = (dact * up * sig * (1.0 + gate * (1.0 - sig))).astype(BF16)
        dgu_ref[part, padded:] = (dact * silu).astype(BF16)
        y_ref[part, :] += matmul(act_ref[part, :], d_ref[...])
        dn_ref[part, :] += contract_last(dgu_ref[part, :], g_ref[...])
    for begin in range(0, 2 * padded, 512):
        made = matmul(nt_ref[...], dgu_ref[:, begin : begin + 512]).astype(BF16)
        for g in range(groups):
            for t in range(512 // lanes):
                at = (begin // lanes + t) * deep
                grad_ref[g, 0, at : at + deep, :] = made[
                    g * deep : (g + 1) * deep, t * lanes : (t + 1) * lanes
                ]
    for begin in range(0, width, 512):
        made = contract_rows(act_ref[...], dy_ref[:, begin : begin + 512]).astype(BF16)
        for t in range(512 // lanes):
            grad_ref[begin // lanes + t, 0, tiles * deep :, :] = made[
                :hidden, t * lanes : (t + 1) * lanes
            ]


def hidden_back_kernel(
    h_ref, ya_ref, yb_ref, dna_ref, dnb_ref, ob_ref, c_ref, wall_ref, gain_ref,
    out_ref, dh_ref, dob_ref, gout_ref, ggain_ref, ow_ref, low_ref,
):
    fill_out_weight(wall_ref, ow_ref)
    groups = wall_ref.shape[0]
    blocks, width = out_ref.shape[0], out_ref.shape[2]
    full = width * blocks
    gain = gain_ref[...]
    ggain = jnp.zeros((1, full), F32)
    for begin in range(0, h_ref.shape[0], 256):
        here = pl.ds(begin, 256)
        h = h_ref[here, :]
        factor = lax.rsqrt(jnp.sum(h * h, axis=1, keepdims=True) / full + EPSILON)
        dn = dna_ref[here, :] + dnb_ref[here, :]
        result = (h + (ya_ref[here, :] + yb_ref[here, :])).astype(BF16)
        for b in range(blocks):
            out_ref[b, here, :] = result[:, b * width : (b + 1) * width]
        weighted = dn * gain
        ggain = ggain + jnp.sum(dn * (h * factor), axis=0, keepdims=True)
        row_inner = jnp.sum(weighted * h, axis=1, keepdims=True)
        dh = (
            jnp.concatenate([c_ref[b, here, :] for b in range(blocks)], axis=1).astype(F32)
            + factor * weighted
            - h * (factor * factor * factor * row_inner / full)
        )
        dh_ref[here, :] = dh
        low_ref[here, :] = dh.astype(BF16)
        made = contract_last(low_ref[here, :], ow_ref[...]).astype(BF16)
        for b in range(blocks):
            dob_ref[b, here, :] = made[:, b * width : (b + 1) * width]
    ggain_ref[...] = ggain
    high, wide = gout_ref.shape[2], gout_ref.shape[3]
    for z in range(gout_ref.shape[1]):
        made = contract_rows(ob_ref[:, z * high : (z + 1) * high], low_ref[...]).astype(BF16)
        for g in range(groups):
            gout_ref[g, z] = made[:, g * wide : (g + 1) * wide]


def last_kernel(x_ref, dh_ref, parts_ref, gain_ref, out_ref, ggain_ref):
    blocks, width = x_ref.shape[0], x_ref.shape[2]
    full = width * blocks
    ggain_ref[...] = jnp.zeros_like(ggain_ref)
    for begin in range(0, x_ref.shape[1], 256):
        part = pl.ds(begin, 256)
        dn = parts_ref[0, part, :].astype(F32)
        for other in range(1, parts_ref.shape[0]):
            dn = dn + parts_ref[other, part, :].astype(F32)
        weighted = dn * gain_ref[...]
        total = jnp.zeros((256, 1), F32)
        inner = jnp.zeros((256, 1), F32)
        for b in range(blocks):
            cols = slice(b * width, (b + 1) * width)
            value = x_ref[b, part, :].astype(F32)
            total = total + jnp.sum(value * value, axis=1, keepdims=True)
            inner = inner + jnp.sum(weighted[:, cols] * value, axis=1, keepdims=True)
        factor = lax.rsqrt(total / full + EPSILON)
        slope = factor * factor * factor * inner / full
        for b in range(blocks):
            cols = slice(b * width, (b + 1) * width)
            value = x_ref[b, part, :].astype(F32)
            ggain_ref[:, cols] += jnp.sum(dn[:, cols] * value * factor, axis=0, keepdims=True)
            out_ref[b, part, :] = (
                dh_ref[part, cols] + factor * weighted[:, cols] - value * slope
            ).astype(BF16)


def last(base, x, dh, parts, gain):
    rows, full = parts.shape[1], gain.shape[1]
    shape = (x.shape[0], rows, x.shape[2])
    return pl.pallas_call(
        last_kernel,
        grid=(1,),
        out_shape=(jax.ShapeDtypeStruct(shape, BF16), jax.ShapeDtypeStruct((1, full), F32)),
        in_specs=[
            once(shape, (0, base // rows, 0)),
            once((rows, full), (base // rows, 0)),
            once(parts.shape),
            once(gain.shape),
        ],
        out_specs=(once(shape), once((1, full))),
        compiler_params=compiler_params(56),
    )(x, dh, parts, gain)


def by_layers():
    def run(
        tokens,
        first_values,
        segment_ids,
        cotangent,
        qkv_weight,
        out_weight,
        gate_up_weight,
        down_weight,
        attn_gain,
        mlp_gain,
    ):
        dp, z, f = (lax.axis_index(a) for a in ("dp", "head", "ffn"))
        depth, side = lax.axis_size("head"), lax.axis_size("ffn")
        group = 2 * side
        length, width = tokens.shape[1], tokens.shape[2]
        half = length // 2
        full_width = width * depth
        seq_len = length * side
        lanes = 2 * HD
        hidden = down_weight.shape[0]
        padded = -(-hidden // lanes) * lanes
        layer = ("dp", "ffn")
        vmem = pl.BlockSpec(memory_space=pltpu.VMEM)

        def to_layers(values):
            keep = lax.dynamic_slice(values, (depth, dp * half, 0), (2, half, width))
            give = lax.dynamic_slice(values, (depth, (1 - dp) * half, 0), (2, half, width))
            got = swap(give)
            early = jnp.where(dp == 0, keep, got)
            late = jnp.where(dp == 0, got, keep)
            return values[:depth], jnp.stack([early[0], late[0], early[1], late[1]])

        def from_layers(main, shared):
            keep = jnp.where(dp == 0, shared[0::2], shared[1::2])
            got = swap(jnp.where(dp == 0, shared[1::2], shared[0::2]))
            early = jnp.where(dp == 0, keep, got)
            late = jnp.where(dp == 0, got, keep)
            return jnp.concatenate([main, jnp.concatenate([early, late], axis=1)], axis=0)

        other_ids = swap(segment_ids)
        pick = depth + z // 2
        ids = [
            lax.dynamic_index_in_dim(segment_ids, z, 0, keepdims=False),
            lax.dynamic_index_in_dim(other_ids, z, 0, keepdims=False),
            jnp.where(
                z % 2 == dp,
                lax.dynamic_index_in_dim(segment_ids, pick, 0, keepdims=False),
                lax.dynamic_index_in_dim(other_ids, pick, 0, keepdims=False),
            ),
        ]
        ids = jnp.stack(ids)
        starts = jnp.sum((ids[:, None, :] < ids[:, :, None]).astype(jnp.int32), axis=2)
        lows = starts[:, ::BQ] // BK

        places = jnp.arange(seq_len, dtype=jnp.int32)
        cos, sin = rope_tables(places, HD)
        cos = jnp.concatenate([cos, cos], axis=1)
        sin = jnp.concatenate([-sin[:, : HD // 2], sin[:, HD // 2 :]], axis=1)
        sin = jnp.concatenate([sin, sin], axis=1)

        out_rows = out_weight.shape[0]
        def in_tiles(values):
            values = jnp.pad(values, ((0, 0), (0, padded - hidden)))
            return values.reshape(-1, padded // lanes, lanes).transpose(1, 0, 2).reshape(-1, lanes)

        wall = jnp.concatenate(
            [out_weight, in_tiles(gate_up_weight[:, 0]), in_tiles(gate_up_weight[:, 1]), down_weight],
            axis=0,
        )
        deep = qkv_weight.shape[0]
        part = qkv_weight.reshape(deep, 3, 2, lanes).transpose(2, 1, 0, 3).reshape(-1, lanes)
        left = jnp.concatenate([attn_gain, mlp_gain]).reshape(-1, lanes)
        pieces = []
        for _ in range(3):
            piece = lax.reduce_precision(left, 8, 7)
            pieces.append(piece.astype(BF16))
            left = left - piece
        tail = jnp.concatenate(pieces + [jnp.zeros((4, lanes), BF16)], axis=0)
        part = jnp.concatenate([part, tail], axis=0)
        part = exchange(jnp.broadcast_to(part[None], (depth,) + part.shape), "head")
        tail = part[:, 6 * deep :].astype(F32)
        step = 2 * width // lanes
        gains = tail[:, :step] + tail[:, step : 2 * step] + tail[:, 2 * step : 3 * step]
        gains = gains.reshape(depth, 2, width).transpose(1, 0, 2).reshape(2, 1, full_width)
        part = part[:, : 6 * deep].reshape(depth, 2, 3, deep, lanes)
        part = part.transpose(1, 0, 2, 3, 4).reshape(group, 3, deep, lanes)
        part = exchange(part, layer)
        weight = part.transpose(0, 2, 1, 3).reshape(group * deep, 3 * lanes)

        x, x_got = send_line(jnp.concatenate(to_layers(tokens), axis=1))
        x_got, weight, cos, sin, starts = after(x_got, weight, cos, sin, starts)
        lows = starts[:, ::BQ] // BK
        x = join_line(x, x_got)
        first = jnp.concatenate(to_layers(first_values), axis=1)
        first, x = after(first, x)
        first_got = send_across(first)
        nm, ns = normalized(x, gains[0], side, length)
        wall, nm = after(wall, nm)
        wall = lax.all_gather(wall, ("dp", "ffn", "head"), axis=0, tiled=False)
        wall = wall.reshape(group, depth, wall.shape[1], lanes)
        nm = exchange(nm, "ffn")
        first_got, ns, nm = after(first_got, ns, nm)
        first = join_across(first_got)

        def pair_halves(blocks):
            mine = lax.dynamic_slice_in_dim(blocks, dp * lanes, lanes, axis=2)
            return mine, swap(lax.dynamic_slice_in_dim(blocks, (1 - dp) * lanes, lanes, axis=2))

        def pair_join(mine, theirs):
            return lane_join(mine, swap(theirs))

        def lane_join(mine, got):
            return jnp.where(
                dp == 0,
                jnp.concatenate([mine, got], axis=2),
                jnp.concatenate([got, mine], axis=2),
            )

        def by_core(shared):
            shared = shared.reshape(side, 2, half, lanes)
            return (
                lax.dynamic_index_in_dim(shared, dp, 1, keepdims=False),
                lax.dynamic_index_in_dim(shared, 1 - dp, 1, keepdims=False),
            )

        first_mine, first_got = pair_halves(first)
        firsts = [(first_mine,), (first_got,), (first_mine, first_got)]
        core = dp.astype(jnp.int32).reshape(1)
        def attend_at(i, rows_in):
            return attend(
                core,
                lows[i],
                rows_in,
                weight,
                firsts[i],
                length if i == 2 else 0,
                starts[i][:, None],
                cos,
                sin,
            )

        ns = exchange(ns, "ffn")
        nm_other = swap(nm)
        kept = [attend_at(0, (nm,))]
        grad_blocks = jnp.concatenate(to_layers(cotangent), axis=1)
        nm_other, ns, grad_blocks, kept[0] = after(nm_other, ns, grad_blocks, kept[0])
        grad_blocks, grad_got = send_line(grad_blocks)
        ns_other = swap(ns)
        kept.append(attend_at(1, (nm_other,)))
        ns_other, grad_got[0], kept[1] = after(ns_other, grad_got[0], kept[1])
        om = pair_join(
            kept[0][3].reshape(side, length, lanes), kept[1][3].reshape(side, length, lanes)
        )
        ns_other, om = after(ns_other, om)
        kept.append(attend_at(2, (ns, ns_other)))
        normed = [(nm,), (nm_other,), (ns, ns_other)]
        om = exchange(om, "ffn")
        om, grad_got[1], kept[2] = after(om, grad_got[1], kept[2])
        os_, om = after(pair_join(*by_core(kept[2][3])), om)
        os_ = exchange(os_, "ffn")

        rows = length + half
        whole = jax.ShapeDtypeStruct((rows, full_width), F32)
        whole_low = jax.ShapeDtypeStruct((rows, full_width), BF16)
        out_spec = pl.BlockSpec((group, depth, out_rows, lanes), lambda i: (0, 0, 0, 0))

        def fixed(shape):
            return pl.BlockSpec(
                shape, lambda i: (0,) * len(shape), pipeline_mode=pl.Buffered(1)
            )

        ow_scratch = pltpu.VMEM((out_rows * depth, group * lanes), BF16)
        h, n2, ob = pl.pallas_call(
            hidden_kernel,
            grid=(1,),
            out_shape=(whole, whole_low, whole_low),
            in_specs=[fixed(a.shape) for a in (om, os_, x)]
            + [out_spec, fixed((1, full_width))],
            out_specs=tuple(fixed((rows, full_width)) for _ in range(3)),
            scratch_shapes=[ow_scratch],
            compiler_params=compiler_params(56),
        )(om, os_, x, wall, gains[1])
        grad_got, n2 = after(grad_got, n2)
        grad_blocks = join_line(grad_blocks, grad_got)

        high = wall.shape[2]
        count = padded // lanes

        def feed_forward(begin_tile, end_tile):
            wide = (end_tile - begin_tile) * lanes
            real = min(hidden, end_tile * lanes) - begin_tile * lanes
            grad_rows = 2 * (end_tile - begin_tile) * deep + real
            return pl.pallas_call(
                functools.partial(
                    mlp_kernel, begin_tile, real, out_rows, out_rows + 2 * count * deep
                ),
                grid=(depth,),
                out_shape=(
                    whole,
                    whole,
                    jax.ShapeDtypeStruct((group, depth, grad_rows, lanes), BF16),
                ),
                in_specs=[
                    fixed((rows, full_width)),
                    fixed((depth, rows, width)),
                    pl.BlockSpec((group, 1, high, lanes), lambda i: (0, i, 0, 0)),
                ],
                out_specs=(
                    fixed((rows, full_width)),
                    fixed((rows, full_width)),
                    pl.BlockSpec((group, 1, grad_rows, lanes), lambda i: (0, i, 0, 0)),
                ),
                scratch_shapes=[
                    pltpu.VMEM((full_width, 2 * wide), BF16),
                    pltpu.VMEM((wide, full_width), BF16),
                    pltpu.VMEM((full_width, rows), BF16),
                    pltpu.VMEM((rows, wide), BF16),
                    pltpu.VMEM((rows, 2 * wide), BF16),
                    pltpu.VMEM((rows, full_width), BF16),
                ],
                compiler_params=compiler_params(60),
            )(n2, grad_blocks, wall)

        ya, dna, grads_a = feed_forward(count - 2, count)
        n2, ya = after(n2, ya)
        yb, dnb, grads_b = feed_forward(0, count - 2)

        def layer_sum(grads):
            shape = grads.shape[1:]
            return lax.psum_scatter(grads, layer, scatter_dimension=0, tiled=True).reshape(shape)

        grads_a = layer_sum(grads_a)
        grads_b = layer_sum(grads_b)

        out, dh, dob, gout, gain_two = pl.pallas_call(
            hidden_back_kernel,
            grid=(1,),
            out_shape=(
                jax.ShapeDtypeStruct(grad_blocks.shape, BF16),
                whole,
                jax.ShapeDtypeStruct(grad_blocks.shape, BF16),
                jax.ShapeDtypeStruct((group, depth, out_rows, lanes), BF16),
                jax.ShapeDtypeStruct((1, full_width), F32),
            ),
            in_specs=[fixed((rows, full_width))] * 6
            + [fixed(grad_blocks.shape), out_spec, fixed((1, full_width))],
            out_specs=tuple(
                fixed(s)
                for s in (
                    grad_blocks.shape,
                    (rows, full_width),
                    grad_blocks.shape,
                    (group, depth, out_rows, lanes),
                    (1, full_width),
                )
            ),
            scratch_shapes=[ow_scratch, pltpu.VMEM((rows, full_width), BF16)],
            compiler_params=compiler_params(60),
        )(h, ya, yb, dna, dnb, ob, grad_blocks, wall, gains[1])

        dob = exchange(dob, "ffn")
        do_mine, do_got = pair_halves(dob)

        def back_of(i, grads_in):
            return attend_back(
                core,
                lows[i],
                normed[i],
                weight,
                kept[i],
                grads_in,
                length if i == 2 else 0,
                starts[i][None],
                cos,
                sin,
            )

        out, out_got = send_line(out)
        do_got, gout = after(do_got, gout)
        gout = exchange(gout, layer)
        dn_b, gw_b, gfv_b = back_of(1, (do_got,))
        dn_b, gw_b, gfv_b, out_got[0], out_got[1] = after(
            dn_b, gw_b, gfv_b, out_got[0], out_got[1]
        )
        do_mine, dn_b, gfv_b, grads_a = after(do_mine, dn_b, gfv_b, grads_a)
        grads_a, a_got = send_line(grads_a)
        dn_other = swap(dn_b)
        dn_a, gw_a, gfv_a = back_of(0, (do_mine,))
        dn_a, gw_a, gfv_a, dn_other, a_got, out_got[2], gout = after(
            dn_a, gw_a, gfv_a, dn_other, a_got, out_got[2], gout
        )
        gfv_other = swap(gfv_b)
        grads_a = join_line(grads_a, a_got)

        def add_low(mine, theirs):
            return (mine.astype(F32) + theirs.astype(F32)).astype(BF16)

        main_sum = add_low(dn_a, dn_other)
        out = join_line(out, out_got)
        gfv_main = lane_join(
            gfv_a.reshape(side, length, lanes), gfv_other.reshape(side, length, lanes)
        )
        do_mine, main_sum, grads_b = after(do_mine, main_sum, grads_b)
        main_sum = exchange(main_sum, "ffn")
        grads_b, b_got = send_line(grads_b)
        dn_s, dn_t, gw_s, gfv_s = back_of(2, (do_mine, do_got))
        b_got, dn_s, dn_t, gw_s, gfv_s = after(b_got, dn_s, dn_t, gw_s, gfv_s)
        gfv_mine, gfv_theirs = by_core(gfv_s)
        dn_t, gfv_theirs = swap(dn_t), swap(gfv_theirs)
        shared_sum, main_sum, gfv_theirs = after(add_low(dn_s, dn_t), main_sum, gfv_theirs)
        gfv = jnp.concatenate([gfv_main, lane_join(gfv_mine, gfv_theirs)], axis=1)
        shared_sum = exchange(shared_sum, "ffn")
        tokm, gain_main = last(0, x, dh, main_sum, gains[0])
        shared_sum, tokm = after(shared_sum, tokm)
        tokm, tokm_got = send_line(tokm)
        gfv, shared_sum, tokm_got[0] = after(gfv, shared_sum, tokm_got[0])
        gfv = exchange(gfv, "ffn")
        toks, gain_shared = last(length, x, dh, shared_sum, gains[0])
        toks, toks_got = send_line(toks)
        tokm_got, toks = after(tokm_got, toks)
        gfv, tokm_got, toks_got = after(gfv, tokm_got, toks_got)
        gfv, gfv_got = send_line(gfv)
        gfv_got[0], grad_w, gout, gain_shared, grads_b, out, toks_got = after(
            gfv_got[0],
            (gw_a + gw_b + gw_s).astype(BF16),
            gout,
            gain_shared,
            grads_b,
            out,
            toks_got,
        )
        out_tokens = from_layers(out[:, :length], out[:, length:])
        grads_b = join_line(grads_b, b_got)
        token_grads = from_layers(join_line(tokm, tokm_got), join_line(toks, toks_got))
        gfv = join_line(gfv, gfv_got)
        value_grads = from_layers(gfv[:, :length], gfv[:, length:])

        gout = jnp.sum(gout.astype(F32), axis=0).astype(BF16)
        grad_out = jnp.sum(exchange_line(gout).astype(F32), axis=0)

        grad_w = grad_w.reshape(3, lanes, group, deep).transpose(2, 0, 3, 1)
        grad_w = exchange(grad_w, layer)
        grad_w = grad_w.reshape(2, side, 3, deep, lanes).transpose(1, 3, 2, 0, 4)
        grad_w = grad_w.reshape(depth, deep, 3, width)
        grad_qkv = jnp.sum(exchange_line(grad_w).astype(F32), axis=0)

        gain_both = jnp.concatenate([gain_main + gain_shared, gain_two]).reshape(2, depth, width)
        gain_both = exchange_line(gain_both.transpose(1, 0, 2))
        gain_both = jnp.sum(gain_both, axis=0, keepdims=True)
        gain_both = exchange(jnp.broadcast_to(gain_both, (group, 2, width)), layer)
        gain_both = jnp.sum(gain_both, axis=0)

        def untile(values):
            return values.reshape(-1, deep, lanes).transpose(1, 0, 2).reshape(deep, -1)

        gates, ups, downs = [], [], []
        for grads, tiles_in in ((grads_b, count - 2), (grads_a, 2)):
            part = jnp.sum(grads.astype(F32), axis=0)
            gates.append(untile(part[: tiles_in * deep]))
            ups.append(untile(part[tiles_in * deep : 2 * tiles_in * deep]))
            downs.append(part[2 * tiles_in * deep :])
        grad_gate = jnp.stack(
            [jnp.concatenate(g, axis=1)[:, :hidden] for g in (gates, ups)], axis=1
        )
        return (
            out_tokens,
            token_grads,
            value_grads,
            grad_qkv,
            grad_out,
            grad_gate,
            jnp.concatenate(downs, axis=0),
            gain_both[0],
            gain_both[1],
        )

    return run


def fits_layers(mesh, seqs, seq_len, full_width, heads):
    sizes = dict(mesh.shape)
    return (
        sizes["dp"] == 2
        and sizes["head"] == 4
        and sizes["ffn"] == 4
        and seqs == 12
        and seq_len % (512 * 4) == 0
        and full_width == 1024
        and heads == 16
    )


def solution(mesh):
    in_specs = (
        P("dp", "ffn", "head"),
        P("dp", "ffn", "head"),
        P("dp", None),
        P("dp", "ffn", "head"),
        P(("dp", "ffn"), None, "head"),
        P("head", ("dp", "ffn")),
        P(("dp", "ffn"), None, "head"),
        P("head", ("dp", "ffn")),
        P("head"),
        P("head"),
    )
    out_specs = (
        P("dp", "ffn", "head"),
        P("dp", "ffn", "head"),
        P("dp", "ffn", "head"),
        P(("dp", "ffn"), None, "head"),
        P("head", ("dp", "ffn")),
        P(("dp", "ffn"), None, "head"),
        P("head", ("dp", "ffn")),
        P("head"),
        P("head"),
    )

    def program(*args):
        seqs, seq_len, full_width = args[0].shape
        heads = args[5].shape[0] // HD
        fast = fits_layers(mesh, seqs, seq_len, full_width, heads)
        body = by_layers() if fast else per_device
        return jax.shard_map(
            body, mesh=mesh, in_specs=in_specs, out_specs=out_specs, check_vma=False
        )(*args)

    return program
```

```python
import functools
import math

import jax
import jax.numpy as jnp
from jax import lax
from jax.experimental import pallas as pl
from jax.experimental.pallas import tpu as pltpu
from jax.sharding import PartitionSpec as P

HD = 64
MICRO = 4


EPSILON = 1e-06
MASKED = -1e30


def rope_tables(positions, head_size):
    half_size = head_size // 2
    exponent = jnp.arange(half_size, dtype=jnp.float32) * (2.0 / head_size)
    frequency = jnp.exp(exponent * -jnp.log(jnp.float32(10000.0)))
    angles = positions.astype(jnp.float32)[:, None] * frequency[None, :]
    angles = jnp.concatenate([angles, angles], axis=1)
    return (jnp.cos(angles), jnp.sin(angles))


def rotate(vectors, cos_table, sin_table):
    half_size = vectors.shape[-1] // 2
    turned = jnp.concatenate([-vectors[..., half_size:], vectors[..., :half_size]], axis=-1)
    return vectors * cos_table + turned * sin_table


def unrotate(gradient, cos_table, sin_table):
    half_size = gradient.shape[-1] // 2
    scaled = gradient * sin_table
    turned = jnp.concatenate([scaled[..., half_size:], -scaled[..., :half_size]], axis=-1)
    return gradient * cos_table + turned


def swiglu(gate_up):
    return jax.nn.silu(gate_up[:, 0]) * gate_up[:, 1]


def contract_rows(former, latter):
    return lax.dot_general(
        former, latter, (((0,), (0,)), ((), ())), preferred_element_type=jnp.float32
    )


def contract_last(former, latter):
    return lax.dot_general(
        former, latter, (((1,), (1,)), ((), ())), preferred_element_type=jnp.float32
    )


def gather_weights(qkv_weight, out_weight, gate_up_weight, down_weight):
    return (
        lax.all_gather(qkv_weight, ("dp", "ffn"), axis=0, tiled=True),
        lax.all_gather(out_weight, ("dp", "ffn"), axis=1, tiled=True),
        lax.all_gather(gate_up_weight, ("dp", "ffn"), axis=0, tiled=True),
        lax.all_gather(down_weight, ("dp", "ffn"), axis=1, tiled=True),
    )


def row_total(values):
    return lax.psum(values, "head")


def spread_rows(values):
    return lax.all_gather(values, "head", axis=1, tiled=True)


def spread_grads(values):
    return lax.all_gather(values, "head", axis=1, tiled=True)


def collect_rows(values):
    return lax.psum_scatter(
        values.astype(jnp.bfloat16), "head", scatter_dimension=1, tiled=True
    ).astype(jnp.float32)


def collect_grads(values):
    return lax.psum_scatter(
        values.astype(jnp.bfloat16), "head", scatter_dimension=1, tiled=True
    ).astype(jnp.float32)


def norm_forward(values, gain_vector, full_width):
    factor = lax.rsqrt(row_total(jnp.sum(values * values, axis=1)) / full_width + EPSILON)
    return (factor, values * factor[:, None] * gain_vector)


def norm_backward(values, factor, gain_vector, gradient, full_width):
    weighted = gradient * gain_vector
    row_inner = row_total(jnp.sum(weighted * values, axis=1))
    norm_grad = (
        factor[:, None] * weighted
        - values * (factor * factor * factor * row_inner / full_width)[:, None]
    )
    gain_grad = jnp.sum(gradient * values * factor[:, None], axis=0)
    return (norm_grad, gain_grad)


def masked_scores(queries, key_rows, query_places, key_places, query_ids, key_ids, score_scale):
    scores = (
        jnp.einsum("qhd,khd->hqk", queries, key_rows, preferred_element_type=jnp.float32)
        * score_scale
    )
    allowed = (key_places[None, :] <= query_places[:, None]) & (
        key_ids[None, :] == query_ids[:, None]
    )
    return jnp.where(allowed[None], scores, MASKED)


def attend_forward(
    queries, key_rows, value_rows, query_places, key_places, query_ids, key_ids, score_scale
):
    scores = masked_scores(
        queries, key_rows, query_places, key_places, query_ids, key_ids, score_scale
    )
    highest = jnp.max(scores, axis=2, keepdims=True)
    log_total = highest + jnp.log(jnp.sum(jnp.exp(scores - highest), axis=2, keepdims=True))
    weights = jnp.exp(scores - log_total).astype(jnp.bfloat16)
    attended = jnp.einsum("hqk,khd->qhd", weights, value_rows, preferred_element_type=jnp.float32)
    return (attended, log_total[:, :, 0])


def query_side(
    queries,
    key_rows,
    value_rows,
    grad_rows,
    log_total,
    query_places,
    key_places,
    query_ids,
    key_ids,
    score_scale,
):
    scores = masked_scores(
        queries, key_rows, query_places, key_places, query_ids, key_ids, score_scale
    )
    weights = jnp.exp(scores - log_total[:, :, None])
    weight_grad = jnp.einsum(
        "qhd,khd->hqk", grad_rows, value_rows, preferred_element_type=jnp.float32
    )
    row_inner = jnp.sum(weights * weight_grad, axis=2)
    score_grad = (weights * (weight_grad - row_inner[:, :, None])).astype(jnp.bfloat16)
    query_grad = (
        jnp.einsum("hqk,khd->qhd", score_grad, key_rows, preferred_element_type=jnp.float32)
        * score_scale
    )
    return (weights, score_grad, row_inner, query_grad)


def per_device(
    tokens,
    first_values,
    segment_ids,
    cotangent,
    qkv_weight,
    out_weight,
    gate_up_weight,
    down_weight,
    attn_gain,
    mlp_gain,
):
    seq_total = tokens.shape[0]
    local_len = tokens.shape[1]
    local_width = tokens.shape[2]
    full_width = local_width * lax.axis_size("head")
    seq_len = local_len * lax.axis_size("ffn")
    head_width = first_values.shape[2]
    head_local = head_width // HD
    hidden_local = down_weight.shape[0]
    score_scale = 1.0 / math.sqrt(HD)
    offset = lax.axis_index("ffn") * local_len
    own_places = offset + jnp.arange(local_len, dtype=jnp.int32)
    all_places = jnp.arange(seq_len, dtype=jnp.int32)
    cos_table, sin_table = rope_tables(own_places, HD)
    cos_table = cos_table[:, None, :]
    sin_table = sin_table[:, None, :]
    base_count = seq_total // MICRO
    remainder = seq_total % MICRO
    qkv_grads = jnp.zeros((full_width, 3, head_width), jnp.float32)
    out_grads = jnp.zeros((head_width, full_width), jnp.float32)
    gate_grads = jnp.zeros((full_width, 2, hidden_local), jnp.float32)
    down_grads = jnp.zeros((hidden_local, full_width), jnp.float32)
    attn_gain_grads = jnp.zeros((local_width,), jnp.float32)
    mlp_gain_grads = jnp.zeros((local_width,), jnp.float32)
    outputs = []
    token_grads = []
    value_grads = []
    seq_start = 0
    for micro_index in range(MICRO):
        seq_count = base_count + (1 if micro_index < remainder else 0)
        row_count = seq_count * local_len
        gathered = gather_weights(qkv_weight, out_weight, gate_up_weight, down_weight)
        qkv_matrix = gathered[0].reshape(full_width, 3 * head_width)
        out_matrix = gathered[1]
        gate_matrix = gathered[2].reshape(full_width, 2 * hidden_local)
        down_matrix = gathered[3]
        token_rows = (
            tokens[seq_start : seq_start + seq_count]
            .reshape(row_count, local_width)
            .astype(jnp.float32)
        )
        factor_one, normed_one = norm_forward(token_rows, attn_gain, full_width)
        normed_full = spread_rows(normed_one.astype(jnp.bfloat16))
        projected = jnp.dot(normed_full, qkv_matrix, preferred_element_type=jnp.float32)
        projected = projected.reshape(seq_count, local_len, 3, head_local, HD)
        queries = rotate(projected[:, :, 0], cos_table, sin_table).astype(jnp.bfloat16)
        key_local = rotate(projected[:, :, 1], cos_table, sin_table).astype(jnp.bfloat16)
        first_block = first_values[seq_start : seq_start + seq_count].reshape(
            seq_count, local_len, head_local, HD
        )
        value_local = (0.5 * projected[:, :, 2] + 0.5 * first_block.astype(jnp.float32)).astype(
            jnp.bfloat16
        )
        key_full, value_full = (
            lax.all_gather(
                key_local.reshape(seq_count, local_len, head_width), "ffn", axis=1, tiled=True
            ),
            lax.all_gather(
                value_local.reshape(seq_count, local_len, head_width), "ffn", axis=1, tiled=True
            ),
        )
        key_full = key_full.reshape(seq_count, seq_len, head_local, HD)
        value_full = value_full.reshape(seq_count, seq_len, head_local, HD)
        ids_full = segment_ids[seq_start : seq_start + seq_count]
        ids_own = lax.dynamic_slice_in_dim(ids_full, offset, local_len, axis=1)

        def forward_one(pieces):
            return attend_forward(
                pieces[0],
                pieces[1],
                pieces[2],
                own_places,
                all_places,
                pieces[3],
                pieces[4],
                score_scale,
            )

        attended, log_totals = lax.map(
            forward_one, (queries, key_full, value_full, ids_own, ids_full)
        )
        attended_low = attended.reshape(row_count, head_width).astype(jnp.bfloat16)
        branch = collect_rows(jnp.dot(attended_low, out_matrix, preferred_element_type=jnp.float32))
        hidden = token_rows + branch
        factor_two, normed_two = norm_forward(hidden, mlp_gain, full_width)
        normed_mlp = spread_rows(normed_two.astype(jnp.bfloat16))
        gate_up = jnp.dot(normed_mlp, gate_matrix, preferred_element_type=jnp.float32).reshape(
            row_count, 2, hidden_local
        )
        active, swiglu_back = jax.vjp(swiglu, gate_up)
        active_low = active.astype(jnp.bfloat16)
        mlp_branch = collect_rows(
            jnp.dot(active_low, down_matrix, preferred_element_type=jnp.float32)
        )
        outputs.append(
            (hidden + mlp_branch).astype(jnp.bfloat16).reshape(seq_count, local_len, local_width)
        )
        grad_out = cotangent[seq_start : seq_start + seq_count].reshape(row_count, local_width)
        grad_full = spread_grads(grad_out)
        active_grad = contract_last(grad_full, down_matrix)
        down_grads = down_grads + contract_rows(active_low, grad_full)
        gate_grad = (
            swiglu_back(active_grad)[0].astype(jnp.bfloat16).reshape(row_count, 2 * hidden_local)
        )
        gate_grads = gate_grads + contract_rows(normed_mlp, gate_grad).reshape(
            full_width, 2, hidden_local
        )
        normed_grad = collect_grads(contract_last(gate_grad, gate_matrix))
        back_two, gain_two = norm_backward(hidden, factor_two, mlp_gain, normed_grad, full_width)
        mlp_gain_grads = mlp_gain_grads + gain_two
        hidden_grad = grad_out.astype(jnp.float32) + back_two
        hidden_full = spread_grads(hidden_grad.astype(jnp.bfloat16))
        attended_grad = contract_last(hidden_full, out_matrix).astype(jnp.bfloat16)
        out_grads = out_grads + contract_rows(attended_low, hidden_full)
        grad_blocks = attended_grad.reshape(seq_count, local_len, head_local, HD)

        def backward_one(pieces):
            (
                queries_one,
                key_one,
                value_one,
                grad_one,
                total_one,
                own_ids,
                full_ids,
                own_key,
                own_value,
            ) = pieces
            weights, score_grad, row_inner, query_grad = query_side(
                queries_one,
                key_one,
                value_one,
                grad_one,
                total_one,
                own_places,
                all_places,
                own_ids,
                full_ids,
                score_scale,
            )
            key_grad = (
                jnp.einsum(
                    "hqk,qhd->khd", score_grad, queries_one, preferred_element_type=jnp.float32
                )
                * score_scale
            )
            value_grad = jnp.einsum(
                "hqk,qhd->khd",
                weights.astype(jnp.bfloat16),
                grad_one,
                preferred_element_type=jnp.float32,
            )
            key_value = jnp.stack([key_grad, value_grad], axis=1).reshape(seq_len, 2, head_width)
            return (
                query_grad,
                lax.psum_scatter(
                    key_value.astype(jnp.bfloat16), "ffn", scatter_dimension=0, tiled=True
                ).astype(jnp.float32),
            )

        query_grads, key_value_grads = lax.map(
            backward_one,
            (
                queries,
                key_full,
                value_full,
                grad_blocks,
                log_totals,
                ids_own,
                ids_full,
                key_local,
                value_local,
            ),
        )
        key_rot_grad = key_value_grads[:, :, 0].reshape(seq_count, local_len, head_local, HD)
        value_mix_grad = key_value_grads[:, :, 1].reshape(seq_count, local_len, head_local, HD)
        value_grads.append(
            (0.5 * value_mix_grad).astype(jnp.bfloat16).reshape(seq_count, local_len, head_width)
        )
        projected_grad = (
            jnp.stack(
                [
                    unrotate(query_grads, cos_table, sin_table),
                    unrotate(key_rot_grad, cos_table, sin_table),
                    0.5 * value_mix_grad,
                ],
                axis=2,
            )
            .astype(jnp.bfloat16)
            .reshape(row_count, 3 * head_width)
        )
        qkv_grads = qkv_grads + contract_rows(normed_full, projected_grad).reshape(
            full_width, 3, head_width
        )
        normed_grad_one = collect_grads(contract_last(projected_grad, qkv_matrix))
        back_one, gain_one = norm_backward(
            token_rows, factor_one, attn_gain, normed_grad_one, full_width
        )
        attn_gain_grads = attn_gain_grads + gain_one
        token_grads.append(
            (hidden_grad + back_one).astype(jnp.bfloat16).reshape(seq_count, local_len, local_width)
        )
        seq_start = seq_start + seq_count
    weight_sums = (
        lax.psum_scatter(
            qkv_grads.astype(jnp.bfloat16), ("dp", "ffn"), scatter_dimension=0, tiled=True
        ).astype(jnp.float32),
        lax.psum_scatter(
            out_grads.astype(jnp.bfloat16), ("dp", "ffn"), scatter_dimension=1, tiled=True
        ).astype(jnp.float32),
        lax.psum_scatter(
            gate_grads.astype(jnp.bfloat16), ("dp", "ffn"), scatter_dimension=0, tiled=True
        ).astype(jnp.float32),
        lax.psum_scatter(
            down_grads.astype(jnp.bfloat16), ("dp", "ffn"), scatter_dimension=1, tiled=True
        ).astype(jnp.float32),
    )
    gain_sums = lax.psum((attn_gain_grads, mlp_gain_grads), ("dp", "ffn"))
    return (
        jnp.concatenate(outputs, axis=0),
        jnp.concatenate(token_grads, axis=0),
        jnp.concatenate(value_grads, axis=0),
        weight_sums[0],
        weight_sums[1],
        weight_sums[2],
        weight_sums[3],
        gain_sums[0],
        gain_sums[1],
    )


BF16 = jnp.bfloat16
F32 = jnp.float32
BQ = 512
BK = 512
MASKED_SCORE = -1e30


def matmul(former, latter):
    return lax.dot_general(former, latter, (((1,), (0,)), ((), ())), preferred_element_type=F32)


def compiler_params(mib):
    return pltpu.CompilerParams(vmem_limit_bytes=mib * 1024 * 1024)


def exchange(blocks, axes):
    return lax.all_to_all(blocks, axes, 0, 0, tiled=True)


def line_sends(blocks, axis="head"):
    me = lax.axis_index(axis)
    return [
        lax.dynamic_index_in_dim(blocks, me ^ step, 0, keepdims=False)
        for step in range(1, blocks.shape[0])
    ]


def line_go(sends, axis="head"):
    count = len(sends) + 1
    return [
        lax.ppermute(send, axis, [(j, j ^ (step + 1)) for j in range(count)])
        for step, send in enumerate(sends)
    ]


def send_line(blocks, axis="head"):
    return blocks, line_go(line_sends(blocks, axis), axis)


def join_line(blocks, got, axis="head"):
    me = lax.axis_index(axis)
    got = after(*got)
    for step, piece in enumerate(got):
        blocks = lax.dynamic_update_index_in_dim(blocks, piece, me ^ (step + 1), 0)
    return blocks


def exchange_line(blocks, axis="head"):
    return join_line(*send_line(blocks, axis), axis)


def after(values, *earlier):
    return lax.optimization_barrier((values, *earlier))


def send_across(blocks):
    count = blocks.shape[0]
    me = lax.axis_index("ffn")
    got = []
    for step in range(count):
        pairs = []
        for j in range(count * count):
            h, f = divmod(j, count)
            pairs.append((j, (f ^ step) * count + h))
        send = lax.dynamic_index_in_dim(blocks, me ^ step, 0, keepdims=False)
        got.append(lax.ppermute(send, ("head", "ffn"), pairs))
    return got


def join_across(got):
    here = lax.axis_index("head")
    a, b, c, d = after(*got)
    return jnp.where(
        here % 2 == 0,
        jnp.where(here < 2, jnp.stack([a, b, c, d]), jnp.stack([c, d, a, b])),
        jnp.where(here < 2, jnp.stack([b, a, d, c]), jnp.stack([d, c, b, a])),
    )


def in_pieces(values):
    pieces = []
    for _ in range(3):
        piece = lax.reduce_precision(values, 8, 7)
        pieces.append(piece.astype(BF16))
        values = values - piece
    return pieces


def from_pieces(pieces):
    return sum(p.astype(F32) for p in pieces)


def swap(values):
    return lax.ppermute(values, "dp", [(0, 1), (1, 0)])


def swap_halves(values):
    low = (lax.broadcasted_iota(jnp.int32, values.shape, 1) % HD) < HD // 2
    lanes = values.shape[1]
    return jnp.where(
        low, pltpu.roll(values, lanes - HD // 2, 1), pltpu.roll(values, HD // 2, 1)
    )


def norm_kernel(x_ref, gain_ref, main_ref, shared_ref):
    blocks, rows, width = x_ref.shape
    for start in range(0, rows, 256):
        part = pl.ds(start, 256)
        values = [x_ref[b, part, :].astype(F32) for b in range(blocks)]
        total = sum(jnp.sum(v * v, axis=1, keepdims=True) for v in values)
        factor = lax.rsqrt(total / (width * blocks) + EPSILON)
        out_ref, base = main_ref, 0
        if start >= main_ref.shape[1]:
            out_ref, base = shared_ref, main_ref.shape[1]
        for b in range(blocks):
            cols = pl.ds(b * width, width)
            normed = (values[b] * factor * gain_ref[:, cols]).astype(BF16)
            for copy in range(out_ref.shape[0]):
                out_ref[copy, start - base : start - base + 256, cols] = normed


def normalized(x, gain, copies, length):
    shapes = [(copies, r, gain.shape[1]) for r in (length, x.shape[1] - length)]
    return pl.pallas_call(
        norm_kernel,
        grid=(1,),
        out_shape=tuple(jax.ShapeDtypeStruct(s, BF16) for s in shapes),
        in_specs=[once(x.shape), once(gain.shape)],
        out_specs=tuple(once(s) for s in shapes),
        compiler_params=compiler_params(48),
    )(x, gain)


def head_masks():
    lane = lax.broadcasted_iota(jnp.int32, (1, 2 * HD), 1)
    first = jnp.where(lane < HD, 1.0, 0.0).astype(BF16)
    return first, (1.0 - first.astype(F32)).astype(BF16)


def row_chunks(refs, side_ref):
    rows = refs[0].shape[1]
    chunks = []
    for number, ref in enumerate(refs):
        for block in range(ref.shape[0]):
            at = block * rows * len(refs)
            if len(refs) == 2:
                half = side_ref[0] if number == 0 else 1 - side_ref[0]
                at = pl.multiple_of(at + half * rows, rows)
            chunks.append((number, block, pl.ds(at, rows)))
    return chunks


def attend_kernel(count, side_ref, low_ref, *refs):
    n_refs, fv_refs = refs[:count], refs[count : 2 * count]
    w_ref, start_ref, cos_ref, sin_ref, q_ref, k_ref, v_ref, o_ref, lse_ref = refs[2 * count :]
    length = q_ref.shape[0]
    lanes = 2 * HD
    for number, block, rows in row_chunks(n_refs, side_ref):
        made = matmul(n_refs[number][block], w_ref[...])
        cos, sin = cos_ref[rows, :], sin_ref[rows, :]
        q = made[:, :lanes]
        k = made[:, lanes : 2 * lanes]
        q_ref[rows, :] = ((q * cos + swap_halves(q) * sin) * (1.0 / math.sqrt(HD))).astype(BF16)
        k_ref[rows, :] = (k * cos + swap_halves(k) * sin).astype(BF16)
        first = fv_refs[number][block].astype(F32)
        v_ref[rows, :] = (0.5 * made[:, 2 * lanes :] + 0.5 * first).astype(BF16)
    mask_a, mask_b = head_masks()
    lane = lax.broadcasted_iota(jnp.int32, (BQ, lanes), 1)
    for i in range(length // BQ):
        rows = pl.ds(i * BQ, BQ)
        q = q_ref[rows, :]
        both = jnp.concatenate([q * mask_a, q * mask_b], axis=0)
        start = start_ref[rows, :]
        start = jnp.concatenate([start, start], axis=0)
        place = i * BQ + lax.broadcasted_iota(jnp.int32, (BQ, 1), 0)
        place = jnp.concatenate([place, place], axis=0)

        def step(j, carry):
            top, total, acc = carry
            keys = pl.ds(pl.multiple_of(j * BK, BK), BK)
            s = contract_last(both, k_ref[keys, :])
            key = j * BK + lax.broadcasted_iota(jnp.int32, s.shape, 1)
            s = jnp.where((key >= start) & (key <= place), s, MASKED_SCORE)
            new_top = jnp.maximum(top, jnp.max(s, axis=1, keepdims=True))
            p = jnp.exp(s - new_top)
            scale = jnp.exp(top - new_top)
            total = total * scale + jnp.sum(p, axis=1, keepdims=True)
            acc = acc * scale + matmul(p.astype(BF16), v_ref[keys, :])
            return new_top, total, acc

        top, total, acc = lax.fori_loop(
            low_ref[i],
            (i * BQ + BQ - 1) // BK + 1,
            step,
            (
                jnp.full((2 * BQ, 1), MASKED_SCORE, F32),
                jnp.zeros((2 * BQ, 1), F32),
                jnp.zeros((2 * BQ, lanes), F32),
            ),
        )
        acc = acc / total
        lse = top + jnp.log(total)
        o_ref[rows, :] = jnp.where(lane < HD, acc[:BQ], acc[BQ:]).astype(BF16)
        lse_ref[rows, :] = jnp.where(
            lane < HD, jnp.broadcast_to(lse[:BQ], (BQ, lanes)), jnp.broadcast_to(lse[BQ:], (BQ, lanes))
        )


def once(shape, index=None):
    index = (0,) * len(shape) if index is None else index
    return pl.BlockSpec(shape, lambda i: index, pipeline_mode=pl.Buffered(1))


def attend(side, low, normed, weight, firsts, begin, start_col, cos, sin):
    count = len(normed)
    blocks, rows, _ = normed[0].shape
    length = start_col.shape[0]
    lanes = 2 * HD
    small = jax.ShapeDtypeStruct((length, lanes), BF16)
    scalar = pl.BlockSpec(memory_space=pltpu.SMEM)
    return pl.pallas_call(
        functools.partial(attend_kernel, count),
        grid=(1,),
        out_shape=(small, small, small, small, jax.ShapeDtypeStruct((length, lanes), F32)),
        in_specs=[scalar, scalar]
        + [once(n.shape) for n in normed]
        + [once((blocks, rows, lanes), (0, begin // rows, 0))] * count
        + [once(a.shape) for a in (weight, start_col, cos, sin)],
        out_specs=(once((length, lanes)),) * 5,
        compiler_params=compiler_params(48),
    )(side, low, *normed, *firsts, weight, start_col, cos, sin)


def attend_back_kernel(count, side_ref, low_ref, *refs):
    n_refs, do_refs = refs[:count], refs[count : 2 * count]
    w_ref, q_ref, k_ref, v_ref, o_ref, lse_ref, start_ref, cos_ref, sin_ref = refs[
        2 * count : 2 * count + 9
    ]
    dn_refs = refs[2 * count + 9 : 3 * count + 9]
    gw_ref, gfv_ref, dq_ref, dk_ref, dv_ref, dp_ref, do_ref = refs[3 * count + 9 :]
    length = q_ref.shape[0]
    lanes = 2 * HD
    chunks = row_chunks(n_refs, side_ref)
    for number, block, rows in chunks:
        do_ref[rows, :] = do_refs[number][block]
    dk_ref[...] = jnp.zeros_like(dk_ref)
    dv_ref[...] = jnp.zeros_like(dv_ref)
    mask_a, mask_b = head_masks()
    lane = lax.broadcasted_iota(jnp.int32, (BQ, lanes), 1)
    for i in range(length // BQ):
        rows = pl.ds(i * BQ, BQ)
        q, do = q_ref[rows, :], do_ref[rows, :]
        q2 = jnp.concatenate([q * mask_a, q * mask_b], axis=0)
        do2 = jnp.concatenate([do * mask_a, do * mask_b], axis=0)
        lse = jnp.transpose(lse_ref[rows, :])
        lse = jnp.concatenate([lse[0:1, :], lse[HD : HD + 1, :]], axis=1)
        inner = jnp.transpose(do.astype(F32) * o_ref[rows, :].astype(F32))
        inner = jnp.concatenate(
            [
                jnp.sum(inner[:HD], axis=0, keepdims=True),
                jnp.sum(inner[HD:], axis=0, keepdims=True),
            ],
            axis=1,
        )
        start = start_ref[:, rows]
        start = jnp.concatenate([start, start], axis=1)
        place = i * BQ + lax.broadcasted_iota(jnp.int32, (1, BQ), 1)
        place = jnp.concatenate([place, place], axis=1)

        def step(j, acc):
            keys = pl.ds(pl.multiple_of(j * BK, BK), BK)
            k, v = k_ref[keys, :], v_ref[keys, :]
            s = contract_last(k, q2)
            key = j * BK + lax.broadcasted_iota(jnp.int32, s.shape, 0)
            s = jnp.where((key >= start) & (key <= place), s, MASKED_SCORE)
            p = jnp.exp(s - lse)
            dp = contract_last(v, do2)
            ds = (p * (dp - inner)).astype(BF16)
            dv_ref[keys, :] += matmul(p.astype(BF16), do2)
            dk_ref[keys, :] += matmul(ds, q2)
            return acc + contract_rows(ds, k)

        acc = lax.fori_loop(
            low_ref[i], (i * BQ + BQ - 1) // BK + 1, step, jnp.zeros((2 * BQ, lanes), F32)
        )
        dq_ref[rows, :] = jnp.where(lane < HD, acc[:BQ], acc[BQ:]) * (1.0 / math.sqrt(HD))
    for begin in range(0, length, 512):
        rows = pl.ds(begin, 512)
        cos, sin = cos_ref[rows, :], sin_ref[rows, :]
        dq, dk = dq_ref[rows, :], dk_ref[rows, :]
        dv = (0.5 * dv_ref[rows, :]).astype(BF16)
        gfv_ref[rows, :] = dv
        dp_ref[rows, 0:lanes] = (dq * cos - swap_halves(dq) * sin).astype(BF16)
        dp_ref[rows, lanes : 2 * lanes] = (dk * cos - swap_halves(dk) * sin).astype(BF16)
        dp_ref[rows, 2 * lanes :] = dv
    for number, block, rows in chunks:
        part = dp_ref[rows, :]
        dn_refs[number][block] = contract_last(part, w_ref[...]).astype(BF16)
        made = contract_rows(part, n_refs[number][block])
        if number + block == 0:
            gw_ref[...] = made
        else:
            gw_ref[...] += made


def attend_back(side, low, normed, weight, kept, grads, begin, start_row, cos, sin):
    count = len(normed)
    blocks, rows, width = normed[0].shape
    length = start_row.shape[1]
    lanes = 2 * HD
    scalar = pl.BlockSpec(memory_space=pltpu.SMEM)
    return pl.pallas_call(
        functools.partial(attend_back_kernel, count),
        grid=(1,),
        out_shape=tuple(jax.ShapeDtypeStruct(n.shape, BF16) for n in normed)
        + (
            jax.ShapeDtypeStruct((3 * lanes, width), F32),
            jax.ShapeDtypeStruct((length, lanes), BF16),
        ),
        in_specs=[scalar, scalar]
        + [once(n.shape) for n in normed]
        + [once((blocks, rows, lanes), (0, begin // rows, 0))] * count
        + [once(a.shape) for a in (weight, *kept, start_row, cos, sin)],
        out_specs=tuple(once(n.shape) for n in normed)
        + (once((3 * lanes, width)), once((length, lanes))),
        scratch_shapes=[
            pltpu.VMEM((length, lanes), F32),
            pltpu.VMEM((length, lanes), F32),
            pltpu.VMEM((length, lanes), F32),
            pltpu.VMEM((length, 3 * lanes), BF16),
            pltpu.VMEM((length, lanes), BF16),
        ],
        compiler_params=compiler_params(56),
    )(side, low, *normed, *grads, weight, *kept, start_row, cos, sin)


def fill_out_weight(wall_ref, ow_ref):
    groups, depth, high, wide = wall_ref.shape
    for g in range(groups):
        for z in range(depth):
            ow_ref[z * high : (z + 1) * high, g * wide : (g + 1) * wide] = wall_ref[g, z]


def hidden_kernel(
    om_ref, os_ref, x_ref, wall_ref, gain_ref,
    h_ref, n_ref, ob_ref, ow_ref,
):
    fill_out_weight(wall_ref, ow_ref)
    blocks, width = x_ref.shape[0], x_ref.shape[2]
    base = 0
    for o in (om_ref, os_ref):
        rows = o.shape[1]
        for begin in range(0, rows, 256):
            part = pl.ds(begin, 256)
            here = pl.ds(base + begin, 256)
            for b in range(blocks):
                ob_ref[here, b * width : (b + 1) * width] = o[b, part, :]
            branch = matmul(ob_ref[here, :], ow_ref[...])
            total = jnp.zeros((256, 1), F32)
            for b in range(blocks):
                cols = slice(b * width, (b + 1) * width)
                h = x_ref[b, here, :].astype(F32) + branch[:, cols]
                h_ref[here, cols] = h
                total = total + jnp.sum(h * h, axis=1, keepdims=True)
            factor = lax.rsqrt(total / (width * blocks) + EPSILON)
            n_ref[here, :] = (h_ref[here, :] * factor * gain_ref[...]).astype(BF16)
        base += rows


def mlp_kernel(
    begin_tile, hidden, first, down_first,
    n_ref, c_ref, wall_ref, y_ref, dn_ref, grad_ref,
    g_ref, d_ref, nt_ref, act_ref, dgu_ref, dy_ref,
):
    groups, lanes = wall_ref.shape[0], wall_ref.shape[3]
    rows, width = n_ref.shape
    padded = d_ref.shape[0]
    deep = width // groups
    tiles = 2 * padded // lanes
    all_tiles = (down_first - first) // deep // 2

    @pl.when(pl.program_id(0) == 0)
    def _():
        y_ref[...] = jnp.zeros_like(y_ref)
        dn_ref[...] = jnp.zeros_like(dn_ref)
        nt_ref[...] = jnp.transpose(n_ref[...])
        for b in range(c_ref.shape[0]):
            part = c_ref.shape[2]
            dy_ref[:, b * part : (b + 1) * part] = c_ref[b]
        if padded > hidden:
            d_ref[hidden:, :] = jnp.zeros((padded - hidden, width), BF16)

    for g in range(groups):
        for t in range(tiles):
            column = begin_tile + t
            if t >= tiles // 2:
                column += all_tiles - tiles // 2
            at = first + column * deep
            g_ref[g * deep : (g + 1) * deep, t * lanes : (t + 1) * lanes] = wall_ref[
                g, 0, at : at + deep, :
            ]
        at = down_first + begin_tile * lanes
        d_ref[0:hidden, g * lanes : (g + 1) * lanes] = wall_ref[g, 0, at : at + hidden, :]
    for begin in range(0, rows, 256):
        part = pl.ds(begin, 256)
        gu = matmul(n_ref[part, :], g_ref[...])
        gate, up = gu[:, :padded], gu[:, padded:]
        sig = 1.0 / (1.0 + jnp.exp(-gate))
        silu = gate * sig
        act_ref[part, :] = (silu * up).astype(BF16)
        dact = contract_last(dy_ref[part, :], d_ref[...])
        dgu_ref[part, :padded] = (dact * up * sig * (1.0 + gate * (1.0 - sig))).astype(BF16)
        dgu_ref[part, padded:] = (dact * silu).astype(BF16)
        y_ref[part, :] += matmul(act_ref[part, :], d_ref[...])
        dn_ref[part, :] += contract_last(dgu_ref[part, :], g_ref[...])
    for begin in range(0, 2 * padded, 512):
        made = matmul(nt_ref[...], dgu_ref[:, begin : begin + 512]).astype(BF16)
        for g in range(groups):
            for t in range(512 // lanes):
                at = (begin // lanes + t) * deep
                grad_ref[g, 0, at : at + deep, :] = made[
                    g * deep : (g + 1) * deep, t * lanes : (t + 1) * lanes
                ]
    for begin in range(0, width, 512):
        made = contract_rows(act_ref[...], dy_ref[:, begin : begin + 512]).astype(BF16)
        for t in range(512 // lanes):
            grad_ref[begin // lanes + t, 0, tiles * deep :, :] = made[
                :hidden, t * lanes : (t + 1) * lanes
            ]


def hidden_back_kernel(
    h_ref, ya_ref, yb_ref, dna_ref, dnb_ref, c_ref, wall_ref, gain_ref,
    out_ref, dh_ref, dob_ref, low_ref, ggain_ref, ow_ref,
):
    fill_out_weight(wall_ref, ow_ref)
    groups = wall_ref.shape[0]
    blocks, width = out_ref.shape[0], out_ref.shape[2]
    full = width * blocks
    gain = gain_ref[...]
    ggain = jnp.zeros((1, full), F32)
    for begin in range(0, h_ref.shape[0], 256):
        here = pl.ds(begin, 256)
        h = h_ref[here, :]
        factor = lax.rsqrt(jnp.sum(h * h, axis=1, keepdims=True) / full + EPSILON)
        dn = dna_ref[here, :] + dnb_ref[here, :]
        result = (h + (ya_ref[here, :] + yb_ref[here, :])).astype(BF16)
        for b in range(blocks):
            out_ref[b, here, :] = result[:, b * width : (b + 1) * width]
        weighted = dn * gain
        ggain = ggain + jnp.sum(dn * (h * factor), axis=0, keepdims=True)
        row_inner = jnp.sum(weighted * h, axis=1, keepdims=True)
        dh = (
            jnp.concatenate([c_ref[b, here, :] for b in range(blocks)], axis=1).astype(F32)
            + factor * weighted
            - h * (factor * factor * factor * row_inner / full)
        )
        dh_ref[here, :] = dh
        low_ref[here, :] = dh.astype(BF16)
        made = contract_last(low_ref[here, :], ow_ref[...]).astype(BF16)
        for b in range(blocks):
            dob_ref[b, here, :] = made[:, b * width : (b + 1) * width]
    ggain_ref[...] = ggain


def out_grad_kernel(ob_ref, low_ref, gout_ref):
    groups = gout_ref.shape[0]
    high, wide = gout_ref.shape[2], gout_ref.shape[3]
    for z in range(gout_ref.shape[1]):
        made = contract_rows(ob_ref[:, z * high : (z + 1) * high], low_ref[...]).astype(BF16)
        for g in range(groups):
            gout_ref[g, z] = made[:, g * wide : (g + 1) * wide]


def last_kernel(x_ref, dh_ref, parts_ref, gain_ref, out_ref, ggain_ref):
    blocks, width = x_ref.shape[0], x_ref.shape[2]
    full = width * blocks
    ggain_ref[...] = jnp.zeros_like(ggain_ref)
    for begin in range(0, x_ref.shape[1], 256):
        part = pl.ds(begin, 256)
        dn = parts_ref[0, part, :].astype(F32)
        for other in range(1, parts_ref.shape[0]):
            dn = dn + parts_ref[other, part, :].astype(F32)
        weighted = dn * gain_ref[...]
        total = jnp.zeros((256, 1), F32)
        inner = jnp.zeros((256, 1), F32)
        for b in range(blocks):
            cols = slice(b * width, (b + 1) * width)
            value = x_ref[b, part, :].astype(F32)
            total = total + jnp.sum(value * value, axis=1, keepdims=True)
            inner = inner + jnp.sum(weighted[:, cols] * value, axis=1, keepdims=True)
        factor = lax.rsqrt(total / full + EPSILON)
        slope = factor * factor * factor * inner / full
        for b in range(blocks):
            cols = slice(b * width, (b + 1) * width)
            value = x_ref[b, part, :].astype(F32)
            ggain_ref[:, cols] += jnp.sum(dn[:, cols] * value * factor, axis=0, keepdims=True)
            out_ref[b, part, :] = (
                dh_ref[part, cols] + factor * weighted[:, cols] - value * slope
            ).astype(BF16)


def last(base, x, dh, parts, gain):
    rows, full = parts.shape[1], gain.shape[1]
    shape = (x.shape[0], rows, x.shape[2])
    return pl.pallas_call(
        last_kernel,
        grid=(1,),
        out_shape=(jax.ShapeDtypeStruct(shape, BF16), jax.ShapeDtypeStruct((1, full), F32)),
        in_specs=[
            once(shape, (0, base // rows, 0)),
            once((rows, full), (base // rows, 0)),
            once(parts.shape),
            once(gain.shape),
        ],
        out_specs=(once(shape), once((1, full))),
        compiler_params=compiler_params(56),
    )(x, dh, parts, gain)


def by_layers():
    def run(
        tokens,
        first_values,
        segment_ids,
        cotangent,
        qkv_weight,
        out_weight,
        gate_up_weight,
        down_weight,
        attn_gain,
        mlp_gain,
    ):
        dp, z, f = (lax.axis_index(a) for a in ("dp", "head", "ffn"))
        depth, side = lax.axis_size("head"), lax.axis_size("ffn")
        group = 2 * side
        length, width = tokens.shape[1], tokens.shape[2]
        half = length // 2
        full_width = width * depth
        seq_len = length * side
        lanes = 2 * HD
        hidden = down_weight.shape[0]
        padded = -(-hidden // lanes) * lanes
        layer = ("dp", "ffn")
        vmem = pl.BlockSpec(memory_space=pltpu.VMEM)

        def to_layers(values):
            keep = lax.dynamic_slice(values, (depth, dp * half, 0), (2, half, width))
            give = lax.dynamic_slice(values, (depth, (1 - dp) * half, 0), (2, half, width))
            got = swap(give)
            early = jnp.where(dp == 0, keep, got)
            late = jnp.where(dp == 0, got, keep)
            return values[:depth], jnp.stack([early[0], late[0], early[1], late[1]])

        def from_layers(main, shared):
            keep = jnp.where(dp == 0, shared[0::2], shared[1::2])
            got = swap(jnp.where(dp == 0, shared[1::2], shared[0::2]))
            early = jnp.where(dp == 0, keep, got)
            late = jnp.where(dp == 0, got, keep)
            return jnp.concatenate([main, jnp.concatenate([early, late], axis=1)], axis=0)

        other_ids = swap(segment_ids)
        pick = depth + z // 2
        ids = [
            lax.dynamic_index_in_dim(segment_ids, z, 0, keepdims=False),
            lax.dynamic_index_in_dim(other_ids, z, 0, keepdims=False),
            jnp.where(
                z % 2 == dp,
                lax.dynamic_index_in_dim(segment_ids, pick, 0, keepdims=False),
                lax.dynamic_index_in_dim(other_ids, pick, 0, keepdims=False),
            ),
        ]
        ids = jnp.stack(ids)
        numbers = jnp.arange(8, dtype=jnp.int32)[None, :, None]
        lower = jnp.sum((ids[:, None, :] < numbers).astype(jnp.int32), axis=2, keepdims=True)
        starts = jnp.sum(jnp.where(ids[:, None, :] == numbers, lower, 0), axis=1)
        lows = starts[:, ::BQ] // BK

        places = jnp.arange(seq_len, dtype=jnp.int32)
        cos, sin = rope_tables(places, HD)
        cos = jnp.concatenate([cos, cos], axis=1)
        sin = jnp.concatenate([-sin[:, : HD // 2], sin[:, HD // 2 :]], axis=1)
        sin = jnp.concatenate([sin, sin], axis=1)

        out_rows = out_weight.shape[0]
        def in_tiles(values):
            values = jnp.pad(values, ((0, 0), (0, padded - hidden)))
            return values.reshape(-1, padded // lanes, lanes).transpose(1, 0, 2).reshape(-1, lanes)

        wall = jnp.concatenate(
            [out_weight, in_tiles(gate_up_weight[:, 0]), in_tiles(gate_up_weight[:, 1]), down_weight],
            axis=0,
        )
        deep = qkv_weight.shape[0]
        part = qkv_weight.reshape(deep, 3, 2, lanes).transpose(2, 1, 0, 3).reshape(-1, lanes)
        pieces = in_pieces(jnp.concatenate([attn_gain, mlp_gain]).reshape(-1, lanes))
        tail = jnp.concatenate(pieces + [jnp.zeros((4, lanes), BF16)], axis=0)
        part = jnp.concatenate([part, tail], axis=0)
        part = exchange(jnp.broadcast_to(part[None], (depth,) + part.shape), "head")
        tail = part[:, 6 * deep :].astype(F32)
        step = 2 * width // lanes
        gains = tail[:, :step] + tail[:, step : 2 * step] + tail[:, 2 * step : 3 * step]
        gains = gains.reshape(depth, 2, width).transpose(1, 0, 2).reshape(2, 1, full_width)
        part = part[:, : 6 * deep].reshape(depth, 2, 3, deep, lanes)
        part = part.transpose(1, 0, 2, 3, 4).reshape(group, 3, deep, lanes)
        part = exchange(part, layer)
        weight = part.transpose(0, 2, 1, 3).reshape(group * deep, 3 * lanes)

        x, x_got = send_line(jnp.concatenate(to_layers(tokens), axis=1))
        x_got, weight, cos, sin, starts = after(x_got, weight, cos, sin, starts)
        lows = starts[:, ::BQ] // BK
        x = join_line(x, x_got)
        first = jnp.concatenate(to_layers(first_values), axis=1)
        first, x = after(first, x)
        first_got = send_across(first)
        nm, ns = normalized(x, gains[0], side, length)
        wall, nm = after(wall, nm)
        wall = lax.all_gather(wall, ("dp", "ffn", "head"), axis=0, tiled=False)
        wall = wall.reshape(group, depth, wall.shape[1], lanes)
        nm = exchange(nm, "ffn")
        grad_blocks = jnp.concatenate(to_layers(cotangent), axis=1)
        grad_sends = line_sends(grad_blocks)
        nm, grad_blocks, grad_sends = after(nm, grad_blocks, grad_sends)
        first_got, ns, nm = after(first_got, ns, nm)
        first = join_across(first_got)

        def pair_halves(blocks):
            mine = lax.dynamic_slice_in_dim(blocks, dp * lanes, lanes, axis=2)
            return mine, swap(lax.dynamic_slice_in_dim(blocks, (1 - dp) * lanes, lanes, axis=2))

        def pair_join(mine, theirs):
            return lane_join(mine, swap(theirs))

        def lane_join(mine, got):
            return jnp.where(
                dp == 0,
                jnp.concatenate([mine, got], axis=2),
                jnp.concatenate([got, mine], axis=2),
            )

        def by_core(shared):
            shared = shared.reshape(side, 2, half, lanes)
            return (
                lax.dynamic_index_in_dim(shared, dp, 1, keepdims=False),
                lax.dynamic_index_in_dim(shared, 1 - dp, 1, keepdims=False),
            )

        first_mine, first_got = pair_halves(first)
        firsts = [(first_mine,), (first_got,), (first_mine, first_got)]
        core = dp.astype(jnp.int32).reshape(1)
        def attend_at(i, rows_in):
            return attend(
                core,
                lows[i],
                rows_in,
                weight,
                firsts[i],
                length if i == 2 else 0,
                starts[i][:, None],
                cos,
                sin,
            )

        ns = exchange(ns, "ffn")
        nm_other = swap(nm)
        kept = [attend_at(0, (nm,))]
        nm_other, ns, grad_sends, kept[0] = after(nm_other, ns, grad_sends, kept[0])
        grad_got = line_go(grad_sends)
        ns_other = swap(ns)
        kept.append(attend_at(1, (nm_other,)))
        ns_other, grad_got[0], kept[1] = after(ns_other, grad_got[0], kept[1])
        om = pair_join(
            kept[0][3].reshape(side, length, lanes), kept[1][3].reshape(side, length, lanes)
        )
        ns_other, om = after(ns_other, om)
        kept.append(attend_at(2, (ns, ns_other)))
        normed = [(nm,), (nm_other,), (ns, ns_other)]
        om = exchange(om, "ffn")
        om, grad_got[1], kept[2] = after(om, grad_got[1], kept[2])
        os_, om = after(pair_join(*by_core(kept[2][3])), om)
        os_ = exchange(os_, "ffn")

        rows = length + half
        whole = jax.ShapeDtypeStruct((rows, full_width), F32)
        whole_low = jax.ShapeDtypeStruct((rows, full_width), BF16)
        out_spec = pl.BlockSpec((group, depth, out_rows, lanes), lambda i: (0, 0, 0, 0))

        def fixed(shape):
            return pl.BlockSpec(
                shape, lambda i: (0,) * len(shape), pipeline_mode=pl.Buffered(1)
            )

        ow_scratch = pltpu.VMEM((out_rows * depth, group * lanes), BF16)
        h, n2, ob = pl.pallas_call(
            hidden_kernel,
            grid=(1,),
            out_shape=(whole, whole_low, whole_low),
            in_specs=[fixed(a.shape) for a in (om, os_, x)]
            + [out_spec, fixed((1, full_width))],
            out_specs=tuple(fixed((rows, full_width)) for _ in range(3)),
            scratch_shapes=[ow_scratch],
            compiler_params=compiler_params(56),
        )(om, os_, x, wall, gains[1])
        grad_got, n2 = after(grad_got, n2)
        grad_blocks = join_line(grad_blocks, grad_got)

        high = wall.shape[2]
        count = padded // lanes

        def feed_forward(begin_tile, end_tile):
            wide = (end_tile - begin_tile) * lanes
            real = min(hidden, end_tile * lanes) - begin_tile * lanes
            grad_rows = 2 * (end_tile - begin_tile) * deep + real
            return pl.pallas_call(
                functools.partial(
                    mlp_kernel, begin_tile, real, out_rows, out_rows + 2 * count * deep
                ),
                grid=(depth,),
                out_shape=(
                    whole,
                    whole,
                    jax.ShapeDtypeStruct((group, depth, grad_rows, lanes), BF16),
                ),
                in_specs=[
                    fixed((rows, full_width)),
                    fixed((depth, rows, width)),
                    pl.BlockSpec((group, 1, high, lanes), lambda i: (0, i, 0, 0)),
                ],
                out_specs=(
                    fixed((rows, full_width)),
                    fixed((rows, full_width)),
                    pl.BlockSpec((group, 1, grad_rows, lanes), lambda i: (0, i, 0, 0)),
                ),
                scratch_shapes=[
                    pltpu.VMEM((full_width, 2 * wide), BF16),
                    pltpu.VMEM((wide, full_width), BF16),
                    pltpu.VMEM((full_width, rows), BF16),
                    pltpu.VMEM((rows, wide), BF16),
                    pltpu.VMEM((rows, 2 * wide), BF16),
                    pltpu.VMEM((rows, full_width), BF16),
                ],
                compiler_params=compiler_params(60),
            )(n2, grad_blocks, wall)

        ya, dna, grads_a = feed_forward(count - 2, count)
        n2, ya = after(n2, ya)
        yb, dnb, grads_b = feed_forward(0, count - 2)

        def layer_sum(grads):
            shape = grads.shape[1:]
            return lax.psum_scatter(grads, layer, scatter_dimension=0, tiled=True).reshape(shape)

        grads_a = layer_sum(grads_a)
        grads_b = layer_sum(grads_b)

        out, dh, dob, low, gain_two = pl.pallas_call(
            hidden_back_kernel,
            grid=(1,),
            out_shape=(
                jax.ShapeDtypeStruct(grad_blocks.shape, BF16),
                whole,
                jax.ShapeDtypeStruct(grad_blocks.shape, BF16),
                whole_low,
                jax.ShapeDtypeStruct((1, full_width), F32),
            ),
            in_specs=[fixed((rows, full_width))] * 5
            + [fixed(grad_blocks.shape), out_spec, fixed((1, full_width))],
            out_specs=tuple(
                fixed(s)
                for s in (
                    grad_blocks.shape,
                    (rows, full_width),
                    grad_blocks.shape,
                    (rows, full_width),
                    (1, full_width),
                )
            ),
            scratch_shapes=[ow_scratch],
            compiler_params=compiler_params(60),
        )(h, ya, yb, dna, dnb, grad_blocks, wall, gains[1])

        low, dob = after(low, dob)
        dob = exchange(dob, "ffn")
        gout_shape = (group, depth, out_rows, lanes)
        gout = pl.pallas_call(
            out_grad_kernel,
            grid=(1,),
            out_shape=jax.ShapeDtypeStruct(gout_shape, BF16),
            in_specs=[fixed((rows, full_width))] * 2,
            out_specs=fixed(gout_shape),
            compiler_params=compiler_params(48),
        )(ob, low)
        dob, gout = after(dob, gout)
        do_mine, do_got = pair_halves(dob)

        def back_of(i, grads_in):
            return attend_back(
                core,
                lows[i],
                normed[i],
                weight,
                kept[i],
                grads_in,
                length if i == 2 else 0,
                starts[i][None],
                cos,
                sin,
            )

        out, out_got = send_line(out)
        do_got, gout = after(do_got, gout)
        gout = exchange(gout, layer)
        dn_b, gw_b, gfv_b = back_of(1, (do_got,))
        dn_b, gw_b, gfv_b, out_got[0], out_got[1] = after(
            dn_b, gw_b, gfv_b, out_got[0], out_got[1]
        )
        do_mine, dn_b, gfv_b, grads_a = after(do_mine, dn_b, gfv_b, grads_a)
        grads_a, a_got = send_line(grads_a)
        dn_other = swap(dn_b)
        dn_a, gw_a, gfv_a = back_of(0, (do_mine,))
        dn_a, gw_a, gfv_a, dn_other, a_got, out_got[2], gout = after(
            dn_a, gw_a, gfv_a, dn_other, a_got, out_got[2], gout
        )
        gfv_other = swap(gfv_b)
        grads_a = join_line(grads_a, a_got)

        def add_low(mine, theirs):
            return (mine.astype(F32) + theirs.astype(F32)).astype(BF16)

        main_sum = add_low(dn_a, dn_other)
        out = join_line(out, out_got)
        gfv_main = lane_join(
            gfv_a.reshape(side, length, lanes), gfv_other.reshape(side, length, lanes)
        )
        gout = exchange_line(jnp.sum(gout.astype(F32), axis=0).astype(BF16))
        do_mine, main_sum, grads_b, gout = after(do_mine, main_sum, grads_b, gout)
        main_sum = exchange(main_sum, "ffn")
        grads_b, b_got = send_line(grads_b)
        dn_s, dn_t, gw_s, gfv_s = back_of(2, (do_mine, do_got))
        b_got, dn_s, dn_t, gw_s, gfv_s = after(b_got, dn_s, dn_t, gw_s, gfv_s)
        gfv_mine, gfv_theirs = by_core(gfv_s)
        dn_t, gfv_theirs = swap(dn_t), swap(gfv_theirs)
        shared_sum, main_sum, gfv_theirs = after(add_low(dn_s, dn_t), main_sum, gfv_theirs)
        gfv = jnp.concatenate([gfv_main, lane_join(gfv_mine, gfv_theirs)], axis=1)
        shared_sum = exchange(shared_sum, "ffn")
        tokm, gain_main = last(0, x, dh, main_sum, gains[0])
        shared_sum, tokm = after(shared_sum, tokm)
        shared_sum, tokm = after(shared_sum, tokm)
        tokm, tokm_got = send_line(tokm)
        gfv, shared_sum = after(gfv, shared_sum)
        gfv = exchange(gfv, "ffn")
        toks, gain_shared = last(length, x, dh, shared_sum, gains[0])
        grad_w = (gw_a + gw_b + gw_s).astype(BF16)
        grad_w = grad_w.reshape(3, lanes, group, deep).transpose(2, 0, 3, 1)
        grad_w = grad_w.reshape(group, 3 * deep, lanes)
        gain_both = jnp.concatenate([gain_main + gain_shared, gain_two]).reshape(-1, lanes)
        gain_rows = gain_both.shape[0]
        tail = jnp.concatenate(in_pieces(gain_both), axis=0)
        tail = jnp.broadcast_to(tail[None], (group,) + tail.shape)
        grad_w = jnp.concatenate([grad_w, tail], axis=1)
        toks, tokm_got = after(toks, tokm_got)
        toks, toks_got = send_line(toks)
        grad_w, gfv = after(grad_w, gfv)
        grad_w = exchange(grad_w, layer)
        gfv, toks_got = after(gfv, toks_got)
        gfv, gfv_got = send_line(gfv)
        tail = grad_w[:, 3 * deep :].astype(F32).reshape(group, 3, gain_rows, lanes)
        tail = jnp.sum(tail, axis=(0, 1)).reshape(2, depth, -1, lanes).transpose(1, 0, 2, 3)
        tail = jnp.concatenate(in_pieces(tail.reshape(depth, -1, lanes)), axis=1)
        grad_w = grad_w[:, : 3 * deep].reshape(2, side, 3, deep, lanes)
        grad_w = grad_w.transpose(1, 2, 0, 3, 4).reshape(depth, 6 * deep, lanes)
        grad_w, w_got = send_line(jnp.concatenate([grad_w, tail], axis=1))
        out_tokens = from_layers(out[:, :length], out[:, length:])
        grads_b = join_line(grads_b, b_got)
        token_grads = from_layers(join_line(tokm, tokm_got), join_line(toks, toks_got))
        grad_out = jnp.sum(gout.astype(F32), axis=0)

        def untile(values):
            return values.reshape(-1, deep, lanes).transpose(1, 0, 2).reshape(deep, -1)

        gates, ups, downs = [], [], []
        for grads, tiles_in in ((grads_b, count - 2), (grads_a, 2)):
            part = jnp.sum(grads.astype(F32), axis=0)
            gates.append(untile(part[: tiles_in * deep]))
            ups.append(untile(part[tiles_in * deep : 2 * tiles_in * deep]))
            downs.append(part[2 * tiles_in * deep :])
        grad_gate = jnp.stack(
            [jnp.concatenate(g, axis=1)[:, :hidden] for g in (gates, ups)], axis=1
        )
        grad_down = jnp.concatenate(downs, axis=0)
        gfv_got, w_got, grad_gate, grad_down, grad_out, out_tokens, token_grads = after(
            gfv_got, w_got, grad_gate, grad_down, grad_out, out_tokens, token_grads
        )
        grad_w = join_line(grad_w, w_got)
        tail = jnp.sum(grad_w[:, 6 * deep :].astype(F32).reshape(depth, 3, 2, width), axis=(0, 1))
        grad_qkv = jnp.sum(grad_w[:, : 6 * deep].astype(F32), axis=0).reshape(3, 2, deep, lanes)
        grad_qkv = grad_qkv.transpose(2, 0, 1, 3).reshape(deep, 3, width)
        gfv = join_line(gfv, gfv_got)
        value_grads = from_layers(gfv[:, :length], gfv[:, length:])

        return (
            out_tokens,
            token_grads,
            value_grads,
            grad_qkv,
            grad_out,
            grad_gate,
            grad_down,
            tail[0],
            tail[1],
        )

    return run


def fits_layers(mesh, seqs, seq_len, full_width, heads):
    sizes = dict(mesh.shape)
    return (
        sizes["dp"] == 2
        and sizes["head"] == 4
        and sizes["ffn"] == 4
        and seqs == 12
        and seq_len % (512 * 4) == 0
        and full_width == 1024
        and heads == 16
    )


def solution(mesh):
    in_specs = (
        P("dp", "ffn", "head"),
        P("dp", "ffn", "head"),
        P("dp", None),
        P("dp", "ffn", "head"),
        P(("dp", "ffn"), None, "head"),
        P("head", ("dp", "ffn")),
        P(("dp", "ffn"), None, "head"),
        P("head", ("dp", "ffn")),
        P("head"),
        P("head"),
    )
    out_specs = (
        P("dp", "ffn", "head"),
        P("dp", "ffn", "head"),
        P("dp", "ffn", "head"),
        P(("dp", "ffn"), None, "head"),
        P("head", ("dp", "ffn")),
        P(("dp", "ffn"), None, "head"),
        P("head", ("dp", "ffn")),
        P("head"),
        P("head"),
    )

    def program(*args):
        seqs, seq_len, full_width = args[0].shape
        heads = args[5].shape[0] // HD
        fast = fits_layers(mesh, seqs, seq_len, full_width, heads)
        body = by_layers() if fast else per_device
        return jax.shard_map(
            body, mesh=mesh, in_specs=in_specs, out_specs=out_specs, check_vma=False
        )(*args)

    return program
```

```python
import functools
import math

import jax
import jax.numpy as jnp
from jax import lax
from jax.experimental import pallas as pl
from jax.experimental.pallas import tpu as pltpu
from jax.sharding import PartitionSpec as P

HD = 64
MICRO = 4


EPSILON = 1e-06
MASKED = -1e30


def rope_tables(positions, head_size):
    half_size = head_size // 2
    exponent = jnp.arange(half_size, dtype=jnp.float32) * (2.0 / head_size)
    frequency = jnp.exp(exponent * -jnp.log(jnp.float32(10000.0)))
    angles = positions.astype(jnp.float32)[:, None] * frequency[None, :]
    angles = jnp.concatenate([angles, angles], axis=1)
    return (jnp.cos(angles), jnp.sin(angles))


def rotate(vectors, cos_table, sin_table):
    half_size = vectors.shape[-1] // 2
    turned = jnp.concatenate([-vectors[..., half_size:], vectors[..., :half_size]], axis=-1)
    return vectors * cos_table + turned * sin_table


def unrotate(gradient, cos_table, sin_table):
    half_size = gradient.shape[-1] // 2
    scaled = gradient * sin_table
    turned = jnp.concatenate([scaled[..., half_size:], -scaled[..., :half_size]], axis=-1)
    return gradient * cos_table + turned


def swiglu(gate_up):
    return jax.nn.silu(gate_up[:, 0]) * gate_up[:, 1]


def contract_rows(former, latter):
    return lax.dot_general(
        former, latter, (((0,), (0,)), ((), ())), preferred_element_type=jnp.float32
    )


def contract_last(former, latter):
    return lax.dot_general(
        former, latter, (((1,), (1,)), ((), ())), preferred_element_type=jnp.float32
    )


def gather_weights(qkv_weight, out_weight, gate_up_weight, down_weight):
    return (
        lax.all_gather(qkv_weight, ("dp", "ffn"), axis=0, tiled=True),
        lax.all_gather(out_weight, ("dp", "ffn"), axis=1, tiled=True),
        lax.all_gather(gate_up_weight, ("dp", "ffn"), axis=0, tiled=True),
        lax.all_gather(down_weight, ("dp", "ffn"), axis=1, tiled=True),
    )


def row_total(values):
    return lax.psum(values, "head")


def spread_rows(values):
    return lax.all_gather(values, "head", axis=1, tiled=True)


def spread_grads(values):
    return lax.all_gather(values, "head", axis=1, tiled=True)


def collect_rows(values):
    return lax.psum_scatter(
        values.astype(jnp.bfloat16), "head", scatter_dimension=1, tiled=True
    ).astype(jnp.float32)


def collect_grads(values):
    return lax.psum_scatter(
        values.astype(jnp.bfloat16), "head", scatter_dimension=1, tiled=True
    ).astype(jnp.float32)


def norm_forward(values, gain_vector, full_width):
    factor = lax.rsqrt(row_total(jnp.sum(values * values, axis=1)) / full_width + EPSILON)
    return (factor, values * factor[:, None] * gain_vector)


def norm_backward(values, factor, gain_vector, gradient, full_width):
    weighted = gradient * gain_vector
    row_inner = row_total(jnp.sum(weighted * values, axis=1))
    norm_grad = (
        factor[:, None] * weighted
        - values * (factor * factor * factor * row_inner / full_width)[:, None]
    )
    gain_grad = jnp.sum(gradient * values * factor[:, None], axis=0)
    return (norm_grad, gain_grad)


def masked_scores(queries, key_rows, query_places, key_places, query_ids, key_ids, score_scale):
    scores = (
        jnp.einsum("qhd,khd->hqk", queries, key_rows, preferred_element_type=jnp.float32)
        * score_scale
    )
    allowed = (key_places[None, :] <= query_places[:, None]) & (
        key_ids[None, :] == query_ids[:, None]
    )
    return jnp.where(allowed[None], scores, MASKED)


def attend_forward(
    queries, key_rows, value_rows, query_places, key_places, query_ids, key_ids, score_scale
):
    scores = masked_scores(
        queries, key_rows, query_places, key_places, query_ids, key_ids, score_scale
    )
    highest = jnp.max(scores, axis=2, keepdims=True)
    log_total = highest + jnp.log(jnp.sum(jnp.exp(scores - highest), axis=2, keepdims=True))
    weights = jnp.exp(scores - log_total).astype(jnp.bfloat16)
    attended = jnp.einsum("hqk,khd->qhd", weights, value_rows, preferred_element_type=jnp.float32)
    return (attended, log_total[:, :, 0])


def query_side(
    queries,
    key_rows,
    value_rows,
    grad_rows,
    log_total,
    query_places,
    key_places,
    query_ids,
    key_ids,
    score_scale,
):
    scores = masked_scores(
        queries, key_rows, query_places, key_places, query_ids, key_ids, score_scale
    )
    weights = jnp.exp(scores - log_total[:, :, None])
    weight_grad = jnp.einsum(
        "qhd,khd->hqk", grad_rows, value_rows, preferred_element_type=jnp.float32
    )
    row_inner = jnp.sum(weights * weight_grad, axis=2)
    score_grad = (weights * (weight_grad - row_inner[:, :, None])).astype(jnp.bfloat16)
    query_grad = (
        jnp.einsum("hqk,khd->qhd", score_grad, key_rows, preferred_element_type=jnp.float32)
        * score_scale
    )
    return (weights, score_grad, row_inner, query_grad)


def per_device(
    tokens,
    first_values,
    segment_ids,
    cotangent,
    qkv_weight,
    out_weight,
    gate_up_weight,
    down_weight,
    attn_gain,
    mlp_gain,
):
    seq_total = tokens.shape[0]
    local_len = tokens.shape[1]
    local_width = tokens.shape[2]
    full_width = local_width * lax.axis_size("head")
    seq_len = local_len * lax.axis_size("ffn")
    head_width = first_values.shape[2]
    head_local = head_width // HD
    hidden_local = down_weight.shape[0]
    score_scale = 1.0 / math.sqrt(HD)
    offset = lax.axis_index("ffn") * local_len
    own_places = offset + jnp.arange(local_len, dtype=jnp.int32)
    all_places = jnp.arange(seq_len, dtype=jnp.int32)
    cos_table, sin_table = rope_tables(own_places, HD)
    cos_table = cos_table[:, None, :]
    sin_table = sin_table[:, None, :]
    base_count = seq_total // MICRO
    remainder = seq_total % MICRO
    qkv_grads = jnp.zeros((full_width, 3, head_width), jnp.float32)
    out_grads = jnp.zeros((head_width, full_width), jnp.float32)
    gate_grads = jnp.zeros((full_width, 2, hidden_local), jnp.float32)
    down_grads = jnp.zeros((hidden_local, full_width), jnp.float32)
    attn_gain_grads = jnp.zeros((local_width,), jnp.float32)
    mlp_gain_grads = jnp.zeros((local_width,), jnp.float32)
    outputs = []
    token_grads = []
    value_grads = []
    seq_start = 0
    for micro_index in range(MICRO):
        seq_count = base_count + (1 if micro_index < remainder else 0)
        row_count = seq_count * local_len
        gathered = gather_weights(qkv_weight, out_weight, gate_up_weight, down_weight)
        qkv_matrix = gathered[0].reshape(full_width, 3 * head_width)
        out_matrix = gathered[1]
        gate_matrix = gathered[2].reshape(full_width, 2 * hidden_local)
        down_matrix = gathered[3]
        token_rows = (
            tokens[seq_start : seq_start + seq_count]
            .reshape(row_count, local_width)
            .astype(jnp.float32)
        )
        factor_one, normed_one = norm_forward(token_rows, attn_gain, full_width)
        normed_full = spread_rows(normed_one.astype(jnp.bfloat16))
        projected = jnp.dot(normed_full, qkv_matrix, preferred_element_type=jnp.float32)
        projected = projected.reshape(seq_count, local_len, 3, head_local, HD)
        queries = rotate(projected[:, :, 0], cos_table, sin_table).astype(jnp.bfloat16)
        key_local = rotate(projected[:, :, 1], cos_table, sin_table).astype(jnp.bfloat16)
        first_block = first_values[seq_start : seq_start + seq_count].reshape(
            seq_count, local_len, head_local, HD
        )
        value_local = (0.5 * projected[:, :, 2] + 0.5 * first_block.astype(jnp.float32)).astype(
            jnp.bfloat16
        )
        key_full, value_full = (
            lax.all_gather(
                key_local.reshape(seq_count, local_len, head_width), "ffn", axis=1, tiled=True
            ),
            lax.all_gather(
                value_local.reshape(seq_count, local_len, head_width), "ffn", axis=1, tiled=True
            ),
        )
        key_full = key_full.reshape(seq_count, seq_len, head_local, HD)
        value_full = value_full.reshape(seq_count, seq_len, head_local, HD)
        ids_full = segment_ids[seq_start : seq_start + seq_count]
        ids_own = lax.dynamic_slice_in_dim(ids_full, offset, local_len, axis=1)

        def forward_one(pieces):
            return attend_forward(
                pieces[0],
                pieces[1],
                pieces[2],
                own_places,
                all_places,
                pieces[3],
                pieces[4],
                score_scale,
            )

        attended, log_totals = lax.map(
            forward_one, (queries, key_full, value_full, ids_own, ids_full)
        )
        attended_low = attended.reshape(row_count, head_width).astype(jnp.bfloat16)
        branch = collect_rows(jnp.dot(attended_low, out_matrix, preferred_element_type=jnp.float32))
        hidden = token_rows + branch
        factor_two, normed_two = norm_forward(hidden, mlp_gain, full_width)
        normed_mlp = spread_rows(normed_two.astype(jnp.bfloat16))
        gate_up = jnp.dot(normed_mlp, gate_matrix, preferred_element_type=jnp.float32).reshape(
            row_count, 2, hidden_local
        )
        active, swiglu_back = jax.vjp(swiglu, gate_up)
        active_low = active.astype(jnp.bfloat16)
        mlp_branch = collect_rows(
            jnp.dot(active_low, down_matrix, preferred_element_type=jnp.float32)
        )
        outputs.append(
            (hidden + mlp_branch).astype(jnp.bfloat16).reshape(seq_count, local_len, local_width)
        )
        grad_out = cotangent[seq_start : seq_start + seq_count].reshape(row_count, local_width)
        grad_full = spread_grads(grad_out)
        active_grad = contract_last(grad_full, down_matrix)
        down_grads = down_grads + contract_rows(active_low, grad_full)
        gate_grad = (
            swiglu_back(active_grad)[0].astype(jnp.bfloat16).reshape(row_count, 2 * hidden_local)
        )
        gate_grads = gate_grads + contract_rows(normed_mlp, gate_grad).reshape(
            full_width, 2, hidden_local
        )
        normed_grad = collect_grads(contract_last(gate_grad, gate_matrix))
        back_two, gain_two = norm_backward(hidden, factor_two, mlp_gain, normed_grad, full_width)
        mlp_gain_grads = mlp_gain_grads + gain_two
        hidden_grad = grad_out.astype(jnp.float32) + back_two
        hidden_full = spread_grads(hidden_grad.astype(jnp.bfloat16))
        attended_grad = contract_last(hidden_full, out_matrix).astype(jnp.bfloat16)
        out_grads = out_grads + contract_rows(attended_low, hidden_full)
        grad_blocks = attended_grad.reshape(seq_count, local_len, head_local, HD)

        def backward_one(pieces):
            (
                queries_one,
                key_one,
                value_one,
                grad_one,
                total_one,
                own_ids,
                full_ids,
                own_key,
                own_value,
            ) = pieces
            weights, score_grad, row_inner, query_grad = query_side(
                queries_one,
                key_one,
                value_one,
                grad_one,
                total_one,
                own_places,
                all_places,
                own_ids,
                full_ids,
                score_scale,
            )
            key_grad = (
                jnp.einsum(
                    "hqk,qhd->khd", score_grad, queries_one, preferred_element_type=jnp.float32
                )
                * score_scale
            )
            value_grad = jnp.einsum(
                "hqk,qhd->khd",
                weights.astype(jnp.bfloat16),
                grad_one,
                preferred_element_type=jnp.float32,
            )
            key_value = jnp.stack([key_grad, value_grad], axis=1).reshape(seq_len, 2, head_width)
            return (
                query_grad,
                lax.psum_scatter(
                    key_value.astype(jnp.bfloat16), "ffn", scatter_dimension=0, tiled=True
                ).astype(jnp.float32),
            )

        query_grads, key_value_grads = lax.map(
            backward_one,
            (
                queries,
                key_full,
                value_full,
                grad_blocks,
                log_totals,
                ids_own,
                ids_full,
                key_local,
                value_local,
            ),
        )
        key_rot_grad = key_value_grads[:, :, 0].reshape(seq_count, local_len, head_local, HD)
        value_mix_grad = key_value_grads[:, :, 1].reshape(seq_count, local_len, head_local, HD)
        value_grads.append(
            (0.5 * value_mix_grad).astype(jnp.bfloat16).reshape(seq_count, local_len, head_width)
        )
        projected_grad = (
            jnp.stack(
                [
                    unrotate(query_grads, cos_table, sin_table),
                    unrotate(key_rot_grad, cos_table, sin_table),
                    0.5 * value_mix_grad,
                ],
                axis=2,
            )
            .astype(jnp.bfloat16)
            .reshape(row_count, 3 * head_width)
        )
        qkv_grads = qkv_grads + contract_rows(normed_full, projected_grad).reshape(
            full_width, 3, head_width
        )
        normed_grad_one = collect_grads(contract_last(projected_grad, qkv_matrix))
        back_one, gain_one = norm_backward(
            token_rows, factor_one, attn_gain, normed_grad_one, full_width
        )
        attn_gain_grads = attn_gain_grads + gain_one
        token_grads.append(
            (hidden_grad + back_one).astype(jnp.bfloat16).reshape(seq_count, local_len, local_width)
        )
        seq_start = seq_start + seq_count
    weight_sums = (
        lax.psum_scatter(
            qkv_grads.astype(jnp.bfloat16), ("dp", "ffn"), scatter_dimension=0, tiled=True
        ).astype(jnp.float32),
        lax.psum_scatter(
            out_grads.astype(jnp.bfloat16), ("dp", "ffn"), scatter_dimension=1, tiled=True
        ).astype(jnp.float32),
        lax.psum_scatter(
            gate_grads.astype(jnp.bfloat16), ("dp", "ffn"), scatter_dimension=0, tiled=True
        ).astype(jnp.float32),
        lax.psum_scatter(
            down_grads.astype(jnp.bfloat16), ("dp", "ffn"), scatter_dimension=1, tiled=True
        ).astype(jnp.float32),
    )
    gain_sums = lax.psum((attn_gain_grads, mlp_gain_grads), ("dp", "ffn"))
    return (
        jnp.concatenate(outputs, axis=0),
        jnp.concatenate(token_grads, axis=0),
        jnp.concatenate(value_grads, axis=0),
        weight_sums[0],
        weight_sums[1],
        weight_sums[2],
        weight_sums[3],
        gain_sums[0],
        gain_sums[1],
    )


BF16 = jnp.bfloat16
F32 = jnp.float32
BQ = 512
BK = 512
MASKED_SCORE = -1e30


def matmul(former, latter):
    return lax.dot_general(former, latter, (((1,), (0,)), ((), ())), preferred_element_type=F32)


def compiler_params(mib):
    return pltpu.CompilerParams(vmem_limit_bytes=mib * 1024 * 1024)


def exchange(blocks, axes):
    return lax.all_to_all(blocks, axes, 0, 0, tiled=True)


def line_sends(blocks, axis="head"):
    me = lax.axis_index(axis)
    return [
        lax.dynamic_index_in_dim(blocks, me ^ step, 0, keepdims=False)
        for step in range(1, blocks.shape[0])
    ]


def line_go(sends, axis="head"):
    count = len(sends) + 1
    return [
        lax.ppermute(send, axis, [(j, j ^ (step + 1)) for j in range(count)])
        for step, send in enumerate(sends)
    ]


def send_line(blocks, axis="head"):
    return blocks, line_go(line_sends(blocks, axis), axis)


def join_line(blocks, got, axis="head"):
    me = lax.axis_index(axis)
    got = after(*got)
    for step, piece in enumerate(got):
        blocks = lax.dynamic_update_index_in_dim(blocks, piece, me ^ (step + 1), 0)
    return blocks


def exchange_line(blocks, axis="head"):
    return join_line(*send_line(blocks, axis), axis)


def after(values, *earlier):
    return lax.optimization_barrier((values, *earlier))


def send_across(blocks):
    count = blocks.shape[0]
    me = lax.axis_index("ffn")
    got = []
    for step in range(count):
        pairs = []
        for j in range(count * count):
            h, f = divmod(j, count)
            pairs.append((j, (f ^ step) * count + h))
        send = lax.dynamic_index_in_dim(blocks, me ^ step, 0, keepdims=False)
        got.append(lax.ppermute(send, ("head", "ffn"), pairs))
    return got


def join_across(got):
    here = lax.axis_index("head")
    a, b, c, d = after(*got)
    return jnp.where(
        here % 2 == 0,
        jnp.where(here < 2, jnp.stack([a, b, c, d]), jnp.stack([c, d, a, b])),
        jnp.where(here < 2, jnp.stack([b, a, d, c]), jnp.stack([d, c, b, a])),
    )


def in_pieces(values):
    pieces = []
    for _ in range(3):
        piece = lax.reduce_precision(values, 8, 7)
        pieces.append(piece.astype(BF16))
        values = values - piece
    return pieces


def from_pieces(pieces):
    return sum(p.astype(F32) for p in pieces)


def swap(values):
    return lax.ppermute(values, "dp", [(0, 1), (1, 0)])


def swap_halves(values):
    low = (lax.broadcasted_iota(jnp.int32, values.shape, 1) % HD) < HD // 2
    lanes = values.shape[1]
    return jnp.where(
        low, pltpu.roll(values, lanes - HD // 2, 1), pltpu.roll(values, HD // 2, 1)
    )


def norm_kernel(x_ref, gain_ref, main_ref, shared_ref):
    blocks, rows, width = x_ref.shape
    for start in range(0, rows, 256):
        part = pl.ds(start, 256)
        values = [x_ref[b, part, :].astype(F32) for b in range(blocks)]
        total = sum(jnp.sum(v * v, axis=1, keepdims=True) for v in values)
        factor = lax.rsqrt(total / (width * blocks) + EPSILON)
        out_ref, base = main_ref, 0
        if start >= main_ref.shape[1]:
            out_ref, base = shared_ref, main_ref.shape[1]
        for b in range(blocks):
            cols = pl.ds(b * width, width)
            normed = (values[b] * factor * gain_ref[:, cols]).astype(BF16)
            for copy in range(out_ref.shape[0]):
                out_ref[copy, start - base : start - base + 256, cols] = normed


def normalized(x, gain, copies, length):
    shapes = [(copies, r, gain.shape[1]) for r in (length, x.shape[1] - length)]
    return pl.pallas_call(
        norm_kernel,
        grid=(1,),
        out_shape=tuple(jax.ShapeDtypeStruct(s, BF16) for s in shapes),
        in_specs=[once(x.shape), once(gain.shape)],
        out_specs=tuple(once(s) for s in shapes),
        compiler_params=compiler_params(48),
    )(x, gain)


def head_masks():
    lane = lax.broadcasted_iota(jnp.int32, (1, 2 * HD), 1)
    first = jnp.where(lane < HD, 1.0, 0.0).astype(BF16)
    return first, (1.0 - first.astype(F32)).astype(BF16)


def row_chunks(refs, side_ref):
    rows = refs[0].shape[1]
    chunks = []
    for number, ref in enumerate(refs):
        for block in range(ref.shape[0]):
            at = block * rows * len(refs)
            if len(refs) == 2:
                half = side_ref[0] if number == 0 else 1 - side_ref[0]
                at = pl.multiple_of(at + half * rows, rows)
            chunks.append((number, block, pl.ds(at, rows)))
    return chunks


def attend_kernel(count, side_ref, low_ref, *refs):
    n_refs, fv_refs = refs[:count], refs[count : 2 * count]
    w_ref, start_ref, cos_ref, sin_ref, q_ref, k_ref, v_ref, o_ref, lse_ref = refs[2 * count :]
    length = q_ref.shape[0]
    lanes = 2 * HD
    for number, block, rows in row_chunks(n_refs, side_ref):
        made = matmul(n_refs[number][block], w_ref[...])
        cos, sin = cos_ref[rows, :], sin_ref[rows, :]
        q = made[:, :lanes]
        k = made[:, lanes : 2 * lanes]
        q_ref[rows, :] = ((q * cos + swap_halves(q) * sin) * (1.0 / math.sqrt(HD))).astype(BF16)
        k_ref[rows, :] = (k * cos + swap_halves(k) * sin).astype(BF16)
        first = fv_refs[number][block].astype(F32)
        v_ref[rows, :] = (0.5 * made[:, 2 * lanes :] + 0.5 * first).astype(BF16)
    mask_a, mask_b = head_masks()
    lane = lax.broadcasted_iota(jnp.int32, (BQ, lanes), 1)
    for i in range(length // BQ):
        rows = pl.ds(i * BQ, BQ)
        q = q_ref[rows, :]
        both = jnp.concatenate([q * mask_a, q * mask_b], axis=0)
        start = start_ref[rows, :]
        start = jnp.concatenate([start, start], axis=0)
        place = i * BQ + lax.broadcasted_iota(jnp.int32, (BQ, 1), 0)
        place = jnp.concatenate([place, place], axis=0)

        def step(j, carry):
            top, total, acc = carry
            keys = pl.ds(pl.multiple_of(j * BK, BK), BK)
            s = contract_last(both, k_ref[keys, :])
            key = j * BK + lax.broadcasted_iota(jnp.int32, s.shape, 1)
            s = jnp.where((key >= start) & (key <= place), s, MASKED_SCORE)
            new_top = jnp.maximum(top, jnp.max(s, axis=1, keepdims=True))
            p = jnp.exp(s - new_top)
            scale = jnp.exp(top - new_top)
            total = total * scale + jnp.sum(p, axis=1, keepdims=True)
            acc = acc * scale + matmul(p.astype(BF16), v_ref[keys, :])
            return new_top, total, acc

        top, total, acc = lax.fori_loop(
            low_ref[i],
            (i * BQ + BQ - 1) // BK + 1,
            step,
            (
                jnp.full((2 * BQ, 1), MASKED_SCORE, F32),
                jnp.zeros((2 * BQ, 1), F32),
                jnp.zeros((2 * BQ, lanes), F32),
            ),
        )
        acc = acc / total
        lse = top + jnp.log(total)
        o_ref[rows, :] = jnp.where(lane < HD, acc[:BQ], acc[BQ:]).astype(BF16)
        lse_ref[rows, :] = jnp.where(
            lane < HD, jnp.broadcast_to(lse[:BQ], (BQ, lanes)), jnp.broadcast_to(lse[BQ:], (BQ, lanes))
        )


def once(shape, index=None):
    index = (0,) * len(shape) if index is None else index
    return pl.BlockSpec(shape, lambda i: index, pipeline_mode=pl.Buffered(1))


def attend(side, low, normed, weight, firsts, begin, start_col, cos, sin):
    count = len(normed)
    blocks, rows, _ = normed[0].shape
    length = start_col.shape[0]
    lanes = 2 * HD
    small = jax.ShapeDtypeStruct((length, lanes), BF16)
    scalar = pl.BlockSpec(memory_space=pltpu.SMEM)
    return pl.pallas_call(
        functools.partial(attend_kernel, count),
        grid=(1,),
        out_shape=(small, small, small, small, jax.ShapeDtypeStruct((length, lanes), F32)),
        in_specs=[scalar, scalar]
        + [once(n.shape) for n in normed]
        + [once((blocks, rows, lanes), (0, begin // rows, 0))] * count
        + [once(a.shape) for a in (weight, start_col, cos, sin)],
        out_specs=(once((length, lanes)),) * 5,
        compiler_params=compiler_params(48),
    )(side, low, *normed, *firsts, weight, start_col, cos, sin)


def attend_back_kernel(count, side_ref, low_ref, *refs):
    n_refs, do_refs = refs[:count], refs[count : 2 * count]
    w_ref, q_ref, k_ref, v_ref, o_ref, lse_ref, start_ref, cos_ref, sin_ref = refs[
        2 * count : 2 * count + 9
    ]
    dn_refs = refs[2 * count + 9 : 3 * count + 9]
    gw_ref, gfv_ref, dq_ref, dk_ref, dv_ref, dp_ref, do_ref = refs[3 * count + 9 :]
    length = q_ref.shape[0]
    lanes = 2 * HD
    chunks = row_chunks(n_refs, side_ref)
    for number, block, rows in chunks:
        do_ref[rows, :] = do_refs[number][block]
    dk_ref[...] = jnp.zeros_like(dk_ref)
    dv_ref[...] = jnp.zeros_like(dv_ref)
    mask_a, mask_b = head_masks()
    lane = lax.broadcasted_iota(jnp.int32, (BQ, lanes), 1)
    for i in range(length // BQ):
        rows = pl.ds(i * BQ, BQ)
        q, do = q_ref[rows, :], do_ref[rows, :]
        q2 = jnp.concatenate([q * mask_a, q * mask_b], axis=0)
        do2 = jnp.concatenate([do * mask_a, do * mask_b], axis=0)
        lse = jnp.transpose(lse_ref[rows, :])
        lse = jnp.concatenate([lse[0:1, :], lse[HD : HD + 1, :]], axis=1)
        inner = jnp.transpose(do.astype(F32) * o_ref[rows, :].astype(F32))
        inner = jnp.concatenate(
            [
                jnp.sum(inner[:HD], axis=0, keepdims=True),
                jnp.sum(inner[HD:], axis=0, keepdims=True),
            ],
            axis=1,
        )
        start = start_ref[:, rows]
        start = jnp.concatenate([start, start], axis=1)
        place = i * BQ + lax.broadcasted_iota(jnp.int32, (1, BQ), 1)
        place = jnp.concatenate([place, place], axis=1)

        def step(j, acc):
            keys = pl.ds(pl.multiple_of(j * BK, BK), BK)
            k, v = k_ref[keys, :], v_ref[keys, :]
            s = contract_last(k, q2)
            key = j * BK + lax.broadcasted_iota(jnp.int32, s.shape, 0)
            s = jnp.where((key >= start) & (key <= place), s, MASKED_SCORE)
            p = jnp.exp(s - lse)
            dp = contract_last(v, do2)
            ds = (p * (dp - inner)).astype(BF16)
            dv_ref[keys, :] += matmul(p.astype(BF16), do2)
            dk_ref[keys, :] += matmul(ds, q2)
            return acc + contract_rows(ds, k)

        acc = lax.fori_loop(
            low_ref[i], (i * BQ + BQ - 1) // BK + 1, step, jnp.zeros((2 * BQ, lanes), F32)
        )
        dq_ref[rows, :] = jnp.where(lane < HD, acc[:BQ], acc[BQ:]) * (1.0 / math.sqrt(HD))
    for begin in range(0, length, 512):
        rows = pl.ds(begin, 512)
        cos, sin = cos_ref[rows, :], sin_ref[rows, :]
        dq, dk = dq_ref[rows, :], dk_ref[rows, :]
        dv = (0.5 * dv_ref[rows, :]).astype(BF16)
        gfv_ref[rows, :] = dv
        dp_ref[rows, 0:lanes] = (dq * cos - swap_halves(dq) * sin).astype(BF16)
        dp_ref[rows, lanes : 2 * lanes] = (dk * cos - swap_halves(dk) * sin).astype(BF16)
        dp_ref[rows, 2 * lanes :] = dv
    for number, block, rows in chunks:
        part = dp_ref[rows, :]
        dn_refs[number][block] = contract_last(part, w_ref[...]).astype(BF16)
        made = contract_rows(part, n_refs[number][block])
        if number + block == 0:
            gw_ref[...] = made
        else:
            gw_ref[...] += made


def attend_back(side, low, normed, weight, kept, grads, begin, start_row, cos, sin):
    count = len(normed)
    blocks, rows, width = normed[0].shape
    length = start_row.shape[1]
    lanes = 2 * HD
    scalar = pl.BlockSpec(memory_space=pltpu.SMEM)
    return pl.pallas_call(
        functools.partial(attend_back_kernel, count),
        grid=(1,),
        out_shape=tuple(jax.ShapeDtypeStruct(n.shape, BF16) for n in normed)
        + (
            jax.ShapeDtypeStruct((3 * lanes, width), F32),
            jax.ShapeDtypeStruct((length, lanes), BF16),
        ),
        in_specs=[scalar, scalar]
        + [once(n.shape) for n in normed]
        + [once((blocks, rows, lanes), (0, begin // rows, 0))] * count
        + [once(a.shape) for a in (weight, *kept, start_row, cos, sin)],
        out_specs=tuple(once(n.shape) for n in normed)
        + (once((3 * lanes, width)), once((length, lanes))),
        scratch_shapes=[
            pltpu.VMEM((length, lanes), F32),
            pltpu.VMEM((length, lanes), F32),
            pltpu.VMEM((length, lanes), F32),
            pltpu.VMEM((length, 3 * lanes), BF16),
            pltpu.VMEM((length, lanes), BF16),
        ],
        compiler_params=compiler_params(56),
    )(side, low, *normed, *grads, weight, *kept, start_row, cos, sin)


def fill_out_weight(wall_ref, ow_ref):
    groups, depth, high, wide = wall_ref.shape
    for g in range(groups):
        for z in range(depth):
            ow_ref[z * high : (z + 1) * high, g * wide : (g + 1) * wide] = wall_ref[g, z]


def hidden_kernel(
    om_ref, os_ref, x_ref, wall_ref, gain_ref,
    h_ref, n_ref, ob_ref, ow_ref,
):
    fill_out_weight(wall_ref, ow_ref)
    blocks, width = x_ref.shape[0], x_ref.shape[2]
    base = 0
    for o in (om_ref, os_ref):
        rows = o.shape[1]
        for begin in range(0, rows, 256):
            part = pl.ds(begin, 256)
            here = pl.ds(base + begin, 256)
            for b in range(blocks):
                ob_ref[here, b * width : (b + 1) * width] = o[b, part, :]
            branch = matmul(ob_ref[here, :], ow_ref[...])
            total = jnp.zeros((256, 1), F32)
            for b in range(blocks):
                cols = slice(b * width, (b + 1) * width)
                h = x_ref[b, here, :].astype(F32) + branch[:, cols]
                h_ref[here, cols] = h
                total = total + jnp.sum(h * h, axis=1, keepdims=True)
            factor = lax.rsqrt(total / (width * blocks) + EPSILON)
            n_ref[here, :] = (h_ref[here, :] * factor * gain_ref[...]).astype(BF16)
        base += rows


def mlp_kernel(
    begin_tile, hidden, first, down_first,
    n_ref, c_ref, wall_ref, y_ref, dn_ref, grad_ref,
    g_ref, d_ref, nt_ref, act_ref, dgu_ref, dy_ref,
):
    groups, lanes = wall_ref.shape[0], wall_ref.shape[3]
    rows, width = n_ref.shape
    padded = d_ref.shape[0]
    deep = width // groups
    tiles = 2 * padded // lanes
    all_tiles = (down_first - first) // deep // 2

    @pl.when(pl.program_id(0) == 0)
    def _():
        y_ref[...] = jnp.zeros_like(y_ref)
        dn_ref[...] = jnp.zeros_like(dn_ref)
        nt_ref[...] = jnp.transpose(n_ref[...])
        for b in range(c_ref.shape[0]):
            part = c_ref.shape[2]
            dy_ref[:, b * part : (b + 1) * part] = c_ref[b]
        if padded > hidden:
            d_ref[hidden:, :] = jnp.zeros((padded - hidden, width), BF16)

    for g in range(groups):
        for t in range(tiles):
            column = begin_tile + t
            if t >= tiles // 2:
                column += all_tiles - tiles // 2
            at = first + column * deep
            g_ref[g * deep : (g + 1) * deep, t * lanes : (t + 1) * lanes] = wall_ref[
                g, 0, at : at + deep, :
            ]
        at = down_first + begin_tile * lanes
        d_ref[0:hidden, g * lanes : (g + 1) * lanes] = wall_ref[g, 0, at : at + hidden, :]
    for begin in range(0, rows, 256):
        part = pl.ds(begin, 256)
        gu = matmul(n_ref[part, :], g_ref[...])
        gate, up = gu[:, :padded], gu[:, padded:]
        sig = 1.0 / (1.0 + jnp.exp(-gate))
        silu = gate * sig
        act_ref[part, :] = (silu * up).astype(BF16)
        dact = contract_last(dy_ref[part, :], d_ref[...])
        dgu_ref[part, :padded] = (dact * up * sig * (1.0 + gate * (1.0 - sig))).astype(BF16)
        dgu_ref[part, padded:] = (dact * silu).astype(BF16)
        y_ref[part, :] += matmul(act_ref[part, :], d_ref[...])
        dn_ref[part, :] += contract_last(dgu_ref[part, :], g_ref[...])
    for begin in range(0, 2 * padded, 512):
        made = matmul(nt_ref[...], dgu_ref[:, begin : begin + 512]).astype(BF16)
        for g in range(groups):
            for t in range(512 // lanes):
                at = (begin // lanes + t) * deep
                grad_ref[g, 0, at : at + deep, :] = made[
                    g * deep : (g + 1) * deep, t * lanes : (t + 1) * lanes
                ]
    for begin in range(0, width, 512):
        made = contract_rows(act_ref[...], dy_ref[:, begin : begin + 512]).astype(BF16)
        for t in range(512 // lanes):
            grad_ref[begin // lanes + t, 0, tiles * deep :, :] = made[
                :hidden, t * lanes : (t + 1) * lanes
            ]


def hidden_back_kernel(
    h_ref, ya_ref, yb_ref, dna_ref, dnb_ref, c_ref, wall_ref, gain_ref,
    out_ref, dh_ref, dob_ref, low_ref, ggain_ref, ow_ref,
):
    fill_out_weight(wall_ref, ow_ref)
    groups = wall_ref.shape[0]
    blocks, width = out_ref.shape[0], out_ref.shape[2]
    full = width * blocks
    gain = gain_ref[...]
    ggain = jnp.zeros((1, full), F32)
    for begin in range(0, h_ref.shape[0], 256):
        here = pl.ds(begin, 256)
        h = h_ref[here, :]
        factor = lax.rsqrt(jnp.sum(h * h, axis=1, keepdims=True) / full + EPSILON)
        dn = dna_ref[here, :] + dnb_ref[here, :]
        result = (h + (ya_ref[here, :] + yb_ref[here, :])).astype(BF16)
        for b in range(blocks):
            out_ref[b, here, :] = result[:, b * width : (b + 1) * width]
        weighted = dn * gain
        ggain = ggain + jnp.sum(dn * (h * factor), axis=0, keepdims=True)
        row_inner = jnp.sum(weighted * h, axis=1, keepdims=True)
        dh = (
            jnp.concatenate([c_ref[b, here, :] for b in range(blocks)], axis=1).astype(F32)
            + factor * weighted
            - h * (factor * factor * factor * row_inner / full)
        )
        dh_ref[here, :] = dh
        low_ref[here, :] = dh.astype(BF16)
        made = contract_last(low_ref[here, :], ow_ref[...]).astype(BF16)
        for b in range(blocks):
            dob_ref[b, here, :] = made[:, b * width : (b + 1) * width]
    ggain_ref[...] = ggain


def out_grad_kernel(ob_ref, low_ref, gout_ref):
    groups = gout_ref.shape[0]
    high, wide = gout_ref.shape[2], gout_ref.shape[3]
    for z in range(gout_ref.shape[1]):
        made = contract_rows(ob_ref[:, z * high : (z + 1) * high], low_ref[...]).astype(BF16)
        for g in range(groups):
            gout_ref[g, z] = made[:, g * wide : (g + 1) * wide]


def last_kernel(x_ref, dh_ref, parts_ref, gain_ref, out_ref, ggain_ref):
    blocks, width = x_ref.shape[0], x_ref.shape[2]
    full = width * blocks
    ggain_ref[...] = jnp.zeros_like(ggain_ref)
    for begin in range(0, x_ref.shape[1], 256):
        part = pl.ds(begin, 256)
        dn = parts_ref[0, part, :].astype(F32)
        for other in range(1, parts_ref.shape[0]):
            dn = dn + parts_ref[other, part, :].astype(F32)
        weighted = dn * gain_ref[...]
        total = jnp.zeros((256, 1), F32)
        inner = jnp.zeros((256, 1), F32)
        for b in range(blocks):
            cols = slice(b * width, (b + 1) * width)
            value = x_ref[b, part, :].astype(F32)
            total = total + jnp.sum(value * value, axis=1, keepdims=True)
            inner = inner + jnp.sum(weighted[:, cols] * value, axis=1, keepdims=True)
        factor = lax.rsqrt(total / full + EPSILON)
        slope = factor * factor * factor * inner / full
        for b in range(blocks):
            cols = slice(b * width, (b + 1) * width)
            value = x_ref[b, part, :].astype(F32)
            ggain_ref[:, cols] += jnp.sum(dn[:, cols] * value * factor, axis=0, keepdims=True)
            out_ref[b, part, :] = (
                dh_ref[part, cols] + factor * weighted[:, cols] - value * slope
            ).astype(BF16)


def last(base, x, dh, parts, gain):
    rows, full = parts.shape[1], gain.shape[1]
    shape = (x.shape[0], rows, x.shape[2])
    return pl.pallas_call(
        last_kernel,
        grid=(1,),
        out_shape=(jax.ShapeDtypeStruct(shape, BF16), jax.ShapeDtypeStruct((1, full), F32)),
        in_specs=[
            once(shape, (0, base // rows, 0)),
            once((rows, full), (base // rows, 0)),
            once(parts.shape),
            once(gain.shape),
        ],
        out_specs=(once(shape), once((1, full))),
        compiler_params=compiler_params(56),
    )(x, dh, parts, gain)


def by_layers():
    def run(
        tokens,
        first_values,
        segment_ids,
        cotangent,
        qkv_weight,
        out_weight,
        gate_up_weight,
        down_weight,
        attn_gain,
        mlp_gain,
    ):
        dp, z, f = (lax.axis_index(a) for a in ("dp", "head", "ffn"))
        depth, side = lax.axis_size("head"), lax.axis_size("ffn")
        group = 2 * side
        length, width = tokens.shape[1], tokens.shape[2]
        half = length // 2
        full_width = width * depth
        seq_len = length * side
        lanes = 2 * HD
        hidden = down_weight.shape[0]
        padded = -(-hidden // lanes) * lanes
        layer = ("dp", "ffn")
        vmem = pl.BlockSpec(memory_space=pltpu.VMEM)

        def to_layers(values):
            keep = lax.dynamic_slice(values, (depth, dp * half, 0), (2, half, width))
            give = lax.dynamic_slice(values, (depth, (1 - dp) * half, 0), (2, half, width))
            got = swap(give)
            early = jnp.where(dp == 0, keep, got)
            late = jnp.where(dp == 0, got, keep)
            return values[:depth], jnp.stack([early[0], late[0], early[1], late[1]])

        def from_layers(main, shared):
            keep = jnp.where(dp == 0, shared[0::2], shared[1::2])
            got = swap(jnp.where(dp == 0, shared[1::2], shared[0::2]))
            early = jnp.where(dp == 0, keep, got)
            late = jnp.where(dp == 0, got, keep)
            return jnp.concatenate([main, jnp.concatenate([early, late], axis=1)], axis=0)

        other_ids = swap(segment_ids)
        pick = depth + z // 2
        ids = [
            lax.dynamic_index_in_dim(segment_ids, z, 0, keepdims=False),
            lax.dynamic_index_in_dim(other_ids, z, 0, keepdims=False),
            jnp.where(
                z % 2 == dp,
                lax.dynamic_index_in_dim(segment_ids, pick, 0, keepdims=False),
                lax.dynamic_index_in_dim(other_ids, pick, 0, keepdims=False),
            ),
        ]
        ids = jnp.stack(ids)
        numbers = jnp.arange(8, dtype=jnp.int32)[None, :, None]
        lower = jnp.sum((ids[:, None, :] < numbers).astype(jnp.int32), axis=2, keepdims=True)
        starts = jnp.sum(jnp.where(ids[:, None, :] == numbers, lower, 0), axis=1)
        lows = starts[:, ::BQ] // BK

        places = jnp.arange(seq_len, dtype=jnp.int32)
        cos, sin = rope_tables(places, HD)
        cos = jnp.concatenate([cos, cos], axis=1)
        sin = jnp.concatenate([-sin[:, : HD // 2], sin[:, HD // 2 :]], axis=1)
        sin = jnp.concatenate([sin, sin], axis=1)

        out_rows = out_weight.shape[0]
        def in_tiles(values):
            values = jnp.pad(values, ((0, 0), (0, padded - hidden)))
            return values.reshape(-1, padded // lanes, lanes).transpose(1, 0, 2).reshape(-1, lanes)

        wall = jnp.concatenate(
            [out_weight, in_tiles(gate_up_weight[:, 0]), in_tiles(gate_up_weight[:, 1]), down_weight],
            axis=0,
        )
        deep = qkv_weight.shape[0]
        part = qkv_weight.reshape(deep, 3, 2, lanes).transpose(2, 1, 0, 3).reshape(-1, lanes)
        pieces = in_pieces(jnp.concatenate([attn_gain, mlp_gain]).reshape(-1, lanes))
        tail = jnp.concatenate(pieces + [jnp.zeros((4, lanes), BF16)], axis=0)
        part = jnp.concatenate([part, tail], axis=0)
        part = exchange(jnp.broadcast_to(part[None], (depth,) + part.shape), "head")
        tail = part[:, 6 * deep :].astype(F32)
        step = 2 * width // lanes
        gains = tail[:, :step] + tail[:, step : 2 * step] + tail[:, 2 * step : 3 * step]
        gains = gains.reshape(depth, 2, width).transpose(1, 0, 2).reshape(2, 1, full_width)
        part = part[:, : 6 * deep].reshape(depth, 2, 3, deep, lanes)
        part = part.transpose(1, 0, 2, 3, 4).reshape(group, 3, deep, lanes)
        part = exchange(part, layer)
        weight = part.transpose(0, 2, 1, 3).reshape(group * deep, 3 * lanes)

        x, x_got = send_line(jnp.concatenate(to_layers(tokens), axis=1))
        x_got, weight, cos, sin, starts = after(x_got, weight, cos, sin, starts)
        lows = starts[:, ::BQ] // BK
        x = join_line(x, x_got)
        first = jnp.concatenate(to_layers(first_values), axis=1)
        first, x = after(first, x)
        first_got = send_across(first)
        nm, ns = normalized(x, gains[0], side, length)
        wall, nm = after(wall, nm)
        wall = lax.all_gather(wall, ("dp", "ffn", "head"), axis=0, tiled=False)
        wall = wall.reshape(group, depth, wall.shape[1], lanes)
        nm = exchange(nm, "ffn")
        grad_blocks = jnp.concatenate(to_layers(cotangent), axis=1)
        grad_sends = line_sends(grad_blocks)
        nm, grad_blocks, grad_sends = after(nm, grad_blocks, grad_sends)
        first_got, ns, nm = after(first_got, ns, nm)
        first = join_across(first_got)

        def pair_halves(blocks):
            mine = lax.dynamic_slice_in_dim(blocks, dp * lanes, lanes, axis=2)
            return mine, swap(lax.dynamic_slice_in_dim(blocks, (1 - dp) * lanes, lanes, axis=2))

        def pair_join(mine, theirs):
            return lane_join(mine, swap(theirs))

        def lane_join(mine, got):
            return jnp.where(
                dp == 0,
                jnp.concatenate([mine, got], axis=2),
                jnp.concatenate([got, mine], axis=2),
            )

        def by_core(shared):
            shared = shared.reshape(side, 2, half, lanes)
            return (
                lax.dynamic_index_in_dim(shared, dp, 1, keepdims=False),
                lax.dynamic_index_in_dim(shared, 1 - dp, 1, keepdims=False),
            )

        first_mine, first_got = pair_halves(first)
        firsts = [(first_mine,), (first_got,), (first_mine, first_got)]
        core = dp.astype(jnp.int32).reshape(1)
        def attend_at(i, rows_in):
            return attend(
                core,
                lows[i],
                rows_in,
                weight,
                firsts[i],
                length if i == 2 else 0,
                starts[i][:, None],
                cos,
                sin,
            )

        ns = exchange(ns, "ffn")
        nm_other = swap(nm)
        kept = [attend_at(0, (nm,))]
        nm_other, ns, grad_sends, kept[0] = after(nm_other, ns, grad_sends, kept[0])
        grad_got = line_go(grad_sends)
        ns_other = swap(ns)
        kept.append(attend_at(1, (nm_other,)))
        ns_other, grad_got[0], kept[1] = after(ns_other, grad_got[0], kept[1])
        om = pair_join(
            kept[0][3].reshape(side, length, lanes), kept[1][3].reshape(side, length, lanes)
        )
        ns_other, om = after(ns_other, om)
        kept.append(attend_at(2, (ns, ns_other)))
        normed = [(nm,), (nm_other,), (ns, ns_other)]
        om = exchange(om, "ffn")
        om, grad_got[1], kept[2] = after(om, grad_got[1], kept[2])
        os_, om = after(pair_join(*by_core(kept[2][3])), om)
        os_ = exchange(os_, "ffn")

        rows = length + half
        whole = jax.ShapeDtypeStruct((rows, full_width), F32)
        whole_low = jax.ShapeDtypeStruct((rows, full_width), BF16)
        out_spec = pl.BlockSpec((group, depth, out_rows, lanes), lambda i: (0, 0, 0, 0))

        def fixed(shape):
            return pl.BlockSpec(
                shape, lambda i: (0,) * len(shape), pipeline_mode=pl.Buffered(1)
            )

        ow_scratch = pltpu.VMEM((out_rows * depth, group * lanes), BF16)
        h, n2, ob = pl.pallas_call(
            hidden_kernel,
            grid=(1,),
            out_shape=(whole, whole_low, whole_low),
            in_specs=[fixed(a.shape) for a in (om, os_, x)]
            + [out_spec, fixed((1, full_width))],
            out_specs=tuple(fixed((rows, full_width)) for _ in range(3)),
            scratch_shapes=[ow_scratch],
            compiler_params=compiler_params(56),
        )(om, os_, x, wall, gains[1])
        grad_got, n2 = after(grad_got, n2)
        grad_blocks = join_line(grad_blocks, grad_got)

        high = wall.shape[2]
        count = padded // lanes

        def feed_forward(begin_tile, end_tile):
            wide = (end_tile - begin_tile) * lanes
            real = min(hidden, end_tile * lanes) - begin_tile * lanes
            grad_rows = 2 * (end_tile - begin_tile) * deep + real
            return pl.pallas_call(
                functools.partial(
                    mlp_kernel, begin_tile, real, out_rows, out_rows + 2 * count * deep
                ),
                grid=(depth,),
                out_shape=(
                    whole,
                    whole,
                    jax.ShapeDtypeStruct((group, depth, grad_rows, lanes), BF16),
                ),
                in_specs=[
                    fixed((rows, full_width)),
                    fixed((depth, rows, width)),
                    pl.BlockSpec((group, 1, high, lanes), lambda i: (0, i, 0, 0)),
                ],
                out_specs=(
                    fixed((rows, full_width)),
                    fixed((rows, full_width)),
                    pl.BlockSpec((group, 1, grad_rows, lanes), lambda i: (0, i, 0, 0)),
                ),
                scratch_shapes=[
                    pltpu.VMEM((full_width, 2 * wide), BF16),
                    pltpu.VMEM((wide, full_width), BF16),
                    pltpu.VMEM((full_width, rows), BF16),
                    pltpu.VMEM((rows, wide), BF16),
                    pltpu.VMEM((rows, 2 * wide), BF16),
                    pltpu.VMEM((rows, full_width), BF16),
                ],
                compiler_params=compiler_params(60),
            )(n2, grad_blocks, wall)

        ya, dna, grads_a = feed_forward(count - 2, count)
        n2, ya = after(n2, ya)
        yb, dnb, grads_b = feed_forward(0, count - 2)

        def layer_sum(grads):
            shape = grads.shape[1:]
            return lax.psum_scatter(grads, layer, scatter_dimension=0, tiled=True).reshape(shape)

        grads_a = layer_sum(grads_a)
        grads_b = layer_sum(grads_b)

        out, dh, dob, low, gain_two = pl.pallas_call(
            hidden_back_kernel,
            grid=(1,),
            out_shape=(
                jax.ShapeDtypeStruct(grad_blocks.shape, BF16),
                whole,
                jax.ShapeDtypeStruct(grad_blocks.shape, BF16),
                whole_low,
                jax.ShapeDtypeStruct((1, full_width), F32),
            ),
            in_specs=[fixed((rows, full_width))] * 5
            + [fixed(grad_blocks.shape), out_spec, fixed((1, full_width))],
            out_specs=tuple(
                fixed(s)
                for s in (
                    grad_blocks.shape,
                    (rows, full_width),
                    grad_blocks.shape,
                    (rows, full_width),
                    (1, full_width),
                )
            ),
            scratch_shapes=[ow_scratch],
            compiler_params=compiler_params(60),
        )(h, ya, yb, dna, dnb, grad_blocks, wall, gains[1])

        low, dob = after(low, dob)
        dob = exchange(dob, "ffn")
        gout_shape = (group, depth, out_rows, lanes)
        gout = pl.pallas_call(
            out_grad_kernel,
            grid=(1,),
            out_shape=jax.ShapeDtypeStruct(gout_shape, BF16),
            in_specs=[fixed((rows, full_width))] * 2,
            out_specs=fixed(gout_shape),
            compiler_params=compiler_params(48),
        )(ob, low)
        dob, gout = after(dob, gout)
        do_mine, do_got = pair_halves(dob)

        def back_of(i, grads_in):
            return attend_back(
                core,
                lows[i],
                normed[i],
                weight,
                kept[i],
                grads_in,
                length if i == 2 else 0,
                starts[i][None],
                cos,
                sin,
            )

        out, out_got = send_line(out)
        do_got, gout = after(do_got, gout)
        gout = exchange(gout, layer)
        dn_b, gw_b, gfv_b = back_of(1, (do_got,))
        dn_b, gw_b, gfv_b, out_got[0], out_got[1] = after(
            dn_b, gw_b, gfv_b, out_got[0], out_got[1]
        )
        do_mine, dn_b, gfv_b, grads_a = after(do_mine, dn_b, gfv_b, grads_a)
        grads_a, a_got = send_line(grads_a)
        dn_other = swap(dn_b)
        dn_a, gw_a, gfv_a = back_of(0, (do_mine,))
        dn_a, gw_a, gfv_a, dn_other, a_got, out_got[2], gout = after(
            dn_a, gw_a, gfv_a, dn_other, a_got, out_got[2], gout
        )
        gfv_other = swap(gfv_b)
        grads_a = join_line(grads_a, a_got)

        def add_low(mine, theirs):
            return (mine.astype(F32) + theirs.astype(F32)).astype(BF16)

        main_sum = add_low(dn_a, dn_other)
        out = join_line(out, out_got)
        gfv_main = lane_join(
            gfv_a.reshape(side, length, lanes), gfv_other.reshape(side, length, lanes)
        )
        gout = exchange_line(jnp.sum(gout.astype(F32), axis=0).astype(BF16))
        do_mine, main_sum, grads_b, gout = after(do_mine, main_sum, grads_b, gout)
        main_sum = exchange(main_sum, "ffn")
        grads_b, b_got = send_line(grads_b)
        dn_s, dn_t, gw_s, gfv_s = back_of(2, (do_mine, do_got))
        b_got, dn_s, dn_t, gw_s, gfv_s = after(b_got, dn_s, dn_t, gw_s, gfv_s)
        dn_t = swap(dn_t)
        tokm, gain_main = last(0, x, dh, main_sum, gains[0])
        shared_sum, tokm, gfv_s, gw_s = after(add_low(dn_s, dn_t), tokm, gfv_s, gw_s)
        shared_sum = exchange(shared_sum, "ffn")
        tokm, tokm_got = send_line(tokm)
        gfv_mine, gfv_theirs = by_core(gfv_s)
        gfv = lane_join(gfv_mine, swap(gfv_theirs))
        gfv = jnp.concatenate([gfv_main, gfv], axis=1)
        gfv, shared_sum, tokm_got = after(gfv, shared_sum, tokm_got)
        gfv = exchange(gfv, "ffn")
        toks, gain_shared = last(length, x, dh, shared_sum, gains[0])
        grad_w = (gw_a + gw_b + gw_s).astype(BF16)
        grad_w = grad_w.reshape(3, lanes, group, deep).transpose(2, 0, 3, 1)
        grad_w = grad_w.reshape(group, 3 * deep, lanes)
        gain_both = jnp.concatenate([gain_main + gain_shared, gain_two]).reshape(-1, lanes)
        gain_rows = gain_both.shape[0]
        tail = jnp.concatenate(in_pieces(gain_both), axis=0)
        tail = jnp.broadcast_to(tail[None], (group,) + tail.shape)
        grad_w = jnp.concatenate([grad_w, tail], axis=1)
        toks, toks_got = send_line(toks)
        grad_w, gfv = after(grad_w, gfv)
        grad_w = exchange(grad_w, layer)
        gfv, toks_got = after(gfv, toks_got)
        gfv, gfv_got = send_line(gfv)
        tail = grad_w[:, 3 * deep :].astype(F32).reshape(group, 3, gain_rows, lanes)
        tail = jnp.sum(tail, axis=(0, 1)).reshape(2, depth, -1, lanes).transpose(1, 0, 2, 3)
        tail = jnp.concatenate(in_pieces(tail.reshape(depth, -1, lanes)), axis=1)
        grad_w = grad_w[:, : 3 * deep].reshape(2, side, 3, deep, lanes)
        grad_w = grad_w.transpose(1, 2, 0, 3, 4).reshape(depth, 6 * deep, lanes)
        grad_w, w_got = send_line(jnp.concatenate([grad_w, tail], axis=1))
        out_tokens = from_layers(out[:, :length], out[:, length:])
        grads_b = join_line(grads_b, b_got)
        token_grads = from_layers(join_line(tokm, tokm_got), join_line(toks, toks_got))
        grad_out = jnp.sum(gout.astype(F32), axis=0)

        def untile(values):
            return values.reshape(-1, deep, lanes).transpose(1, 0, 2).reshape(deep, -1)

        gates, ups, downs = [], [], []
        for grads, tiles_in in ((grads_b, count - 2), (grads_a, 2)):
            part = jnp.sum(grads.astype(F32), axis=0)
            gates.append(untile(part[: tiles_in * deep]))
            ups.append(untile(part[tiles_in * deep : 2 * tiles_in * deep]))
            downs.append(part[2 * tiles_in * deep :])
        grad_gate = jnp.stack(
            [jnp.concatenate(g, axis=1)[:, :hidden] for g in (gates, ups)], axis=1
        )
        grad_down = jnp.concatenate(downs, axis=0)
        gfv_got, w_got, grad_gate, grad_down, grad_out, out_tokens, token_grads = after(
            gfv_got, w_got, grad_gate, grad_down, grad_out, out_tokens, token_grads
        )
        grad_w = join_line(grad_w, w_got)
        tail = jnp.sum(grad_w[:, 6 * deep :].astype(F32).reshape(depth, 3, 2, width), axis=(0, 1))
        grad_qkv = jnp.sum(grad_w[:, : 6 * deep].astype(F32), axis=0).reshape(3, 2, deep, lanes)
        grad_qkv = grad_qkv.transpose(2, 0, 1, 3).reshape(deep, 3, width)
        gfv = join_line(gfv, gfv_got)
        value_grads = from_layers(gfv[:, :length], gfv[:, length:])

        return (
            out_tokens,
            token_grads,
            value_grads,
            grad_qkv,
            grad_out,
            grad_gate,
            grad_down,
            tail[0],
            tail[1],
        )

    return run


def fits_layers(mesh, seqs, seq_len, full_width, heads):
    sizes = dict(mesh.shape)
    return (
        sizes["dp"] == 2
        and sizes["head"] == 4
        and sizes["ffn"] == 4
        and seqs == 12
        and seq_len % (512 * 4) == 0
        and full_width == 1024
        and heads == 16
    )


def solution(mesh):
    in_specs = (
        P("dp", "ffn", "head"),
        P("dp", "ffn", "head"),
        P("dp", None),
        P("dp", "ffn", "head"),
        P(("dp", "ffn"), None, "head"),
        P("head", ("dp", "ffn")),
        P(("dp", "ffn"), None, "head"),
        P("head", ("dp", "ffn")),
        P("head"),
        P("head"),
    )
    out_specs = (
        P("dp", "ffn", "head"),
        P("dp", "ffn", "head"),
        P("dp", "ffn", "head"),
        P(("dp", "ffn"), None, "head"),
        P("head", ("dp", "ffn")),
        P(("dp", "ffn"), None, "head"),
        P("head", ("dp", "ffn")),
        P("head"),
        P("head"),
    )

    def program(*args):
        seqs, seq_len, full_width = args[0].shape
        heads = args[5].shape[0] // HD
        fast = fits_layers(mesh, seqs, seq_len, full_width, heads)
        body = by_layers() if fast else per_device
        return jax.shard_map(
            body, mesh=mesh, in_specs=in_specs, out_specs=out_specs, check_vma=False
        )(*args)

    return program
```

```python
import functools
import math

import jax
import jax.numpy as jnp
from jax import lax
from jax.experimental import pallas as pl
from jax.experimental.pallas import tpu as pltpu
from jax.sharding import PartitionSpec as P

HD = 64
MICRO = 4


EPSILON = 1e-06
MASKED = -1e30


def rope_tables(positions, head_size):
    half_size = head_size // 2
    exponent = jnp.arange(half_size, dtype=jnp.float32) * (2.0 / head_size)
    frequency = jnp.exp(exponent * -jnp.log(jnp.float32(10000.0)))
    angles = positions.astype(jnp.float32)[:, None] * frequency[None, :]
    angles = jnp.concatenate([angles, angles], axis=1)
    return (jnp.cos(angles), jnp.sin(angles))


def rotate(vectors, cos_table, sin_table):
    half_size = vectors.shape[-1] // 2
    turned = jnp.concatenate([-vectors[..., half_size:], vectors[..., :half_size]], axis=-1)
    return vectors * cos_table + turned * sin_table


def unrotate(gradient, cos_table, sin_table):
    half_size = gradient.shape[-1] // 2
    scaled = gradient * sin_table
    turned = jnp.concatenate([scaled[..., half_size:], -scaled[..., :half_size]], axis=-1)
    return gradient * cos_table + turned


def swiglu(gate_up):
    return jax.nn.silu(gate_up[:, 0]) * gate_up[:, 1]


def contract_rows(former, latter):
    return lax.dot_general(
        former, latter, (((0,), (0,)), ((), ())), preferred_element_type=jnp.float32
    )


def contract_last(former, latter):
    return lax.dot_general(
        former, latter, (((1,), (1,)), ((), ())), preferred_element_type=jnp.float32
    )


def gather_weights(qkv_weight, out_weight, gate_up_weight, down_weight):
    return (
        lax.all_gather(qkv_weight, ("dp", "ffn"), axis=0, tiled=True),
        lax.all_gather(out_weight, ("dp", "ffn"), axis=1, tiled=True),
        lax.all_gather(gate_up_weight, ("dp", "ffn"), axis=0, tiled=True),
        lax.all_gather(down_weight, ("dp", "ffn"), axis=1, tiled=True),
    )


def row_total(values):
    return lax.psum(values, "head")


def spread_rows(values):
    return lax.all_gather(values, "head", axis=1, tiled=True)


def spread_grads(values):
    return lax.all_gather(values, "head", axis=1, tiled=True)


def collect_rows(values):
    return lax.psum_scatter(
        values.astype(jnp.bfloat16), "head", scatter_dimension=1, tiled=True
    ).astype(jnp.float32)


def collect_grads(values):
    return lax.psum_scatter(
        values.astype(jnp.bfloat16), "head", scatter_dimension=1, tiled=True
    ).astype(jnp.float32)


def norm_forward(values, gain_vector, full_width):
    factor = lax.rsqrt(row_total(jnp.sum(values * values, axis=1)) / full_width + EPSILON)
    return (factor, values * factor[:, None] * gain_vector)


def norm_backward(values, factor, gain_vector, gradient, full_width):
    weighted = gradient * gain_vector
    row_inner = row_total(jnp.sum(weighted * values, axis=1))
    norm_grad = (
        factor[:, None] * weighted
        - values * (factor * factor * factor * row_inner / full_width)[:, None]
    )
    gain_grad = jnp.sum(gradient * values * factor[:, None], axis=0)
    return (norm_grad, gain_grad)


def masked_scores(queries, key_rows, query_places, key_places, query_ids, key_ids, score_scale):
    scores = (
        jnp.einsum("qhd,khd->hqk", queries, key_rows, preferred_element_type=jnp.float32)
        * score_scale
    )
    allowed = (key_places[None, :] <= query_places[:, None]) & (
        key_ids[None, :] == query_ids[:, None]
    )
    return jnp.where(allowed[None], scores, MASKED)


def attend_forward(
    queries, key_rows, value_rows, query_places, key_places, query_ids, key_ids, score_scale
):
    scores = masked_scores(
        queries, key_rows, query_places, key_places, query_ids, key_ids, score_scale
    )
    highest = jnp.max(scores, axis=2, keepdims=True)
    log_total = highest + jnp.log(jnp.sum(jnp.exp(scores - highest), axis=2, keepdims=True))
    weights = jnp.exp(scores - log_total).astype(jnp.bfloat16)
    attended = jnp.einsum("hqk,khd->qhd", weights, value_rows, preferred_element_type=jnp.float32)
    return (attended, log_total[:, :, 0])


def query_side(
    queries,
    key_rows,
    value_rows,
    grad_rows,
    log_total,
    query_places,
    key_places,
    query_ids,
    key_ids,
    score_scale,
):
    scores = masked_scores(
        queries, key_rows, query_places, key_places, query_ids, key_ids, score_scale
    )
    weights = jnp.exp(scores - log_total[:, :, None])
    weight_grad = jnp.einsum(
        "qhd,khd->hqk", grad_rows, value_rows, preferred_element_type=jnp.float32
    )
    row_inner = jnp.sum(weights * weight_grad, axis=2)
    score_grad = (weights * (weight_grad - row_inner[:, :, None])).astype(jnp.bfloat16)
    query_grad = (
        jnp.einsum("hqk,khd->qhd", score_grad, key_rows, preferred_element_type=jnp.float32)
        * score_scale
    )
    return (weights, score_grad, row_inner, query_grad)


def per_device(
    tokens,
    first_values,
    segment_ids,
    cotangent,
    qkv_weight,
    out_weight,
    gate_up_weight,
    down_weight,
    attn_gain,
    mlp_gain,
):
    seq_total = tokens.shape[0]
    local_len = tokens.shape[1]
    local_width = tokens.shape[2]
    full_width = local_width * lax.axis_size("head")
    seq_len = local_len * lax.axis_size("ffn")
    head_width = first_values.shape[2]
    head_local = head_width // HD
    hidden_local = down_weight.shape[0]
    score_scale = 1.0 / math.sqrt(HD)
    offset = lax.axis_index("ffn") * local_len
    own_places = offset + jnp.arange(local_len, dtype=jnp.int32)
    all_places = jnp.arange(seq_len, dtype=jnp.int32)
    cos_table, sin_table = rope_tables(own_places, HD)
    cos_table = cos_table[:, None, :]
    sin_table = sin_table[:, None, :]
    base_count = seq_total // MICRO
    remainder = seq_total % MICRO
    qkv_grads = jnp.zeros((full_width, 3, head_width), jnp.float32)
    out_grads = jnp.zeros((head_width, full_width), jnp.float32)
    gate_grads = jnp.zeros((full_width, 2, hidden_local), jnp.float32)
    down_grads = jnp.zeros((hidden_local, full_width), jnp.float32)
    attn_gain_grads = jnp.zeros((local_width,), jnp.float32)
    mlp_gain_grads = jnp.zeros((local_width,), jnp.float32)
    outputs = []
    token_grads = []
    value_grads = []
    seq_start = 0
    for micro_index in range(MICRO):
        seq_count = base_count + (1 if micro_index < remainder else 0)
        row_count = seq_count * local_len
        gathered = gather_weights(qkv_weight, out_weight, gate_up_weight, down_weight)
        qkv_matrix = gathered[0].reshape(full_width, 3 * head_width)
        out_matrix = gathered[1]
        gate_matrix = gathered[2].reshape(full_width, 2 * hidden_local)
        down_matrix = gathered[3]
        token_rows = (
            tokens[seq_start : seq_start + seq_count]
            .reshape(row_count, local_width)
            .astype(jnp.float32)
        )
        factor_one, normed_one = norm_forward(token_rows, attn_gain, full_width)
        normed_full = spread_rows(normed_one.astype(jnp.bfloat16))
        projected = jnp.dot(normed_full, qkv_matrix, preferred_element_type=jnp.float32)
        projected = projected.reshape(seq_count, local_len, 3, head_local, HD)
        queries = rotate(projected[:, :, 0], cos_table, sin_table).astype(jnp.bfloat16)
        key_local = rotate(projected[:, :, 1], cos_table, sin_table).astype(jnp.bfloat16)
        first_block = first_values[seq_start : seq_start + seq_count].reshape(
            seq_count, local_len, head_local, HD
        )
        value_local = (0.5 * projected[:, :, 2] + 0.5 * first_block.astype(jnp.float32)).astype(
            jnp.bfloat16
        )
        key_full, value_full = (
            lax.all_gather(
                key_local.reshape(seq_count, local_len, head_width), "ffn", axis=1, tiled=True
            ),
            lax.all_gather(
                value_local.reshape(seq_count, local_len, head_width), "ffn", axis=1, tiled=True
            ),
        )
        key_full = key_full.reshape(seq_count, seq_len, head_local, HD)
        value_full = value_full.reshape(seq_count, seq_len, head_local, HD)
        ids_full = segment_ids[seq_start : seq_start + seq_count]
        ids_own = lax.dynamic_slice_in_dim(ids_full, offset, local_len, axis=1)

        def forward_one(pieces):
            return attend_forward(
                pieces[0],
                pieces[1],
                pieces[2],
                own_places,
                all_places,
                pieces[3],
                pieces[4],
                score_scale,
            )

        attended, log_totals = lax.map(
            forward_one, (queries, key_full, value_full, ids_own, ids_full)
        )
        attended_low = attended.reshape(row_count, head_width).astype(jnp.bfloat16)
        branch = collect_rows(jnp.dot(attended_low, out_matrix, preferred_element_type=jnp.float32))
        hidden = token_rows + branch
        factor_two, normed_two = norm_forward(hidden, mlp_gain, full_width)
        normed_mlp = spread_rows(normed_two.astype(jnp.bfloat16))
        gate_up = jnp.dot(normed_mlp, gate_matrix, preferred_element_type=jnp.float32).reshape(
            row_count, 2, hidden_local
        )
        active, swiglu_back = jax.vjp(swiglu, gate_up)
        active_low = active.astype(jnp.bfloat16)
        mlp_branch = collect_rows(
            jnp.dot(active_low, down_matrix, preferred_element_type=jnp.float32)
        )
        outputs.append(
            (hidden + mlp_branch).astype(jnp.bfloat16).reshape(seq_count, local_len, local_width)
        )
        grad_out = cotangent[seq_start : seq_start + seq_count].reshape(row_count, local_width)
        grad_full = spread_grads(grad_out)
        active_grad = contract_last(grad_full, down_matrix)
        down_grads = down_grads + contract_rows(active_low, grad_full)
        gate_grad = (
            swiglu_back(active_grad)[0].astype(jnp.bfloat16).reshape(row_count, 2 * hidden_local)
        )
        gate_grads = gate_grads + contract_rows(normed_mlp, gate_grad).reshape(
            full_width, 2, hidden_local
        )
        normed_grad = collect_grads(contract_last(gate_grad, gate_matrix))
        back_two, gain_two = norm_backward(hidden, factor_two, mlp_gain, normed_grad, full_width)
        mlp_gain_grads = mlp_gain_grads + gain_two
        hidden_grad = grad_out.astype(jnp.float32) + back_two
        hidden_full = spread_grads(hidden_grad.astype(jnp.bfloat16))
        attended_grad = contract_last(hidden_full, out_matrix).astype(jnp.bfloat16)
        out_grads = out_grads + contract_rows(attended_low, hidden_full)
        grad_blocks = attended_grad.reshape(seq_count, local_len, head_local, HD)

        def backward_one(pieces):
            (
                queries_one,
                key_one,
                value_one,
                grad_one,
                total_one,
                own_ids,
                full_ids,
                own_key,
                own_value,
            ) = pieces
            weights, score_grad, row_inner, query_grad = query_side(
                queries_one,
                key_one,
                value_one,
                grad_one,
                total_one,
                own_places,
                all_places,
                own_ids,
                full_ids,
                score_scale,
            )
            key_grad = (
                jnp.einsum(
                    "hqk,qhd->khd", score_grad, queries_one, preferred_element_type=jnp.float32
                )
                * score_scale
            )
            value_grad = jnp.einsum(
                "hqk,qhd->khd",
                weights.astype(jnp.bfloat16),
                grad_one,
                preferred_element_type=jnp.float32,
            )
            key_value = jnp.stack([key_grad, value_grad], axis=1).reshape(seq_len, 2, head_width)
            return (
                query_grad,
                lax.psum_scatter(
                    key_value.astype(jnp.bfloat16), "ffn", scatter_dimension=0, tiled=True
                ).astype(jnp.float32),
            )

        query_grads, key_value_grads = lax.map(
            backward_one,
            (
                queries,
                key_full,
                value_full,
                grad_blocks,
                log_totals,
                ids_own,
                ids_full,
                key_local,
                value_local,
            ),
        )
        key_rot_grad = key_value_grads[:, :, 0].reshape(seq_count, local_len, head_local, HD)
        value_mix_grad = key_value_grads[:, :, 1].reshape(seq_count, local_len, head_local, HD)
        value_grads.append(
            (0.5 * value_mix_grad).astype(jnp.bfloat16).reshape(seq_count, local_len, head_width)
        )
        projected_grad = (
            jnp.stack(
                [
                    unrotate(query_grads, cos_table, sin_table),
                    unrotate(key_rot_grad, cos_table, sin_table),
                    0.5 * value_mix_grad,
                ],
                axis=2,
            )
            .astype(jnp.bfloat16)
            .reshape(row_count, 3 * head_width)
        )
        qkv_grads = qkv_grads + contract_rows(normed_full, projected_grad).reshape(
            full_width, 3, head_width
        )
        normed_grad_one = collect_grads(contract_last(projected_grad, qkv_matrix))
        back_one, gain_one = norm_backward(
            token_rows, factor_one, attn_gain, normed_grad_one, full_width
        )
        attn_gain_grads = attn_gain_grads + gain_one
        token_grads.append(
            (hidden_grad + back_one).astype(jnp.bfloat16).reshape(seq_count, local_len, local_width)
        )
        seq_start = seq_start + seq_count
    weight_sums = (
        lax.psum_scatter(
            qkv_grads.astype(jnp.bfloat16), ("dp", "ffn"), scatter_dimension=0, tiled=True
        ).astype(jnp.float32),
        lax.psum_scatter(
            out_grads.astype(jnp.bfloat16), ("dp", "ffn"), scatter_dimension=1, tiled=True
        ).astype(jnp.float32),
        lax.psum_scatter(
            gate_grads.astype(jnp.bfloat16), ("dp", "ffn"), scatter_dimension=0, tiled=True
        ).astype(jnp.float32),
        lax.psum_scatter(
            down_grads.astype(jnp.bfloat16), ("dp", "ffn"), scatter_dimension=1, tiled=True
        ).astype(jnp.float32),
    )
    gain_sums = lax.psum((attn_gain_grads, mlp_gain_grads), ("dp", "ffn"))
    return (
        jnp.concatenate(outputs, axis=0),
        jnp.concatenate(token_grads, axis=0),
        jnp.concatenate(value_grads, axis=0),
        weight_sums[0],
        weight_sums[1],
        weight_sums[2],
        weight_sums[3],
        gain_sums[0],
        gain_sums[1],
    )


BF16 = jnp.bfloat16
F32 = jnp.float32
BQ = 512
BK = 512
MASKED_SCORE = -1e30


def matmul(former, latter):
    return lax.dot_general(former, latter, (((1,), (0,)), ((), ())), preferred_element_type=F32)


def compiler_params(mib):
    return pltpu.CompilerParams(vmem_limit_bytes=mib * 1024 * 1024)


def exchange(blocks, axes):
    return lax.all_to_all(blocks, axes, 0, 0, tiled=True)


def line_sends(blocks, axis="head"):
    me = lax.axis_index(axis)
    return [
        lax.dynamic_index_in_dim(blocks, me ^ step, 0, keepdims=False)
        for step in range(1, blocks.shape[0])
    ]


def line_go(sends, axis="head"):
    count = len(sends) + 1
    return [
        lax.ppermute(send, axis, [(j, j ^ (step + 1)) for j in range(count)])
        for step, send in enumerate(sends)
    ]


def send_line(blocks, axis="head"):
    return blocks, line_go(line_sends(blocks, axis), axis)


def join_line(blocks, got, axis="head"):
    me = lax.axis_index(axis)
    got = after(*got)
    for step, piece in enumerate(got):
        blocks = lax.dynamic_update_index_in_dim(blocks, piece, me ^ (step + 1), 0)
    return blocks


def exchange_line(blocks, axis="head"):
    return join_line(*send_line(blocks, axis), axis)


def after(values, *earlier):
    return lax.optimization_barrier((values, *earlier))


def send_across(blocks):
    count = blocks.shape[0]
    me = lax.axis_index("ffn")
    got = []
    for step in range(count):
        pairs = []
        for j in range(count * count):
            h, f = divmod(j, count)
            pairs.append((j, (f ^ step) * count + h))
        send = lax.dynamic_index_in_dim(blocks, me ^ step, 0, keepdims=False)
        got.append(lax.ppermute(send, ("head", "ffn"), pairs))
    return got


def join_across(got):
    here = lax.axis_index("head")
    a, b, c, d = after(*got)
    return jnp.where(
        here % 2 == 0,
        jnp.where(here < 2, jnp.stack([a, b, c, d]), jnp.stack([c, d, a, b])),
        jnp.where(here < 2, jnp.stack([b, a, d, c]), jnp.stack([d, c, b, a])),
    )


def in_pieces(values):
    pieces = []
    for _ in range(3):
        piece = lax.reduce_precision(values, 8, 7)
        pieces.append(piece.astype(BF16))
        values = values - piece
    return pieces


def from_pieces(pieces):
    return sum(p.astype(F32) for p in pieces)


def swap(values):
    return lax.ppermute(values, "dp", [(0, 1), (1, 0)])


def swap_halves(values):
    low = (lax.broadcasted_iota(jnp.int32, values.shape, 1) % HD) < HD // 2
    lanes = values.shape[1]
    return jnp.where(
        low, pltpu.roll(values, lanes - HD // 2, 1), pltpu.roll(values, HD // 2, 1)
    )


def norm_kernel(x_ref, gain_ref, main_ref, shared_ref):
    blocks, rows, width = x_ref.shape
    for start in range(0, rows, 256):
        part = pl.ds(start, 256)
        values = [x_ref[b, part, :].astype(F32) for b in range(blocks)]
        total = sum(jnp.sum(v * v, axis=1, keepdims=True) for v in values)
        factor = lax.rsqrt(total / (width * blocks) + EPSILON)
        out_ref, base = main_ref, 0
        if start >= main_ref.shape[1]:
            out_ref, base = shared_ref, main_ref.shape[1]
        for b in range(blocks):
            cols = pl.ds(b * width, width)
            normed = (values[b] * factor * gain_ref[:, cols]).astype(BF16)
            for copy in range(out_ref.shape[0]):
                out_ref[copy, start - base : start - base + 256, cols] = normed


def normalized(x, gain, copies, length):
    shapes = [(copies, r, gain.shape[1]) for r in (length, x.shape[1] - length)]
    return pl.pallas_call(
        norm_kernel,
        grid=(1,),
        out_shape=tuple(jax.ShapeDtypeStruct(s, BF16) for s in shapes),
        in_specs=[once(x.shape), once(gain.shape)],
        out_specs=tuple(once(s) for s in shapes),
        compiler_params=compiler_params(48),
    )(x, gain)


def head_masks():
    lane = lax.broadcasted_iota(jnp.int32, (1, 2 * HD), 1)
    first = jnp.where(lane < HD, 1.0, 0.0).astype(BF16)
    return first, (1.0 - first.astype(F32)).astype(BF16)


def row_chunks(refs, side_ref):
    rows = refs[0].shape[1]
    chunks = []
    for number, ref in enumerate(refs):
        for block in range(ref.shape[0]):
            at = block * rows * len(refs)
            if len(refs) == 2:
                half = side_ref[0] if number == 0 else 1 - side_ref[0]
                at = pl.multiple_of(at + half * rows, rows)
            chunks.append((number, block, pl.ds(at, rows)))
    return chunks


def attend_kernel(count, side_ref, low_ref, *refs):
    n_refs, fv_refs = refs[:count], refs[count : 2 * count]
    w_ref, start_ref, cos_ref, sin_ref, q_ref, k_ref, v_ref, o_ref, lse_ref = refs[2 * count :]
    length = q_ref.shape[0]
    lanes = 2 * HD
    for number, block, rows in row_chunks(n_refs, side_ref):
        made = matmul(n_refs[number][block], w_ref[...])
        cos, sin = cos_ref[rows, :], sin_ref[rows, :]
        q = made[:, :lanes]
        k = made[:, lanes : 2 * lanes]
        q_ref[rows, :] = ((q * cos + swap_halves(q) * sin) * (1.0 / math.sqrt(HD))).astype(BF16)
        k_ref[rows, :] = (k * cos + swap_halves(k) * sin).astype(BF16)
        first = fv_refs[number][block].astype(F32)
        v_ref[rows, :] = (0.5 * made[:, 2 * lanes :] + 0.5 * first).astype(BF16)
    mask_a, mask_b = head_masks()
    lane = lax.broadcasted_iota(jnp.int32, (BQ, lanes), 1)
    for i in range(length // BQ):
        rows = pl.ds(i * BQ, BQ)
        q = q_ref[rows, :]
        both = jnp.concatenate([q * mask_a, q * mask_b], axis=0)
        start = start_ref[rows, :]
        start = jnp.concatenate([start, start], axis=0)
        place = i * BQ + lax.broadcasted_iota(jnp.int32, (BQ, 1), 0)
        place = jnp.concatenate([place, place], axis=0)

        def step(j, carry):
            top, total, acc = carry
            keys = pl.ds(pl.multiple_of(j * BK, BK), BK)
            s = contract_last(both, k_ref[keys, :])
            key = j * BK + lax.broadcasted_iota(jnp.int32, s.shape, 1)
            s = jnp.where((key >= start) & (key <= place), s, MASKED_SCORE)
            new_top = jnp.maximum(top, jnp.max(s, axis=1, keepdims=True))
            p = jnp.exp(s - new_top)
            scale = jnp.exp(top - new_top)
            total = total * scale + jnp.sum(p, axis=1, keepdims=True)
            acc = acc * scale + matmul(p.astype(BF16), v_ref[keys, :])
            return new_top, total, acc

        top, total, acc = lax.fori_loop(
            low_ref[i],
            (i * BQ + BQ - 1) // BK + 1,
            step,
            (
                jnp.full((2 * BQ, 1), MASKED_SCORE, F32),
                jnp.zeros((2 * BQ, 1), F32),
                jnp.zeros((2 * BQ, lanes), F32),
            ),
        )
        acc = acc / total
        lse = top + jnp.log(total)
        o_ref[rows, :] = jnp.where(lane < HD, acc[:BQ], acc[BQ:]).astype(BF16)
        lse_ref[rows, :] = jnp.where(
            lane < HD, jnp.broadcast_to(lse[:BQ], (BQ, lanes)), jnp.broadcast_to(lse[BQ:], (BQ, lanes))
        )


def once(shape, index=None):
    index = (0,) * len(shape) if index is None else index
    return pl.BlockSpec(shape, lambda i: index, pipeline_mode=pl.Buffered(1))


def attend(side, low, normed, weight, firsts, begin, start_col, cos, sin):
    count = len(normed)
    blocks, rows, _ = normed[0].shape
    length = start_col.shape[0]
    lanes = 2 * HD
    small = jax.ShapeDtypeStruct((length, lanes), BF16)
    scalar = pl.BlockSpec(memory_space=pltpu.SMEM)
    return pl.pallas_call(
        functools.partial(attend_kernel, count),
        grid=(1,),
        out_shape=(small, small, small, small, jax.ShapeDtypeStruct((length, lanes), F32)),
        in_specs=[scalar, scalar]
        + [once(n.shape) for n in normed]
        + [once((blocks, rows, lanes), (0, begin // rows, 0))] * count
        + [once(a.shape) for a in (weight, start_col, cos, sin)],
        out_specs=(once((length, lanes)),) * 5,
        compiler_params=compiler_params(48),
    )(side, low, *normed, *firsts, weight, start_col, cos, sin)


def attend_back_kernel(count, side_ref, low_ref, *refs):
    n_refs, do_refs = refs[:count], refs[count : 2 * count]
    w_ref, q_ref, k_ref, v_ref, o_ref, lse_ref, start_ref, cos_ref, sin_ref = refs[
        2 * count : 2 * count + 9
    ]
    dn_refs = refs[2 * count + 9 : 3 * count + 9]
    gw_ref, gfv_ref, dq_ref, dk_ref, dv_ref, dp_ref, do_ref = refs[3 * count + 9 :]
    length = q_ref.shape[0]
    lanes = 2 * HD
    chunks = row_chunks(n_refs, side_ref)
    for number, block, rows in chunks:
        do_ref[rows, :] = do_refs[number][block]
    dk_ref[...] = jnp.zeros_like(dk_ref)
    dv_ref[...] = jnp.zeros_like(dv_ref)
    mask_a, mask_b = head_masks()
    lane = lax.broadcasted_iota(jnp.int32, (BQ, lanes), 1)
    for i in range(length // BQ):
        rows = pl.ds(i * BQ, BQ)
        q, do = q_ref[rows, :], do_ref[rows, :]
        q2 = jnp.concatenate([q * mask_a, q * mask_b], axis=0)
        do2 = jnp.concatenate([do * mask_a, do * mask_b], axis=0)
        lse = jnp.transpose(lse_ref[rows, :])
        lse = jnp.concatenate([lse[0:1, :], lse[HD : HD + 1, :]], axis=1)
        inner = jnp.transpose(do.astype(F32) * o_ref[rows, :].astype(F32))
        inner = jnp.concatenate(
            [
                jnp.sum(inner[:HD], axis=0, keepdims=True),
                jnp.sum(inner[HD:], axis=0, keepdims=True),
            ],
            axis=1,
        )
        start = start_ref[:, rows]
        start = jnp.concatenate([start, start], axis=1)
        place = i * BQ + lax.broadcasted_iota(jnp.int32, (1, BQ), 1)
        place = jnp.concatenate([place, place], axis=1)

        def step(j, acc):
            keys = pl.ds(pl.multiple_of(j * BK, BK), BK)
            k, v = k_ref[keys, :], v_ref[keys, :]
            s = contract_last(k, q2)
            key = j * BK + lax.broadcasted_iota(jnp.int32, s.shape, 0)
            s = jnp.where((key >= start) & (key <= place), s, MASKED_SCORE)
            p = jnp.exp(s - lse)
            dp = contract_last(v, do2)
            ds = (p * (dp - inner)).astype(BF16)
            dv_ref[keys, :] += matmul(p.astype(BF16), do2)
            dk_ref[keys, :] += matmul(ds, q2)
            return acc + contract_rows(ds, k)

        acc = lax.fori_loop(
            low_ref[i], (i * BQ + BQ - 1) // BK + 1, step, jnp.zeros((2 * BQ, lanes), F32)
        )
        dq_ref[rows, :] = jnp.where(lane < HD, acc[:BQ], acc[BQ:]) * (1.0 / math.sqrt(HD))
    for begin in range(0, length, 512):
        rows = pl.ds(begin, 512)
        cos, sin = cos_ref[rows, :], sin_ref[rows, :]
        dq, dk = dq_ref[rows, :], dk_ref[rows, :]
        dv = (0.5 * dv_ref[rows, :]).astype(BF16)
        gfv_ref[rows, :] = dv
        dp_ref[rows, 0:lanes] = (dq * cos - swap_halves(dq) * sin).astype(BF16)
        dp_ref[rows, lanes : 2 * lanes] = (dk * cos - swap_halves(dk) * sin).astype(BF16)
        dp_ref[rows, 2 * lanes :] = dv
    for number, block, rows in chunks:
        part = dp_ref[rows, :]
        dn_refs[number][block] = contract_last(part, w_ref[...]).astype(BF16)
        made = contract_rows(part, n_refs[number][block])
        if number + block == 0:
            gw_ref[...] = made
        else:
            gw_ref[...] += made


def attend_back(side, low, normed, weight, kept, grads, begin, start_row, cos, sin):
    count = len(normed)
    blocks, rows, width = normed[0].shape
    length = start_row.shape[1]
    lanes = 2 * HD
    scalar = pl.BlockSpec(memory_space=pltpu.SMEM)
    return pl.pallas_call(
        functools.partial(attend_back_kernel, count),
        grid=(1,),
        out_shape=tuple(jax.ShapeDtypeStruct(n.shape, BF16) for n in normed)
        + (
            jax.ShapeDtypeStruct((3 * lanes, width), F32),
            jax.ShapeDtypeStruct((length, lanes), BF16),
        ),
        in_specs=[scalar, scalar]
        + [once(n.shape) for n in normed]
        + [once((blocks, rows, lanes), (0, begin // rows, 0))] * count
        + [once(a.shape) for a in (weight, *kept, start_row, cos, sin)],
        out_specs=tuple(once(n.shape) for n in normed)
        + (once((3 * lanes, width)), once((length, lanes))),
        scratch_shapes=[
            pltpu.VMEM((length, lanes), F32),
            pltpu.VMEM((length, lanes), F32),
            pltpu.VMEM((length, lanes), F32),
            pltpu.VMEM((length, 3 * lanes), BF16),
            pltpu.VMEM((length, lanes), BF16),
        ],
        compiler_params=compiler_params(56),
    )(side, low, *normed, *grads, weight, *kept, start_row, cos, sin)


def fill_out_weight(wall_ref, ow_ref):
    groups, depth, high, wide = wall_ref.shape
    for g in range(groups):
        for z in range(depth):
            ow_ref[z * high : (z + 1) * high, g * wide : (g + 1) * wide] = wall_ref[g, z]


def hidden_kernel(
    om_ref, os_ref, x_ref, wall_ref, gain_ref,
    h_ref, n_ref, ob_ref, ow_ref,
):
    fill_out_weight(wall_ref, ow_ref)
    blocks, width = x_ref.shape[0], x_ref.shape[2]
    base = 0
    for o in (om_ref, os_ref):
        rows = o.shape[1]
        for begin in range(0, rows, 256):
            part = pl.ds(begin, 256)
            here = pl.ds(base + begin, 256)
            for b in range(blocks):
                ob_ref[here, b * width : (b + 1) * width] = o[b, part, :]
            branch = matmul(ob_ref[here, :], ow_ref[...])
            total = jnp.zeros((256, 1), F32)
            for b in range(blocks):
                cols = slice(b * width, (b + 1) * width)
                h = x_ref[b, here, :].astype(F32) + branch[:, cols]
                h_ref[here, cols] = h
                total = total + jnp.sum(h * h, axis=1, keepdims=True)
            factor = lax.rsqrt(total / (width * blocks) + EPSILON)
            n_ref[here, :] = (h_ref[here, :] * factor * gain_ref[...]).astype(BF16)
        base += rows


def mlp_kernel(
    begin_tile, hidden, first, down_first,
    n_ref, c_ref, wall_ref, y_ref, dn_ref, grad_ref,
    g_ref, d_ref, nt_ref, act_ref, dgu_ref, dy_ref,
):
    groups, lanes = wall_ref.shape[0], wall_ref.shape[3]
    rows, width = n_ref.shape
    padded = d_ref.shape[0]
    deep = width // groups
    tiles = 2 * padded // lanes
    all_tiles = (down_first - first) // deep // 2

    @pl.when(pl.program_id(0) == 0)
    def _():
        y_ref[...] = jnp.zeros_like(y_ref)
        dn_ref[...] = jnp.zeros_like(dn_ref)
        nt_ref[...] = jnp.transpose(n_ref[...])
        for b in range(c_ref.shape[0]):
            part = c_ref.shape[2]
            dy_ref[:, b * part : (b + 1) * part] = c_ref[b]
        if padded > hidden:
            d_ref[hidden:, :] = jnp.zeros((padded - hidden, width), BF16)

    for g in range(groups):
        for t in range(tiles):
            column = begin_tile + t
            if t >= tiles // 2:
                column += all_tiles - tiles // 2
            at = first + column * deep
            g_ref[g * deep : (g + 1) * deep, t * lanes : (t + 1) * lanes] = wall_ref[
                g, 0, at : at + deep, :
            ]
        at = down_first + begin_tile * lanes
        d_ref[0:hidden, g * lanes : (g + 1) * lanes] = wall_ref[g, 0, at : at + hidden, :]
    for begin in range(0, rows, 256):
        part = pl.ds(begin, 256)
        gu = matmul(n_ref[part, :], g_ref[...])
        gate, up = gu[:, :padded], gu[:, padded:]
        sig = 1.0 / (1.0 + jnp.exp(-gate))
        silu = gate * sig
        act_ref[part, :] = (silu * up).astype(BF16)
        dact = contract_last(dy_ref[part, :], d_ref[...])
        dgu_ref[part, :padded] = (dact * up * sig * (1.0 + gate * (1.0 - sig))).astype(BF16)
        dgu_ref[part, padded:] = (dact * silu).astype(BF16)
        y_ref[part, :] += matmul(act_ref[part, :], d_ref[...])
        dn_ref[part, :] += contract_last(dgu_ref[part, :], g_ref[...])
    for begin in range(0, 2 * padded, 512):
        made = matmul(nt_ref[...], dgu_ref[:, begin : begin + 512]).astype(BF16)
        for g in range(groups):
            for t in range(512 // lanes):
                at = (begin // lanes + t) * deep
                grad_ref[g, 0, at : at + deep, :] = made[
                    g * deep : (g + 1) * deep, t * lanes : (t + 1) * lanes
                ]
    for begin in range(0, width, 512):
        made = contract_rows(act_ref[...], dy_ref[:, begin : begin + 512]).astype(BF16)
        for t in range(512 // lanes):
            grad_ref[begin // lanes + t, 0, tiles * deep :, :] = made[
                :hidden, t * lanes : (t + 1) * lanes
            ]


def hidden_back_kernel(
    h_ref, ya_ref, yb_ref, dna_ref, dnb_ref, c_ref, wall_ref, gain_ref,
    out_ref, dh_ref, dob_ref, low_ref, ggain_ref, ow_ref,
):
    fill_out_weight(wall_ref, ow_ref)
    groups = wall_ref.shape[0]
    blocks, width = out_ref.shape[0], out_ref.shape[2]
    full = width * blocks
    gain = gain_ref[...]
    ggain = jnp.zeros((1, full), F32)
    for begin in range(0, h_ref.shape[0], 256):
        here = pl.ds(begin, 256)
        h = h_ref[here, :]
        factor = lax.rsqrt(jnp.sum(h * h, axis=1, keepdims=True) / full + EPSILON)
        dn = dna_ref[here, :] + dnb_ref[here, :]
        result = (h + (ya_ref[here, :] + yb_ref[here, :])).astype(BF16)
        for b in range(blocks):
            out_ref[b, here, :] = result[:, b * width : (b + 1) * width]
        weighted = dn * gain
        ggain = ggain + jnp.sum(dn * (h * factor), axis=0, keepdims=True)
        row_inner = jnp.sum(weighted * h, axis=1, keepdims=True)
        dh = (
            jnp.concatenate([c_ref[b, here, :] for b in range(blocks)], axis=1).astype(F32)
            + factor * weighted
            - h * (factor * factor * factor * row_inner / full)
        )
        dh_ref[here, :] = dh
        low_ref[here, :] = dh.astype(BF16)
        made = contract_last(low_ref[here, :], ow_ref[...]).astype(BF16)
        for b in range(blocks):
            dob_ref[b, here, :] = made[:, b * width : (b + 1) * width]
    ggain_ref[...] = ggain


def out_grad_kernel(ob_ref, low_ref, gout_ref):
    groups = gout_ref.shape[0]
    high, wide = gout_ref.shape[2], gout_ref.shape[3]
    for z in range(gout_ref.shape[1]):
        made = contract_rows(ob_ref[:, z * high : (z + 1) * high], low_ref[...]).astype(BF16)
        for g in range(groups):
            gout_ref[g, z] = made[:, g * wide : (g + 1) * wide]


def last_kernel(x_ref, dh_ref, parts_ref, gain_ref, out_ref, ggain_ref):
    blocks, width = x_ref.shape[0], x_ref.shape[2]
    full = width * blocks
    ggain_ref[...] = jnp.zeros_like(ggain_ref)
    for begin in range(0, x_ref.shape[1], 256):
        part = pl.ds(begin, 256)
        dn = parts_ref[0, part, :].astype(F32)
        for other in range(1, parts_ref.shape[0]):
            dn = dn + parts_ref[other, part, :].astype(F32)
        weighted = dn * gain_ref[...]
        total = jnp.zeros((256, 1), F32)
        inner = jnp.zeros((256, 1), F32)
        for b in range(blocks):
            cols = slice(b * width, (b + 1) * width)
            value = x_ref[b, part, :].astype(F32)
            total = total + jnp.sum(value * value, axis=1, keepdims=True)
            inner = inner + jnp.sum(weighted[:, cols] * value, axis=1, keepdims=True)
        factor = lax.rsqrt(total / full + EPSILON)
        slope = factor * factor * factor * inner / full
        for b in range(blocks):
            cols = slice(b * width, (b + 1) * width)
            value = x_ref[b, part, :].astype(F32)
            ggain_ref[:, cols] += jnp.sum(dn[:, cols] * value * factor, axis=0, keepdims=True)
            out_ref[b, part, :] = (
                dh_ref[part, cols] + factor * weighted[:, cols] - value * slope
            ).astype(BF16)


def last(base, x, dh, parts, gain):
    rows, full = parts.shape[1], gain.shape[1]
    shape = (x.shape[0], rows, x.shape[2])
    return pl.pallas_call(
        last_kernel,
        grid=(1,),
        out_shape=(jax.ShapeDtypeStruct(shape, BF16), jax.ShapeDtypeStruct((1, full), F32)),
        in_specs=[
            once(shape, (0, base // rows, 0)),
            once((rows, full), (base // rows, 0)),
            once(parts.shape),
            once(gain.shape),
        ],
        out_specs=(once(shape), once((1, full))),
        compiler_params=compiler_params(56),
    )(x, dh, parts, gain)


def by_layers():
    def run(
        tokens,
        first_values,
        segment_ids,
        cotangent,
        qkv_weight,
        out_weight,
        gate_up_weight,
        down_weight,
        attn_gain,
        mlp_gain,
    ):
        dp, z, f = (lax.axis_index(a) for a in ("dp", "head", "ffn"))
        depth, side = lax.axis_size("head"), lax.axis_size("ffn")
        group = 2 * side
        length, width = tokens.shape[1], tokens.shape[2]
        half = length // 2
        full_width = width * depth
        seq_len = length * side
        lanes = 2 * HD
        hidden = down_weight.shape[0]
        padded = -(-hidden // lanes) * lanes
        layer = ("dp", "ffn")
        vmem = pl.BlockSpec(memory_space=pltpu.VMEM)

        def to_layers(values):
            keep = lax.dynamic_slice(values, (depth, dp * half, 0), (2, half, width))
            give = lax.dynamic_slice(values, (depth, (1 - dp) * half, 0), (2, half, width))
            got = swap(give)
            early = jnp.where(dp == 0, keep, got)
            late = jnp.where(dp == 0, got, keep)
            return values[:depth], jnp.stack([early[0], late[0], early[1], late[1]])

        def from_layers(main, shared):
            keep = jnp.where(dp == 0, shared[0::2], shared[1::2])
            got = swap(jnp.where(dp == 0, shared[1::2], shared[0::2]))
            early = jnp.where(dp == 0, keep, got)
            late = jnp.where(dp == 0, got, keep)
            return jnp.concatenate([main, jnp.concatenate([early, late], axis=1)], axis=0)

        other_ids = swap(segment_ids)
        pick = depth + z // 2
        ids = [
            lax.dynamic_index_in_dim(segment_ids, z, 0, keepdims=False),
            lax.dynamic_index_in_dim(other_ids, z, 0, keepdims=False),
            jnp.where(
                z % 2 == dp,
                lax.dynamic_index_in_dim(segment_ids, pick, 0, keepdims=False),
                lax.dynamic_index_in_dim(other_ids, pick, 0, keepdims=False),
            ),
        ]
        ids = jnp.stack(ids)
        numbers = jnp.arange(8, dtype=jnp.int32)[None, :, None]
        lower = jnp.sum((ids[:, None, :] < numbers).astype(jnp.int32), axis=2, keepdims=True)
        starts = jnp.sum(jnp.where(ids[:, None, :] == numbers, lower, 0), axis=1)
        lows = starts[:, ::BQ] // BK

        places = jnp.arange(seq_len, dtype=jnp.int32)
        cos, sin = rope_tables(places, HD)
        cos = jnp.concatenate([cos, cos], axis=1)
        sin = jnp.concatenate([-sin[:, : HD // 2], sin[:, HD // 2 :]], axis=1)
        sin = jnp.concatenate([sin, sin], axis=1)

        out_rows = out_weight.shape[0]
        def in_tiles(values):
            values = jnp.pad(values, ((0, 0), (0, padded - hidden)))
            return values.reshape(-1, padded // lanes, lanes).transpose(1, 0, 2).reshape(-1, lanes)

        wall = jnp.concatenate(
            [out_weight, in_tiles(gate_up_weight[:, 0]), in_tiles(gate_up_weight[:, 1]), down_weight],
            axis=0,
        )
        deep = qkv_weight.shape[0]
        part = qkv_weight.reshape(deep, 3, 2, lanes).transpose(2, 1, 0, 3).reshape(-1, lanes)
        pieces = in_pieces(jnp.concatenate([attn_gain, mlp_gain]).reshape(-1, lanes))
        tail = jnp.concatenate(pieces + [jnp.zeros((4, lanes), BF16)], axis=0)
        part = jnp.concatenate([part, tail], axis=0)
        part = exchange(jnp.broadcast_to(part[None], (depth,) + part.shape), "head")
        tail = part[:, 6 * deep :].astype(F32)
        step = 2 * width // lanes
        gains = tail[:, :step] + tail[:, step : 2 * step] + tail[:, 2 * step : 3 * step]
        gains = gains.reshape(depth, 2, width).transpose(1, 0, 2).reshape(2, 1, full_width)
        part = part[:, : 6 * deep].reshape(depth, 2, 3, deep, lanes)
        part = part.transpose(1, 0, 2, 3, 4).reshape(group, 3, deep, lanes)
        part = exchange(part, layer)
        weight = part.transpose(0, 2, 1, 3).reshape(group * deep, 3 * lanes)

        x, x_got = send_line(jnp.concatenate(to_layers(tokens), axis=1))
        x_got, weight, cos, sin, starts = after(x_got, weight, cos, sin, starts)
        lows = starts[:, ::BQ] // BK
        x = join_line(x, x_got)
        first = jnp.concatenate(to_layers(first_values), axis=1)
        first, x = after(first, x)
        first_got = send_across(first)
        nm, ns = normalized(x, gains[0], side, length)
        wall, nm = after(wall, nm)
        wall = lax.all_gather(wall, ("dp", "ffn", "head"), axis=0, tiled=False)
        wall = wall.reshape(group, depth, wall.shape[1], lanes)
        nm = exchange(nm, "ffn")
        grad_blocks = jnp.concatenate(to_layers(cotangent), axis=1)
        grad_sends = line_sends(grad_blocks)
        nm, grad_blocks, grad_sends = after(nm, grad_blocks, grad_sends)
        first_got, ns, nm = after(first_got, ns, nm)
        first = join_across(first_got)

        def pair_halves(blocks):
            mine = lax.dynamic_slice_in_dim(blocks, dp * lanes, lanes, axis=2)
            return mine, swap(lax.dynamic_slice_in_dim(blocks, (1 - dp) * lanes, lanes, axis=2))

        def pair_join(mine, theirs):
            return lane_join(mine, swap(theirs))

        def lane_join(mine, got):
            return jnp.where(
                dp == 0,
                jnp.concatenate([mine, got], axis=2),
                jnp.concatenate([got, mine], axis=2),
            )

        def by_core(shared):
            shared = shared.reshape(side, 2, half, lanes)
            return (
                lax.dynamic_index_in_dim(shared, dp, 1, keepdims=False),
                lax.dynamic_index_in_dim(shared, 1 - dp, 1, keepdims=False),
            )

        first_mine, first_got = pair_halves(first)
        firsts = [(first_mine,), (first_got,), (first_mine, first_got)]
        core = dp.astype(jnp.int32).reshape(1)
        def attend_at(i, rows_in):
            return attend(
                core,
                lows[i],
                rows_in,
                weight,
                firsts[i],
                length if i == 2 else 0,
                starts[i][:, None],
                cos,
                sin,
            )

        ns = exchange(ns, "ffn")
        nm_other = swap(nm)
        kept = [attend_at(0, (nm,))]
        nm_other, ns, grad_sends, kept[0] = after(nm_other, ns, grad_sends, kept[0])
        grad_got = line_go(grad_sends)
        ns_other = swap(ns)
        kept.append(attend_at(1, (nm_other,)))
        ns_other, grad_got[0], kept[1] = after(ns_other, grad_got[0], kept[1])
        om = pair_join(
            kept[0][3].reshape(side, length, lanes), kept[1][3].reshape(side, length, lanes)
        )
        ns_other, om = after(ns_other, om)
        kept.append(attend_at(2, (ns, ns_other)))
        normed = [(nm,), (nm_other,), (ns, ns_other)]
        om = exchange(om, "ffn")
        om, grad_got[1], kept[2] = after(om, grad_got[1], kept[2])
        os_, om = after(pair_join(*by_core(kept[2][3])), om)
        os_ = exchange(os_, "ffn")

        rows = length + half
        whole = jax.ShapeDtypeStruct((rows, full_width), F32)
        whole_low = jax.ShapeDtypeStruct((rows, full_width), BF16)
        out_spec = pl.BlockSpec((group, depth, out_rows, lanes), lambda i: (0, 0, 0, 0))

        def fixed(shape):
            return pl.BlockSpec(
                shape, lambda i: (0,) * len(shape), pipeline_mode=pl.Buffered(1)
            )

        ow_scratch = pltpu.VMEM((out_rows * depth, group * lanes), BF16)
        h, n2, ob = pl.pallas_call(
            hidden_kernel,
            grid=(1,),
            out_shape=(whole, whole_low, whole_low),
            in_specs=[fixed(a.shape) for a in (om, os_, x)]
            + [out_spec, fixed((1, full_width))],
            out_specs=tuple(fixed((rows, full_width)) for _ in range(3)),
            scratch_shapes=[ow_scratch],
            compiler_params=compiler_params(56),
        )(om, os_, x, wall, gains[1])
        grad_got, n2 = after(grad_got, n2)
        grad_blocks = join_line(grad_blocks, grad_got)

        high = wall.shape[2]
        count = padded // lanes

        def feed_forward(begin_tile, end_tile):
            wide = (end_tile - begin_tile) * lanes
            real = min(hidden, end_tile * lanes) - begin_tile * lanes
            grad_rows = 2 * (end_tile - begin_tile) * deep + real
            return pl.pallas_call(
                functools.partial(
                    mlp_kernel, begin_tile, real, out_rows, out_rows + 2 * count * deep
                ),
                grid=(depth,),
                out_shape=(
                    whole,
                    whole,
                    jax.ShapeDtypeStruct((group, depth, grad_rows, lanes), BF16),
                ),
                in_specs=[
                    fixed((rows, full_width)),
                    fixed((depth, rows, width)),
                    pl.BlockSpec((group, 1, high, lanes), lambda i: (0, i, 0, 0)),
                ],
                out_specs=(
                    fixed((rows, full_width)),
                    fixed((rows, full_width)),
                    pl.BlockSpec((group, 1, grad_rows, lanes), lambda i: (0, i, 0, 0)),
                ),
                scratch_shapes=[
                    pltpu.VMEM((full_width, 2 * wide), BF16),
                    pltpu.VMEM((wide, full_width), BF16),
                    pltpu.VMEM((full_width, rows), BF16),
                    pltpu.VMEM((rows, wide), BF16),
                    pltpu.VMEM((rows, 2 * wide), BF16),
                    pltpu.VMEM((rows, full_width), BF16),
                ],
                compiler_params=compiler_params(60),
            )(n2, grad_blocks, wall)

        ya, dna, grads_a = feed_forward(count - 2, count)
        n2, ya = after(n2, ya)
        yb, dnb, grads_b = feed_forward(0, count - 2)

        def layer_sum(grads):
            shape = grads.shape[1:]
            return lax.psum_scatter(grads, layer, scatter_dimension=0, tiled=True).reshape(shape)

        grads_a = layer_sum(grads_a)
        grads_b = layer_sum(grads_b)

        out, dh, dob, low, gain_two = pl.pallas_call(
            hidden_back_kernel,
            grid=(1,),
            out_shape=(
                jax.ShapeDtypeStruct(grad_blocks.shape, BF16),
                whole,
                jax.ShapeDtypeStruct(grad_blocks.shape, BF16),
                whole_low,
                jax.ShapeDtypeStruct((1, full_width), F32),
            ),
            in_specs=[fixed((rows, full_width))] * 5
            + [fixed(grad_blocks.shape), out_spec, fixed((1, full_width))],
            out_specs=tuple(
                fixed(s)
                for s in (
                    grad_blocks.shape,
                    (rows, full_width),
                    grad_blocks.shape,
                    (rows, full_width),
                    (1, full_width),
                )
            ),
            scratch_shapes=[ow_scratch],
            compiler_params=compiler_params(60),
        )(h, ya, yb, dna, dnb, grad_blocks, wall, gains[1])

        low, dob = after(low, dob)
        dob = exchange(dob, "ffn")
        gout_shape = (group, depth, out_rows, lanes)
        gout = pl.pallas_call(
            out_grad_kernel,
            grid=(1,),
            out_shape=jax.ShapeDtypeStruct(gout_shape, BF16),
            in_specs=[fixed((rows, full_width))] * 2,
            out_specs=fixed(gout_shape),
            compiler_params=compiler_params(48),
        )(ob, low)
        dob, gout = after(dob, gout)
        do_mine, do_got = pair_halves(dob)

        def back_of(i, grads_in):
            return attend_back(
                core,
                lows[i],
                normed[i],
                weight,
                kept[i],
                grads_in,
                length if i == 2 else 0,
                starts[i][None],
                cos,
                sin,
            )

        out, out_got = send_line(out)
        do_got, gout = after(do_got, gout)
        gout = exchange(gout, layer)
        dn_b, gw_b, gfv_b = back_of(1, (do_got,))
        dn_b, gw_b, gfv_b, out_got[0], out_got[1] = after(
            dn_b, gw_b, gfv_b, out_got[0], out_got[1]
        )
        do_mine, dn_b, gfv_b, grads_a = after(do_mine, dn_b, gfv_b, grads_a)
        grads_a, a_got = send_line(grads_a)
        dn_other = swap(dn_b)
        dn_a, gw_a, gfv_a = back_of(0, (do_mine,))
        dn_a, gw_a, gfv_a, dn_other, a_got, out_got[2], gout = after(
            dn_a, gw_a, gfv_a, dn_other, a_got, out_got[2], gout
        )
        gfv_other = swap(gfv_b)
        grads_a = join_line(grads_a, a_got)

        def add_low(mine, theirs):
            return (mine.astype(F32) + theirs.astype(F32)).astype(BF16)

        main_sum = add_low(dn_a, dn_other)
        out = join_line(out, out_got)
        gfv_main = lane_join(
            gfv_a.reshape(side, length, lanes), gfv_other.reshape(side, length, lanes)
        )
        gout = exchange_line(jnp.sum(gout.astype(F32), axis=0).astype(BF16))
        do_mine, main_sum, grads_b, gout = after(do_mine, main_sum, grads_b, gout)
        main_sum = exchange(main_sum, "ffn")
        grads_b, b_got = send_line(grads_b)
        dn_s, dn_t, gw_s, gfv_s = back_of(2, (do_mine, do_got))
        b_got, dn_s, dn_t, gw_s, gfv_s = after(b_got, dn_s, dn_t, gw_s, gfv_s)
        dn_t = swap(dn_t)
        tokm, gain_main = last(0, x, dh, main_sum, gains[0])
        shared_sum, tokm = after(add_low(dn_s, dn_t), tokm)
        shared_sum = exchange(shared_sum, "ffn")
        tokm, tokm_got = send_line(tokm)
        tokm_got, gfv_s, gw_s, b_got = after(tokm_got, gfv_s, gw_s, b_got)
        gfv_mine, gfv_theirs = by_core(gfv_s)
        gfv = lane_join(gfv_mine, swap(gfv_theirs))
        gfv = jnp.concatenate([gfv_main, gfv], axis=1)
        gfv, shared_sum, tokm_got = after(gfv, shared_sum, tokm_got)
        gfv = exchange(gfv, "ffn")
        toks, gain_shared = last(length, x, dh, shared_sum, gains[0])
        grad_w = (gw_a + gw_b + gw_s).astype(BF16)
        grad_w = grad_w.reshape(3, lanes, group, deep).transpose(2, 0, 3, 1)
        grad_w = grad_w.reshape(group, 3 * deep, lanes)
        gain_both = jnp.concatenate([gain_main + gain_shared, gain_two]).reshape(-1, lanes)
        gain_rows = gain_both.shape[0]
        tail = jnp.concatenate(in_pieces(gain_both), axis=0)
        tail = jnp.broadcast_to(tail[None], (group,) + tail.shape)
        grad_w = jnp.concatenate([grad_w, tail], axis=1)
        toks, toks_got = send_line(toks)
        grad_w, gfv = after(grad_w, gfv)
        grad_w = exchange(grad_w, layer)
        gfv, toks_got = after(gfv, toks_got)
        gfv, gfv_got = send_line(gfv)
        tail = grad_w[:, 3 * deep :].astype(F32).reshape(group, 3, gain_rows, lanes)
        tail = jnp.sum(tail, axis=(0, 1)).reshape(2, depth, -1, lanes).transpose(1, 0, 2, 3)
        tail = jnp.concatenate(in_pieces(tail.reshape(depth, -1, lanes)), axis=1)
        grad_w = grad_w[:, : 3 * deep].reshape(2, side, 3, deep, lanes)
        grad_w = grad_w.transpose(1, 2, 0, 3, 4).reshape(depth, 6 * deep, lanes)
        grad_w, w_got = send_line(jnp.concatenate([grad_w, tail], axis=1))
        out_tokens = from_layers(out[:, :length], out[:, length:])
        grads_b = join_line(grads_b, b_got)
        token_grads = from_layers(join_line(tokm, tokm_got), join_line(toks, toks_got))
        grad_out = jnp.sum(gout.astype(F32), axis=0)

        def untile(values):
            return values.reshape(-1, deep, lanes).transpose(1, 0, 2).reshape(deep, -1)

        gates, ups, downs = [], [], []
        for grads, tiles_in in ((grads_b, count - 2), (grads_a, 2)):
            part = jnp.sum(grads.astype(F32), axis=0)
            gates.append(untile(part[: tiles_in * deep]))
            ups.append(untile(part[tiles_in * deep : 2 * tiles_in * deep]))
            downs.append(part[2 * tiles_in * deep :])
        grad_gate = jnp.stack(
            [jnp.concatenate(g, axis=1)[:, :hidden] for g in (gates, ups)], axis=1
        )
        grad_down = jnp.concatenate(downs, axis=0)
        gfv_got, w_got, grad_gate, grad_down, grad_out, out_tokens, token_grads = after(
            gfv_got, w_got, grad_gate, grad_down, grad_out, out_tokens, token_grads
        )
        grad_w = join_line(grad_w, w_got)
        tail = jnp.sum(grad_w[:, 6 * deep :].astype(F32).reshape(depth, 3, 2, width), axis=(0, 1))
        grad_qkv = jnp.sum(grad_w[:, : 6 * deep].astype(F32), axis=0).reshape(3, 2, deep, lanes)
        grad_qkv = grad_qkv.transpose(2, 0, 1, 3).reshape(deep, 3, width)
        gfv = join_line(gfv, gfv_got)
        value_grads = from_layers(gfv[:, :length], gfv[:, length:])

        return (
            out_tokens,
            token_grads,
            value_grads,
            grad_qkv,
            grad_out,
            grad_gate,
            grad_down,
            tail[0],
            tail[1],
        )

    return run


def fits_layers(mesh, seqs, seq_len, full_width, heads):
    sizes = dict(mesh.shape)
    return (
        sizes["dp"] == 2
        and sizes["head"] == 4
        and sizes["ffn"] == 4
        and seqs == 12
        and seq_len % (512 * 4) == 0
        and full_width == 1024
        and heads == 16
    )


def solution(mesh):
    in_specs = (
        P("dp", "ffn", "head"),
        P("dp", "ffn", "head"),
        P("dp", None),
        P("dp", "ffn", "head"),
        P(("dp", "ffn"), None, "head"),
        P("head", ("dp", "ffn")),
        P(("dp", "ffn"), None, "head"),
        P("head", ("dp", "ffn")),
        P("head"),
        P("head"),
    )
    out_specs = (
        P("dp", "ffn", "head"),
        P("dp", "ffn", "head"),
        P("dp", "ffn", "head"),
        P(("dp", "ffn"), None, "head"),
        P("head", ("dp", "ffn")),
        P(("dp", "ffn"), None, "head"),
        P("head", ("dp", "ffn")),
        P("head"),
        P("head"),
    )

    def program(*args):
        seqs, seq_len, full_width = args[0].shape
        heads = args[5].shape[0] // HD
        fast = fits_layers(mesh, seqs, seq_len, full_width, heads)
        body = by_layers() if fast else per_device
        return jax.shard_map(
            body, mesh=mesh, in_specs=in_specs, out_specs=out_specs, check_vma=False
        )(*args)

    return program
```

```python
import functools
import math

import jax
import jax.numpy as jnp
from jax import lax
from jax.experimental import pallas as pl
from jax.experimental.pallas import tpu as pltpu
from jax.sharding import PartitionSpec as P

HD = 64
MICRO = 4


EPSILON = 1e-06
MASKED = -1e30


def rope_tables(positions, head_size):
    half_size = head_size // 2
    exponent = jnp.arange(half_size, dtype=jnp.float32) * (2.0 / head_size)
    frequency = jnp.exp(exponent * -jnp.log(jnp.float32(10000.0)))
    angles = positions.astype(jnp.float32)[:, None] * frequency[None, :]
    angles = jnp.concatenate([angles, angles], axis=1)
    return (jnp.cos(angles), jnp.sin(angles))


def rotate(vectors, cos_table, sin_table):
    half_size = vectors.shape[-1] // 2
    turned = jnp.concatenate([-vectors[..., half_size:], vectors[..., :half_size]], axis=-1)
    return vectors * cos_table + turned * sin_table


def unrotate(gradient, cos_table, sin_table):
    half_size = gradient.shape[-1] // 2
    scaled = gradient * sin_table
    turned = jnp.concatenate([scaled[..., half_size:], -scaled[..., :half_size]], axis=-1)
    return gradient * cos_table + turned


def swiglu(gate_up):
    return jax.nn.silu(gate_up[:, 0]) * gate_up[:, 1]


def contract_rows(former, latter):
    return lax.dot_general(
        former, latter, (((0,), (0,)), ((), ())), preferred_element_type=jnp.float32
    )


def contract_last(former, latter):
    return lax.dot_general(
        former, latter, (((1,), (1,)), ((), ())), preferred_element_type=jnp.float32
    )


def gather_weights(qkv_weight, out_weight, gate_up_weight, down_weight):
    return (
        lax.all_gather(qkv_weight, ("dp", "ffn"), axis=0, tiled=True),
        lax.all_gather(out_weight, ("dp", "ffn"), axis=1, tiled=True),
        lax.all_gather(gate_up_weight, ("dp", "ffn"), axis=0, tiled=True),
        lax.all_gather(down_weight, ("dp", "ffn"), axis=1, tiled=True),
    )


def row_total(values):
    return lax.psum(values, "head")


def spread_rows(values):
    return lax.all_gather(values, "head", axis=1, tiled=True)


def spread_grads(values):
    return lax.all_gather(values, "head", axis=1, tiled=True)


def collect_rows(values):
    return lax.psum_scatter(
        values.astype(jnp.bfloat16), "head", scatter_dimension=1, tiled=True
    ).astype(jnp.float32)


def collect_grads(values):
    return lax.psum_scatter(
        values.astype(jnp.bfloat16), "head", scatter_dimension=1, tiled=True
    ).astype(jnp.float32)


def norm_forward(values, gain_vector, full_width):
    factor = lax.rsqrt(row_total(jnp.sum(values * values, axis=1)) / full_width + EPSILON)
    return (factor, values * factor[:, None] * gain_vector)


def norm_backward(values, factor, gain_vector, gradient, full_width):
    weighted = gradient * gain_vector
    row_inner = row_total(jnp.sum(weighted * values, axis=1))
    norm_grad = (
        factor[:, None] * weighted
        - values * (factor * factor * factor * row_inner / full_width)[:, None]
    )
    gain_grad = jnp.sum(gradient * values * factor[:, None], axis=0)
    return (norm_grad, gain_grad)


def masked_scores(queries, key_rows, query_places, key_places, query_ids, key_ids, score_scale):
    scores = (
        jnp.einsum("qhd,khd->hqk", queries, key_rows, preferred_element_type=jnp.float32)
        * score_scale
    )
    allowed = (key_places[None, :] <= query_places[:, None]) & (
        key_ids[None, :] == query_ids[:, None]
    )
    return jnp.where(allowed[None], scores, MASKED)


def attend_forward(
    queries, key_rows, value_rows, query_places, key_places, query_ids, key_ids, score_scale
):
    scores = masked_scores(
        queries, key_rows, query_places, key_places, query_ids, key_ids, score_scale
    )
    highest = jnp.max(scores, axis=2, keepdims=True)
    log_total = highest + jnp.log(jnp.sum(jnp.exp(scores - highest), axis=2, keepdims=True))
    weights = jnp.exp(scores - log_total).astype(jnp.bfloat16)
    attended = jnp.einsum("hqk,khd->qhd", weights, value_rows, preferred_element_type=jnp.float32)
    return (attended, log_total[:, :, 0])


def query_side(
    queries,
    key_rows,
    value_rows,
    grad_rows,
    log_total,
    query_places,
    key_places,
    query_ids,
    key_ids,
    score_scale,
):
    scores = masked_scores(
        queries, key_rows, query_places, key_places, query_ids, key_ids, score_scale
    )
    weights = jnp.exp(scores - log_total[:, :, None])
    weight_grad = jnp.einsum(
        "qhd,khd->hqk", grad_rows, value_rows, preferred_element_type=jnp.float32
    )
    row_inner = jnp.sum(weights * weight_grad, axis=2)
    score_grad = (weights * (weight_grad - row_inner[:, :, None])).astype(jnp.bfloat16)
    query_grad = (
        jnp.einsum("hqk,khd->qhd", score_grad, key_rows, preferred_element_type=jnp.float32)
        * score_scale
    )
    return (weights, score_grad, row_inner, query_grad)


def per_device(
    tokens,
    first_values,
    segment_ids,
    cotangent,
    qkv_weight,
    out_weight,
    gate_up_weight,
    down_weight,
    attn_gain,
    mlp_gain,
):
    seq_total = tokens.shape[0]
    local_len = tokens.shape[1]
    local_width = tokens.shape[2]
    full_width = local_width * lax.axis_size("head")
    seq_len = local_len * lax.axis_size("ffn")
    head_width = first_values.shape[2]
    head_local = head_width // HD
    hidden_local = down_weight.shape[0]
    score_scale = 1.0 / math.sqrt(HD)
    offset = lax.axis_index("ffn") * local_len
    own_places = offset + jnp.arange(local_len, dtype=jnp.int32)
    all_places = jnp.arange(seq_len, dtype=jnp.int32)
    cos_table, sin_table = rope_tables(own_places, HD)
    cos_table = cos_table[:, None, :]
    sin_table = sin_table[:, None, :]
    base_count = seq_total // MICRO
    remainder = seq_total % MICRO
    qkv_grads = jnp.zeros((full_width, 3, head_width), jnp.float32)
    out_grads = jnp.zeros((head_width, full_width), jnp.float32)
    gate_grads = jnp.zeros((full_width, 2, hidden_local), jnp.float32)
    down_grads = jnp.zeros((hidden_local, full_width), jnp.float32)
    attn_gain_grads = jnp.zeros((local_width,), jnp.float32)
    mlp_gain_grads = jnp.zeros((local_width,), jnp.float32)
    outputs = []
    token_grads = []
    value_grads = []
    seq_start = 0
    for micro_index in range(MICRO):
        seq_count = base_count + (1 if micro_index < remainder else 0)
        row_count = seq_count * local_len
        gathered = gather_weights(qkv_weight, out_weight, gate_up_weight, down_weight)
        qkv_matrix = gathered[0].reshape(full_width, 3 * head_width)
        out_matrix = gathered[1]
        gate_matrix = gathered[2].reshape(full_width, 2 * hidden_local)
        down_matrix = gathered[3]
        token_rows = (
            tokens[seq_start : seq_start + seq_count]
            .reshape(row_count, local_width)
            .astype(jnp.float32)
        )
        factor_one, normed_one = norm_forward(token_rows, attn_gain, full_width)
        normed_full = spread_rows(normed_one.astype(jnp.bfloat16))
        projected = jnp.dot(normed_full, qkv_matrix, preferred_element_type=jnp.float32)
        projected = projected.reshape(seq_count, local_len, 3, head_local, HD)
        queries = rotate(projected[:, :, 0], cos_table, sin_table).astype(jnp.bfloat16)
        key_local = rotate(projected[:, :, 1], cos_table, sin_table).astype(jnp.bfloat16)
        first_block = first_values[seq_start : seq_start + seq_count].reshape(
            seq_count, local_len, head_local, HD
        )
        value_local = (0.5 * projected[:, :, 2] + 0.5 * first_block.astype(jnp.float32)).astype(
            jnp.bfloat16
        )
        key_full, value_full = (
            lax.all_gather(
                key_local.reshape(seq_count, local_len, head_width), "ffn", axis=1, tiled=True
            ),
            lax.all_gather(
                value_local.reshape(seq_count, local_len, head_width), "ffn", axis=1, tiled=True
            ),
        )
        key_full = key_full.reshape(seq_count, seq_len, head_local, HD)
        value_full = value_full.reshape(seq_count, seq_len, head_local, HD)
        ids_full = segment_ids[seq_start : seq_start + seq_count]
        ids_own = lax.dynamic_slice_in_dim(ids_full, offset, local_len, axis=1)

        def forward_one(pieces):
            return attend_forward(
                pieces[0],
                pieces[1],
                pieces[2],
                own_places,
                all_places,
                pieces[3],
                pieces[4],
                score_scale,
            )

        attended, log_totals = lax.map(
            forward_one, (queries, key_full, value_full, ids_own, ids_full)
        )
        attended_low = attended.reshape(row_count, head_width).astype(jnp.bfloat16)
        branch = collect_rows(jnp.dot(attended_low, out_matrix, preferred_element_type=jnp.float32))
        hidden = token_rows + branch
        factor_two, normed_two = norm_forward(hidden, mlp_gain, full_width)
        normed_mlp = spread_rows(normed_two.astype(jnp.bfloat16))
        gate_up = jnp.dot(normed_mlp, gate_matrix, preferred_element_type=jnp.float32).reshape(
            row_count, 2, hidden_local
        )
        active, swiglu_back = jax.vjp(swiglu, gate_up)
        active_low = active.astype(jnp.bfloat16)
        mlp_branch = collect_rows(
            jnp.dot(active_low, down_matrix, preferred_element_type=jnp.float32)
        )
        outputs.append(
            (hidden + mlp_branch).astype(jnp.bfloat16).reshape(seq_count, local_len, local_width)
        )
        grad_out = cotangent[seq_start : seq_start + seq_count].reshape(row_count, local_width)
        grad_full = spread_grads(grad_out)
        active_grad = contract_last(grad_full, down_matrix)
        down_grads = down_grads + contract_rows(active_low, grad_full)
        gate_grad = (
            swiglu_back(active_grad)[0].astype(jnp.bfloat16).reshape(row_count, 2 * hidden_local)
        )
        gate_grads = gate_grads + contract_rows(normed_mlp, gate_grad).reshape(
            full_width, 2, hidden_local
        )
        normed_grad = collect_grads(contract_last(gate_grad, gate_matrix))
        back_two, gain_two = norm_backward(hidden, factor_two, mlp_gain, normed_grad, full_width)
        mlp_gain_grads = mlp_gain_grads + gain_two
        hidden_grad = grad_out.astype(jnp.float32) + back_two
        hidden_full = spread_grads(hidden_grad.astype(jnp.bfloat16))
        attended_grad = contract_last(hidden_full, out_matrix).astype(jnp.bfloat16)
        out_grads = out_grads + contract_rows(attended_low, hidden_full)
        grad_blocks = attended_grad.reshape(seq_count, local_len, head_local, HD)

        def backward_one(pieces):
            (
                queries_one,
                key_one,
                value_one,
                grad_one,
                total_one,
                own_ids,
                full_ids,
                own_key,
                own_value,
            ) = pieces
            weights, score_grad, row_inner, query_grad = query_side(
                queries_one,
                key_one,
                value_one,
                grad_one,
                total_one,
                own_places,
                all_places,
                own_ids,
                full_ids,
                score_scale,
            )
            key_grad = (
                jnp.einsum(
                    "hqk,qhd->khd", score_grad, queries_one, preferred_element_type=jnp.float32
                )
                * score_scale
            )
            value_grad = jnp.einsum(
                "hqk,qhd->khd",
                weights.astype(jnp.bfloat16),
                grad_one,
                preferred_element_type=jnp.float32,
            )
            key_value = jnp.stack([key_grad, value_grad], axis=1).reshape(seq_len, 2, head_width)
            return (
                query_grad,
                lax.psum_scatter(
                    key_value.astype(jnp.bfloat16), "ffn", scatter_dimension=0, tiled=True
                ).astype(jnp.float32),
            )

        query_grads, key_value_grads = lax.map(
            backward_one,
            (
                queries,
                key_full,
                value_full,
                grad_blocks,
                log_totals,
                ids_own,
                ids_full,
                key_local,
                value_local,
            ),
        )
        key_rot_grad = key_value_grads[:, :, 0].reshape(seq_count, local_len, head_local, HD)
        value_mix_grad = key_value_grads[:, :, 1].reshape(seq_count, local_len, head_local, HD)
        value_grads.append(
            (0.5 * value_mix_grad).astype(jnp.bfloat16).reshape(seq_count, local_len, head_width)
        )
        projected_grad = (
            jnp.stack(
                [
                    unrotate(query_grads, cos_table, sin_table),
                    unrotate(key_rot_grad, cos_table, sin_table),
                    0.5 * value_mix_grad,
                ],
                axis=2,
            )
            .astype(jnp.bfloat16)
            .reshape(row_count, 3 * head_width)
        )
        qkv_grads = qkv_grads + contract_rows(normed_full, projected_grad).reshape(
            full_width, 3, head_width
        )
        normed_grad_one = collect_grads(contract_last(projected_grad, qkv_matrix))
        back_one, gain_one = norm_backward(
            token_rows, factor_one, attn_gain, normed_grad_one, full_width
        )
        attn_gain_grads = attn_gain_grads + gain_one
        token_grads.append(
            (hidden_grad + back_one).astype(jnp.bfloat16).reshape(seq_count, local_len, local_width)
        )
        seq_start = seq_start + seq_count
    weight_sums = (
        lax.psum_scatter(
            qkv_grads.astype(jnp.bfloat16), ("dp", "ffn"), scatter_dimension=0, tiled=True
        ).astype(jnp.float32),
        lax.psum_scatter(
            out_grads.astype(jnp.bfloat16), ("dp", "ffn"), scatter_dimension=1, tiled=True
        ).astype(jnp.float32),
        lax.psum_scatter(
            gate_grads.astype(jnp.bfloat16), ("dp", "ffn"), scatter_dimension=0, tiled=True
        ).astype(jnp.float32),
        lax.psum_scatter(
            down_grads.astype(jnp.bfloat16), ("dp", "ffn"), scatter_dimension=1, tiled=True
        ).astype(jnp.float32),
    )
    gain_sums = lax.psum((attn_gain_grads, mlp_gain_grads), ("dp", "ffn"))
    return (
        jnp.concatenate(outputs, axis=0),
        jnp.concatenate(token_grads, axis=0),
        jnp.concatenate(value_grads, axis=0),
        weight_sums[0],
        weight_sums[1],
        weight_sums[2],
        weight_sums[3],
        gain_sums[0],
        gain_sums[1],
    )


BF16 = jnp.bfloat16
F32 = jnp.float32
BQ = 512
BK = 512
MASKED_SCORE = -1e30


def matmul(former, latter):
    return lax.dot_general(former, latter, (((1,), (0,)), ((), ())), preferred_element_type=F32)


def compiler_params(mib):
    return pltpu.CompilerParams(vmem_limit_bytes=mib * 1024 * 1024)


def exchange(blocks, axes):
    return lax.all_to_all(blocks, axes, 0, 0, tiled=True)


def line_sends(blocks, axis="head"):
    me = lax.axis_index(axis)
    return [
        lax.dynamic_index_in_dim(blocks, me ^ step, 0, keepdims=False)
        for step in range(1, blocks.shape[0])
    ]


def line_go(sends, axis="head"):
    count = len(sends) + 1
    return [
        lax.ppermute(send, axis, [(j, j ^ (step + 1)) for j in range(count)])
        for step, send in enumerate(sends)
    ]


def send_line(blocks, axis="head"):
    return blocks, line_go(line_sends(blocks, axis), axis)


def join_line(blocks, got, axis="head"):
    me = lax.axis_index(axis)
    got = after(*got)
    for step, piece in enumerate(got):
        blocks = lax.dynamic_update_index_in_dim(blocks, piece, me ^ (step + 1), 0)
    return blocks


def exchange_line(blocks, axis="head"):
    return join_line(*send_line(blocks, axis), axis)


def after(values, *earlier):
    return lax.optimization_barrier((values, *earlier))


def send_across(blocks):
    count = blocks.shape[0]
    me = lax.axis_index("ffn")
    got = []
    for step in range(count):
        pairs = []
        for j in range(count * count):
            h, f = divmod(j, count)
            pairs.append((j, (f ^ step) * count + h))
        send = lax.dynamic_index_in_dim(blocks, me ^ step, 0, keepdims=False)
        got.append(lax.ppermute(send, ("head", "ffn"), pairs))
    return got


def join_across(got):
    here = lax.axis_index("head")
    a, b, c, d = after(*got)
    return jnp.where(
        here % 2 == 0,
        jnp.where(here < 2, jnp.stack([a, b, c, d]), jnp.stack([c, d, a, b])),
        jnp.where(here < 2, jnp.stack([b, a, d, c]), jnp.stack([d, c, b, a])),
    )


def in_pieces(values):
    pieces = []
    for _ in range(3):
        piece = lax.reduce_precision(values, 8, 7)
        pieces.append(piece.astype(BF16))
        values = values - piece
    return pieces


def from_pieces(pieces):
    return sum(p.astype(F32) for p in pieces)


def swap(values):
    return lax.ppermute(values, "dp", [(0, 1), (1, 0)])


def swap_halves(values):
    low = (lax.broadcasted_iota(jnp.int32, values.shape, 1) % HD) < HD // 2
    lanes = values.shape[1]
    return jnp.where(
        low, pltpu.roll(values, lanes - HD // 2, 1), pltpu.roll(values, HD // 2, 1)
    )


def norm_kernel(x_ref, gain_ref, main_ref, shared_ref):
    blocks, rows, width = x_ref.shape
    for start in range(0, rows, 256):
        part = pl.ds(start, 256)
        values = [x_ref[b, part, :].astype(F32) for b in range(blocks)]
        total = sum(jnp.sum(v * v, axis=1, keepdims=True) for v in values)
        factor = lax.rsqrt(total / (width * blocks) + EPSILON)
        out_ref, base = main_ref, 0
        if start >= main_ref.shape[1]:
            out_ref, base = shared_ref, main_ref.shape[1]
        for b in range(blocks):
            cols = pl.ds(b * width, width)
            normed = (values[b] * factor * gain_ref[:, cols]).astype(BF16)
            for copy in range(out_ref.shape[0]):
                out_ref[copy, start - base : start - base + 256, cols] = normed


def normalized(x, gain, copies, length):
    shapes = [(copies, r, gain.shape[1]) for r in (length, x.shape[1] - length)]
    return pl.pallas_call(
        norm_kernel,
        grid=(1,),
        out_shape=tuple(jax.ShapeDtypeStruct(s, BF16) for s in shapes),
        in_specs=[once(x.shape), once(gain.shape)],
        out_specs=tuple(once(s) for s in shapes),
        compiler_params=compiler_params(48),
    )(x, gain)


def head_masks():
    lane = lax.broadcasted_iota(jnp.int32, (1, 2 * HD), 1)
    first = jnp.where(lane < HD, 1.0, 0.0).astype(BF16)
    return first, (1.0 - first.astype(F32)).astype(BF16)


def row_chunks(refs, side_ref):
    rows = refs[0].shape[1]
    chunks = []
    for number, ref in enumerate(refs):
        for block in range(ref.shape[0]):
            at = block * rows * len(refs)
            if len(refs) == 2:
                half = side_ref[0] if number == 0 else 1 - side_ref[0]
                at = pl.multiple_of(at + half * rows, rows)
            chunks.append((number, block, pl.ds(at, rows)))
    return chunks


def attend_kernel(count, side_ref, low_ref, *refs):
    n_refs, fv_refs = refs[:count], refs[count : 2 * count]
    w_ref, start_ref, cos_ref, sin_ref, q_ref, k_ref, v_ref, o_ref, lse_ref = refs[2 * count :]
    length = q_ref.shape[0]
    lanes = 2 * HD
    for number, block, rows in row_chunks(n_refs, side_ref):
        made = matmul(n_refs[number][block], w_ref[...])
        cos, sin = cos_ref[rows, :], sin_ref[rows, :]
        q = made[:, :lanes]
        k = made[:, lanes : 2 * lanes]
        q_ref[rows, :] = ((q * cos + swap_halves(q) * sin) * (1.0 / math.sqrt(HD))).astype(BF16)
        k_ref[rows, :] = (k * cos + swap_halves(k) * sin).astype(BF16)
        first = fv_refs[number][block].astype(F32)
        v_ref[rows, :] = (0.5 * made[:, 2 * lanes :] + 0.5 * first).astype(BF16)
    mask_a, mask_b = head_masks()
    lane = lax.broadcasted_iota(jnp.int32, (BQ, lanes), 1)
    for i in range(length // BQ):
        rows = pl.ds(i * BQ, BQ)
        q = q_ref[rows, :]
        both = jnp.concatenate([q * mask_a, q * mask_b], axis=0)
        start = start_ref[rows, :]
        start = jnp.concatenate([start, start], axis=0)
        place = i * BQ + lax.broadcasted_iota(jnp.int32, (BQ, 1), 0)
        place = jnp.concatenate([place, place], axis=0)

        def step(j, carry):
            top, total, acc = carry
            keys = pl.ds(pl.multiple_of(j * BK, BK), BK)
            s = contract_last(both, k_ref[keys, :])
            key = j * BK + lax.broadcasted_iota(jnp.int32, s.shape, 1)
            s = jnp.where((key >= start) & (key <= place), s, MASKED_SCORE)
            new_top = jnp.maximum(top, jnp.max(s, axis=1, keepdims=True))
            p = jnp.exp(s - new_top)
            scale = jnp.exp(top - new_top)
            total = total * scale + jnp.sum(p, axis=1, keepdims=True)
            acc = acc * scale + matmul(p.astype(BF16), v_ref[keys, :])
            return new_top, total, acc

        top, total, acc = lax.fori_loop(
            low_ref[i],
            (i * BQ + BQ - 1) // BK + 1,
            step,
            (
                jnp.full((2 * BQ, 1), MASKED_SCORE, F32),
                jnp.zeros((2 * BQ, 1), F32),
                jnp.zeros((2 * BQ, lanes), F32),
            ),
        )
        acc = acc / total
        lse = top + jnp.log(total)
        o_ref[rows, :] = jnp.where(lane < HD, acc[:BQ], acc[BQ:]).astype(BF16)
        lse_ref[rows, :] = jnp.where(
            lane < HD, jnp.broadcast_to(lse[:BQ], (BQ, lanes)), jnp.broadcast_to(lse[BQ:], (BQ, lanes))
        )


def once(shape, index=None):
    index = (0,) * len(shape) if index is None else index
    return pl.BlockSpec(shape, lambda i: index, pipeline_mode=pl.Buffered(1))


def attend(side, low, normed, weight, firsts, begin, start_col, cos, sin):
    count = len(normed)
    blocks, rows, _ = normed[0].shape
    length = start_col.shape[0]
    lanes = 2 * HD
    small = jax.ShapeDtypeStruct((length, lanes), BF16)
    scalar = pl.BlockSpec(memory_space=pltpu.SMEM)
    return pl.pallas_call(
        functools.partial(attend_kernel, count),
        grid=(1,),
        out_shape=(small, small, small, small, jax.ShapeDtypeStruct((length, lanes), F32)),
        in_specs=[scalar, scalar]
        + [once(n.shape) for n in normed]
        + [once((blocks, rows, lanes), (0, begin // rows, 0))] * count
        + [once(a.shape) for a in (weight, start_col, cos, sin)],
        out_specs=(once((length, lanes)),) * 5,
        compiler_params=compiler_params(48),
    )(side, low, *normed, *firsts, weight, start_col, cos, sin)


def attend_back_kernel(count, side_ref, low_ref, *refs):
    n_refs, do_refs = refs[:count], refs[count : 2 * count]
    w_ref, q_ref, k_ref, v_ref, o_ref, lse_ref, start_ref, cos_ref, sin_ref = refs[
        2 * count : 2 * count + 9
    ]
    dn_refs = refs[2 * count + 9 : 3 * count + 9]
    gw_ref, gfv_ref, dq_ref, dk_ref, dv_ref, dp_ref, do_ref = refs[3 * count + 9 :]
    length = q_ref.shape[0]
    lanes = 2 * HD
    chunks = row_chunks(n_refs, side_ref)
    for number, block, rows in chunks:
        do_ref[rows, :] = do_refs[number][block]
    dk_ref[...] = jnp.zeros_like(dk_ref)
    dv_ref[...] = jnp.zeros_like(dv_ref)
    mask_a, mask_b = head_masks()
    lane = lax.broadcasted_iota(jnp.int32, (BQ, lanes), 1)
    for i in range(length // BQ):
        rows = pl.ds(i * BQ, BQ)
        q, do = q_ref[rows, :], do_ref[rows, :]
        q2 = jnp.concatenate([q * mask_a, q * mask_b], axis=0)
        do2 = jnp.concatenate([do * mask_a, do * mask_b], axis=0)
        lse = jnp.transpose(lse_ref[rows, :])
        lse = jnp.concatenate([lse[0:1, :], lse[HD : HD + 1, :]], axis=1)
        inner = jnp.transpose(do.astype(F32) * o_ref[rows, :].astype(F32))
        inner = jnp.concatenate(
            [
                jnp.sum(inner[:HD], axis=0, keepdims=True),
                jnp.sum(inner[HD:], axis=0, keepdims=True),
            ],
            axis=1,
        )
        start = start_ref[:, rows]
        start = jnp.concatenate([start, start], axis=1)
        place = i * BQ + lax.broadcasted_iota(jnp.int32, (1, BQ), 1)
        place = jnp.concatenate([place, place], axis=1)

        def step(j, acc):
            keys = pl.ds(pl.multiple_of(j * BK, BK), BK)
            k, v = k_ref[keys, :], v_ref[keys, :]
            s = contract_last(k, q2)
            key = j * BK + lax.broadcasted_iota(jnp.int32, s.shape, 0)
            s = jnp.where((key >= start) & (key <= place), s, MASKED_SCORE)
            p = jnp.exp(s - lse)
            dp = contract_last(v, do2)
            ds = (p * (dp - inner)).astype(BF16)
            dv_ref[keys, :] += matmul(p.astype(BF16), do2)
            dk_ref[keys, :] += matmul(ds, q2)
            return acc + contract_rows(ds, k)

        acc = lax.fori_loop(
            low_ref[i], (i * BQ + BQ - 1) // BK + 1, step, jnp.zeros((2 * BQ, lanes), F32)
        )
        dq_ref[rows, :] = jnp.where(lane < HD, acc[:BQ], acc[BQ:]) * (1.0 / math.sqrt(HD))
    for begin in range(0, length, 512):
        rows = pl.ds(begin, 512)
        cos, sin = cos_ref[rows, :], sin_ref[rows, :]
        dq, dk = dq_ref[rows, :], dk_ref[rows, :]
        dv = (0.5 * dv_ref[rows, :]).astype(BF16)
        gfv_ref[rows, :] = dv
        dp_ref[rows, 0:lanes] = (dq * cos - swap_halves(dq) * sin).astype(BF16)
        dp_ref[rows, lanes : 2 * lanes] = (dk * cos - swap_halves(dk) * sin).astype(BF16)
        dp_ref[rows, 2 * lanes :] = dv
    for number, block, rows in chunks:
        part = dp_ref[rows, :]
        dn_refs[number][block] = contract_last(part, w_ref[...]).astype(BF16)
        made = contract_rows(part, n_refs[number][block])
        if number + block == 0:
            gw_ref[...] = made
        else:
            gw_ref[...] += made


def attend_back(side, low, normed, weight, kept, grads, begin, start_row, cos, sin):
    count = len(normed)
    blocks, rows, width = normed[0].shape
    length = start_row.shape[1]
    lanes = 2 * HD
    scalar = pl.BlockSpec(memory_space=pltpu.SMEM)
    return pl.pallas_call(
        functools.partial(attend_back_kernel, count),
        grid=(1,),
        out_shape=tuple(jax.ShapeDtypeStruct(n.shape, BF16) for n in normed)
        + (
            jax.ShapeDtypeStruct((3 * lanes, width), F32),
            jax.ShapeDtypeStruct((length, lanes), BF16),
        ),
        in_specs=[scalar, scalar]
        + [once(n.shape) for n in normed]
        + [once((blocks, rows, lanes), (0, begin // rows, 0))] * count
        + [once(a.shape) for a in (weight, *kept, start_row, cos, sin)],
        out_specs=tuple(once(n.shape) for n in normed)
        + (once((3 * lanes, width)), once((length, lanes))),
        scratch_shapes=[
            pltpu.VMEM((length, lanes), F32),
            pltpu.VMEM((length, lanes), F32),
            pltpu.VMEM((length, lanes), F32),
            pltpu.VMEM((length, 3 * lanes), BF16),
            pltpu.VMEM((length, lanes), BF16),
        ],
        compiler_params=compiler_params(56),
    )(side, low, *normed, *grads, weight, *kept, start_row, cos, sin)


def fill_out_weight(wall_ref, ow_ref):
    groups, depth, high, wide = wall_ref.shape
    for g in range(groups):
        for z in range(depth):
            ow_ref[z * high : (z + 1) * high, g * wide : (g + 1) * wide] = wall_ref[g, z]


def hidden_kernel(
    om_ref, os_ref, x_ref, wall_ref, gain_ref,
    h_ref, n_ref, ob_ref, ow_ref,
):
    fill_out_weight(wall_ref, ow_ref)
    blocks, width = x_ref.shape[0], x_ref.shape[2]
    base = 0
    for o in (om_ref, os_ref):
        rows = o.shape[1]
        for begin in range(0, rows, 256):
            part = pl.ds(begin, 256)
            here = pl.ds(base + begin, 256)
            for b in range(blocks):
                ob_ref[here, b * width : (b + 1) * width] = o[b, part, :]
            branch = matmul(ob_ref[here, :], ow_ref[...])
            total = jnp.zeros((256, 1), F32)
            for b in range(blocks):
                cols = slice(b * width, (b + 1) * width)
                h = x_ref[b, here, :].astype(F32) + branch[:, cols]
                h_ref[here, cols] = h
                total = total + jnp.sum(h * h, axis=1, keepdims=True)
            factor = lax.rsqrt(total / (width * blocks) + EPSILON)
            n_ref[here, :] = (h_ref[here, :] * factor * gain_ref[...]).astype(BF16)
        base += rows


def mlp_kernel(
    begin_tile, hidden, first, down_first,
    n_ref, c_ref, wall_ref, y_ref, dn_ref, grad_ref,
    g_ref, d_ref, nt_ref, act_ref, dgu_ref, dy_ref,
):
    groups, lanes = wall_ref.shape[0], wall_ref.shape[3]
    rows, width = n_ref.shape
    padded = d_ref.shape[0]
    deep = width // groups
    tiles = 2 * padded // lanes
    all_tiles = (down_first - first) // deep // 2

    @pl.when(pl.program_id(0) == 0)
    def _():
        y_ref[...] = jnp.zeros_like(y_ref)
        dn_ref[...] = jnp.zeros_like(dn_ref)
        nt_ref[...] = jnp.transpose(n_ref[...])
        for b in range(c_ref.shape[0]):
            part = c_ref.shape[2]
            dy_ref[:, b * part : (b + 1) * part] = c_ref[b]
        if padded > hidden:
            d_ref[hidden:, :] = jnp.zeros((padded - hidden, width), BF16)

    for g in range(groups):
        for t in range(tiles):
            column = begin_tile + t
            if t >= tiles // 2:
                column += all_tiles - tiles // 2
            at = first + column * deep
            g_ref[g * deep : (g + 1) * deep, t * lanes : (t + 1) * lanes] = wall_ref[
                g, 0, at : at + deep, :
            ]
        at = down_first + begin_tile * lanes
        d_ref[0:hidden, g * lanes : (g + 1) * lanes] = wall_ref[g, 0, at : at + hidden, :]
    for begin in range(0, rows, 256):
        part = pl.ds(begin, 256)
        gu = matmul(n_ref[part, :], g_ref[...])
        gate, up = gu[:, :padded], gu[:, padded:]
        sig = 1.0 / (1.0 + jnp.exp(-gate))
        silu = gate * sig
        act_ref[part, :] = (silu * up).astype(BF16)
        dact = contract_last(dy_ref[part, :], d_ref[...])
        dgu_ref[part, :padded] = (dact * up * sig * (1.0 + gate * (1.0 - sig))).astype(BF16)
        dgu_ref[part, padded:] = (dact * silu).astype(BF16)
        y_ref[part, :] += matmul(act_ref[part, :], d_ref[...])
        dn_ref[part, :] += contract_last(dgu_ref[part, :], g_ref[...])
    for begin in range(0, 2 * padded, 512):
        made = matmul(nt_ref[...], dgu_ref[:, begin : begin + 512]).astype(BF16)
        for g in range(groups):
            for t in range(512 // lanes):
                at = (begin // lanes + t) * deep
                grad_ref[g, 0, at : at + deep, :] = made[
                    g * deep : (g + 1) * deep, t * lanes : (t + 1) * lanes
                ]
    for begin in range(0, width, 512):
        made = contract_rows(act_ref[...], dy_ref[:, begin : begin + 512]).astype(BF16)
        for t in range(512 // lanes):
            grad_ref[begin // lanes + t, 0, tiles * deep :, :] = made[
                :hidden, t * lanes : (t + 1) * lanes
            ]


def hidden_back_kernel(
    h_ref, ya_ref, yb_ref, dna_ref, dnb_ref, c_ref, wall_ref, gain_ref,
    out_ref, dh_ref, dob_ref, low_ref, ggain_ref, ow_ref,
):
    fill_out_weight(wall_ref, ow_ref)
    groups = wall_ref.shape[0]
    blocks, width = out_ref.shape[0], out_ref.shape[2]
    full = width * blocks
    gain = gain_ref[...]
    ggain = jnp.zeros((1, full), F32)
    for begin in range(0, h_ref.shape[0], 256):
        here = pl.ds(begin, 256)
        h = h_ref[here, :]
        factor = lax.rsqrt(jnp.sum(h * h, axis=1, keepdims=True) / full + EPSILON)
        dn = dna_ref[here, :] + dnb_ref[here, :]
        result = (h + (ya_ref[here, :] + yb_ref[here, :])).astype(BF16)
        for b in range(blocks):
            out_ref[b, here, :] = result[:, b * width : (b + 1) * width]
        weighted = dn * gain
        ggain = ggain + jnp.sum(dn * (h * factor), axis=0, keepdims=True)
        row_inner = jnp.sum(weighted * h, axis=1, keepdims=True)
        dh = (
            jnp.concatenate([c_ref[b, here, :] for b in range(blocks)], axis=1).astype(F32)
            + factor * weighted
            - h * (factor * factor * factor * row_inner / full)
        )
        dh_ref[here, :] = dh
        low_ref[here, :] = dh.astype(BF16)
        made = contract_last(low_ref[here, :], ow_ref[...]).astype(BF16)
        for b in range(blocks):
            dob_ref[b, here, :] = made[:, b * width : (b + 1) * width]
    ggain_ref[...] = ggain


def out_grad_kernel(ob_ref, low_ref, gout_ref):
    groups = gout_ref.shape[0]
    high, wide = gout_ref.shape[2], gout_ref.shape[3]
    for z in range(gout_ref.shape[1]):
        made = contract_rows(ob_ref[:, z * high : (z + 1) * high], low_ref[...]).astype(BF16)
        for g in range(groups):
            gout_ref[g, z] = made[:, g * wide : (g + 1) * wide]


def last_kernel(x_ref, dh_ref, parts_ref, gain_ref, out_ref, ggain_ref):
    blocks, width = x_ref.shape[0], x_ref.shape[2]
    full = width * blocks
    ggain_ref[...] = jnp.zeros_like(ggain_ref)
    for begin in range(0, x_ref.shape[1], 256):
        part = pl.ds(begin, 256)
        dn = parts_ref[0, part, :].astype(F32)
        for other in range(1, parts_ref.shape[0]):
            dn = dn + parts_ref[other, part, :].astype(F32)
        weighted = dn * gain_ref[...]
        total = jnp.zeros((256, 1), F32)
        inner = jnp.zeros((256, 1), F32)
        for b in range(blocks):
            cols = slice(b * width, (b + 1) * width)
            value = x_ref[b, part, :].astype(F32)
            total = total + jnp.sum(value * value, axis=1, keepdims=True)
            inner = inner + jnp.sum(weighted[:, cols] * value, axis=1, keepdims=True)
        factor = lax.rsqrt(total / full + EPSILON)
        slope = factor * factor * factor * inner / full
        for b in range(blocks):
            cols = slice(b * width, (b + 1) * width)
            value = x_ref[b, part, :].astype(F32)
            ggain_ref[:, cols] += jnp.sum(dn[:, cols] * value * factor, axis=0, keepdims=True)
            out_ref[b, part, :] = (
                dh_ref[part, cols] + factor * weighted[:, cols] - value * slope
            ).astype(BF16)


def last(base, x, dh, parts, gain):
    rows, full = parts.shape[1], gain.shape[1]
    shape = (x.shape[0], rows, x.shape[2])
    return pl.pallas_call(
        last_kernel,
        grid=(1,),
        out_shape=(jax.ShapeDtypeStruct(shape, BF16), jax.ShapeDtypeStruct((1, full), F32)),
        in_specs=[
            once(shape, (0, base // rows, 0)),
            once((rows, full), (base // rows, 0)),
            once(parts.shape),
            once(gain.shape),
        ],
        out_specs=(once(shape), once((1, full))),
        compiler_params=compiler_params(56),
    )(x, dh, parts, gain)


def by_layers():
    def run(
        tokens,
        first_values,
        segment_ids,
        cotangent,
        qkv_weight,
        out_weight,
        gate_up_weight,
        down_weight,
        attn_gain,
        mlp_gain,
    ):
        dp, z, f = (lax.axis_index(a) for a in ("dp", "head", "ffn"))
        depth, side = lax.axis_size("head"), lax.axis_size("ffn")
        group = 2 * side
        length, width = tokens.shape[1], tokens.shape[2]
        half = length // 2
        full_width = width * depth
        seq_len = length * side
        lanes = 2 * HD
        hidden = down_weight.shape[0]
        padded = -(-hidden // lanes) * lanes
        layer = ("dp", "ffn")
        vmem = pl.BlockSpec(memory_space=pltpu.VMEM)

        def to_layers(values):
            keep = lax.dynamic_slice(values, (depth, dp * half, 0), (2, half, width))
            give = lax.dynamic_slice(values, (depth, (1 - dp) * half, 0), (2, half, width))
            got = swap(give)
            early = jnp.where(dp == 0, keep, got)
            late = jnp.where(dp == 0, got, keep)
            return values[:depth], jnp.stack([early[0], late[0], early[1], late[1]])

        def from_layers(main, shared):
            keep = jnp.where(dp == 0, shared[0::2], shared[1::2])
            got = swap(jnp.where(dp == 0, shared[1::2], shared[0::2]))
            early = jnp.where(dp == 0, keep, got)
            late = jnp.where(dp == 0, got, keep)
            return jnp.concatenate([main, jnp.concatenate([early, late], axis=1)], axis=0)

        other_ids = swap(segment_ids)
        pick = depth + z // 2
        ids = [
            lax.dynamic_index_in_dim(segment_ids, z, 0, keepdims=False),
            lax.dynamic_index_in_dim(other_ids, z, 0, keepdims=False),
            jnp.where(
                z % 2 == dp,
                lax.dynamic_index_in_dim(segment_ids, pick, 0, keepdims=False),
                lax.dynamic_index_in_dim(other_ids, pick, 0, keepdims=False),
            ),
        ]
        ids = jnp.stack(ids)
        numbers = jnp.arange(8, dtype=jnp.int32)[None, :, None]
        lower = jnp.sum((ids[:, None, :] < numbers).astype(jnp.int32), axis=2, keepdims=True)
        starts = jnp.sum(jnp.where(ids[:, None, :] == numbers, lower, 0), axis=1)
        lows = starts[:, ::BQ] // BK

        places = jnp.arange(seq_len, dtype=jnp.int32)
        cos, sin = rope_tables(places, HD)
        cos = jnp.concatenate([cos, cos], axis=1)
        sin = jnp.concatenate([-sin[:, : HD // 2], sin[:, HD // 2 :]], axis=1)
        sin = jnp.concatenate([sin, sin], axis=1)

        out_rows = out_weight.shape[0]
        def in_tiles(values):
            values = jnp.pad(values, ((0, 0), (0, padded - hidden)))
            return values.reshape(-1, padded // lanes, lanes).transpose(1, 0, 2).reshape(-1, lanes)

        wall = jnp.concatenate(
            [out_weight, in_tiles(gate_up_weight[:, 0]), in_tiles(gate_up_weight[:, 1]), down_weight],
            axis=0,
        )
        deep = qkv_weight.shape[0]
        part = qkv_weight.reshape(deep, 3, 2, lanes).transpose(2, 1, 0, 3).reshape(-1, lanes)
        pieces = in_pieces(jnp.concatenate([attn_gain, mlp_gain]).reshape(-1, lanes))
        tail = jnp.concatenate(pieces + [jnp.zeros((4, lanes), BF16)], axis=0)
        part = jnp.concatenate([part, tail], axis=0)
        part = exchange(jnp.broadcast_to(part[None], (depth,) + part.shape), "head")
        tail = part[:, 6 * deep :].astype(F32)
        step = 2 * width // lanes
        gains = tail[:, :step] + tail[:, step : 2 * step] + tail[:, 2 * step : 3 * step]
        gains = gains.reshape(depth, 2, width).transpose(1, 0, 2).reshape(2, 1, full_width)
        part = part[:, : 6 * deep].reshape(depth, 2, 3, deep, lanes)
        part = part.transpose(1, 0, 2, 3, 4).reshape(group, 3, deep, lanes)
        part = exchange(part, layer)
        weight = part.transpose(0, 2, 1, 3).reshape(group * deep, 3 * lanes)

        x, x_got = send_line(jnp.concatenate(to_layers(tokens), axis=1))
        x_got, weight, cos, sin, starts = after(x_got, weight, cos, sin, starts)
        lows = starts[:, ::BQ] // BK
        x = join_line(x, x_got)
        first = jnp.concatenate(to_layers(first_values), axis=1)
        first, x = after(first, x)
        first_got = send_across(first)
        nm, ns = normalized(x, gains[0], side, length)
        wall, nm = after(wall, nm)
        wall = lax.all_gather(wall, ("dp", "ffn", "head"), axis=0, tiled=False)
        wall = wall.reshape(group, depth, wall.shape[1], lanes)
        nm = exchange(nm, "ffn")
        grad_blocks = jnp.concatenate(to_layers(cotangent), axis=1)
        grad_sends = line_sends(grad_blocks)
        nm, grad_blocks, grad_sends = after(nm, grad_blocks, grad_sends)
        first_got, ns, nm = after(first_got, ns, nm)
        first = join_across(first_got)

        def pair_halves(blocks):
            mine = lax.dynamic_slice_in_dim(blocks, dp * lanes, lanes, axis=2)
            return mine, swap(lax.dynamic_slice_in_dim(blocks, (1 - dp) * lanes, lanes, axis=2))

        def pair_join(mine, theirs):
            return lane_join(mine, swap(theirs))

        def lane_join(mine, got):
            return jnp.where(
                dp == 0,
                jnp.concatenate([mine, got], axis=2),
                jnp.concatenate([got, mine], axis=2),
            )

        def by_core(shared):
            shared = shared.reshape(side, 2, half, lanes)
            return (
                lax.dynamic_index_in_dim(shared, dp, 1, keepdims=False),
                lax.dynamic_index_in_dim(shared, 1 - dp, 1, keepdims=False),
            )

        first_mine, first_got = pair_halves(first)
        firsts = [(first_mine,), (first_got,), (first_mine, first_got)]
        core = dp.astype(jnp.int32).reshape(1)
        def attend_at(i, rows_in):
            return attend(
                core,
                lows[i],
                rows_in,
                weight,
                firsts[i],
                length if i == 2 else 0,
                starts[i][:, None],
                cos,
                sin,
            )

        ns = exchange(ns, "ffn")
        nm_other = swap(nm)
        kept = [attend_at(0, (nm,))]
        nm_other, ns, grad_sends, kept[0] = after(nm_other, ns, grad_sends, kept[0])
        grad_got = line_go(grad_sends)
        ns_other = swap(ns)
        kept.append(attend_at(1, (nm_other,)))
        ns_other, grad_got[0], kept[1] = after(ns_other, grad_got[0], kept[1])
        om = pair_join(
            kept[0][3].reshape(side, length, lanes), kept[1][3].reshape(side, length, lanes)
        )
        ns_other, om = after(ns_other, om)
        kept.append(attend_at(2, (ns, ns_other)))
        normed = [(nm,), (nm_other,), (ns, ns_other)]
        om = exchange(om, "ffn")
        om, grad_got[1], kept[2] = after(om, grad_got[1], kept[2])
        os_, om = after(pair_join(*by_core(kept[2][3])), om)
        os_ = exchange(os_, "ffn")

        rows = length + half
        whole = jax.ShapeDtypeStruct((rows, full_width), F32)
        whole_low = jax.ShapeDtypeStruct((rows, full_width), BF16)
        out_spec = pl.BlockSpec((group, depth, out_rows, lanes), lambda i: (0, 0, 0, 0))

        def fixed(shape):
            return pl.BlockSpec(
                shape, lambda i: (0,) * len(shape), pipeline_mode=pl.Buffered(1)
            )

        ow_scratch = pltpu.VMEM((out_rows * depth, group * lanes), BF16)
        h, n2, ob = pl.pallas_call(
            hidden_kernel,
            grid=(1,),
            out_shape=(whole, whole_low, whole_low),
            in_specs=[fixed(a.shape) for a in (om, os_, x)]
            + [out_spec, fixed((1, full_width))],
            out_specs=tuple(fixed((rows, full_width)) for _ in range(3)),
            scratch_shapes=[ow_scratch],
            compiler_params=compiler_params(56),
        )(om, os_, x, wall, gains[1])
        grad_got, n2 = after(grad_got, n2)
        grad_blocks = join_line(grad_blocks, grad_got)

        high = wall.shape[2]
        count = padded // lanes

        def feed_forward(begin_tile, end_tile):
            wide = (end_tile - begin_tile) * lanes
            real = min(hidden, end_tile * lanes) - begin_tile * lanes
            grad_rows = 2 * (end_tile - begin_tile) * deep + real
            return pl.pallas_call(
                functools.partial(
                    mlp_kernel, begin_tile, real, out_rows, out_rows + 2 * count * deep
                ),
                grid=(depth,),
                out_shape=(
                    whole,
                    whole,
                    jax.ShapeDtypeStruct((group, depth, grad_rows, lanes), BF16),
                ),
                in_specs=[
                    fixed((rows, full_width)),
                    fixed((depth, rows, width)),
                    pl.BlockSpec((group, 1, high, lanes), lambda i: (0, i, 0, 0)),
                ],
                out_specs=(
                    fixed((rows, full_width)),
                    fixed((rows, full_width)),
                    pl.BlockSpec((group, 1, grad_rows, lanes), lambda i: (0, i, 0, 0)),
                ),
                scratch_shapes=[
                    pltpu.VMEM((full_width, 2 * wide), BF16),
                    pltpu.VMEM((wide, full_width), BF16),
                    pltpu.VMEM((full_width, rows), BF16),
                    pltpu.VMEM((rows, wide), BF16),
                    pltpu.VMEM((rows, 2 * wide), BF16),
                    pltpu.VMEM((rows, full_width), BF16),
                ],
                compiler_params=compiler_params(60),
            )(n2, grad_blocks, wall)

        ya, dna, grads_a = feed_forward(count - 2, count)
        n2, ya = after(n2, ya)
        yb, dnb, grads_b = feed_forward(0, count - 2)

        def layer_sum(grads):
            shape = grads.shape[1:]
            return lax.psum_scatter(grads, layer, scatter_dimension=0, tiled=True).reshape(shape)

        grads_a = layer_sum(grads_a)
        grads_b = layer_sum(grads_b)

        out, dh, dob, low, gain_two = pl.pallas_call(
            hidden_back_kernel,
            grid=(1,),
            out_shape=(
                jax.ShapeDtypeStruct(grad_blocks.shape, BF16),
                whole,
                jax.ShapeDtypeStruct(grad_blocks.shape, BF16),
                whole_low,
                jax.ShapeDtypeStruct((1, full_width), F32),
            ),
            in_specs=[fixed((rows, full_width))] * 5
            + [fixed(grad_blocks.shape), out_spec, fixed((1, full_width))],
            out_specs=tuple(
                fixed(s)
                for s in (
                    grad_blocks.shape,
                    (rows, full_width),
                    grad_blocks.shape,
                    (rows, full_width),
                    (1, full_width),
                )
            ),
            scratch_shapes=[ow_scratch],
            compiler_params=compiler_params(60),
        )(h, ya, yb, dna, dnb, grad_blocks, wall, gains[1])

        low, dob = after(low, dob)
        dob = exchange(dob, "ffn")
        gout_shape = (group, depth, out_rows, lanes)
        gout = pl.pallas_call(
            out_grad_kernel,
            grid=(1,),
            out_shape=jax.ShapeDtypeStruct(gout_shape, BF16),
            in_specs=[fixed((rows, full_width))] * 2,
            out_specs=fixed(gout_shape),
            compiler_params=compiler_params(48),
        )(ob, low)
        dob, gout = after(dob, gout)
        do_mine, do_got = pair_halves(dob)

        def back_of(i, grads_in):
            return attend_back(
                core,
                lows[i],
                normed[i],
                weight,
                kept[i],
                grads_in,
                length if i == 2 else 0,
                starts[i][None],
                cos,
                sin,
            )

        out, out_got = send_line(out)
        do_got, gout = after(do_got, gout)
        gout = exchange(gout, layer)
        dn_b, gw_b, gfv_b = back_of(1, (do_got,))
        dn_b, gw_b, gfv_b, out_got[0], out_got[1] = after(
            dn_b, gw_b, gfv_b, out_got[0], out_got[1]
        )
        do_mine, dn_b, gfv_b, grads_a = after(do_mine, dn_b, gfv_b, grads_a)
        grads_a, a_got = send_line(grads_a)
        dn_other = swap(dn_b)
        dn_a, gw_a, gfv_a = back_of(0, (do_mine,))
        dn_a, gw_a, gfv_a, dn_other, a_got, out_got[2], gout = after(
            dn_a, gw_a, gfv_a, dn_other, a_got, out_got[2], gout
        )
        gfv_other = swap(gfv_b)
        grads_a = join_line(grads_a, a_got)

        def add_low(mine, theirs):
            return (mine.astype(F32) + theirs.astype(F32)).astype(BF16)

        main_sum = add_low(dn_a, dn_other)
        out = join_line(out, out_got)
        gfv_main = lane_join(
            gfv_a.reshape(side, length, lanes), gfv_other.reshape(side, length, lanes)
        )
        gout = exchange_line(jnp.sum(gout.astype(F32), axis=0).astype(BF16))
        do_mine, main_sum, gout = after(do_mine, main_sum, gout)
        main_sum = exchange(main_sum, "ffn")
        dn_s, dn_t, gw_s, gfv_s = back_of(2, (do_mine, do_got))
        grads_b, dn_s, dn_t, gw_s, gfv_s = after(grads_b, dn_s, dn_t, gw_s, gfv_s)
        grads_b, b_got = send_line(grads_b)
        dn_t = swap(dn_t)
        shared_sum, main_sum, b_got[0], b_got[1] = after(
            add_low(dn_s, dn_t), main_sum, b_got[0], b_got[1]
        )
        shared_sum = exchange(shared_sum, "ffn")
        tokm, gain_main = last(0, x, dh, main_sum, gains[0])
        tokm, b_got[2], gfv_s, gw_s, gfv_main, shared_sum = after(
            tokm, b_got[2], gfv_s, gw_s, gfv_main, shared_sum
        )
        tokm, tokm_got = send_line(tokm)
        gfv_mine, gfv_theirs = by_core(gfv_s)
        gfv = lane_join(gfv_mine, swap(gfv_theirs))
        gfv = exchange(jnp.concatenate([gfv_main, gfv], axis=1), "ffn")
        toks, gain_shared = last(length, x, dh, shared_sum, gains[0])
        grad_w = (gw_a + gw_b + gw_s).astype(BF16)
        grad_w = grad_w.reshape(3, lanes, group, deep).transpose(2, 0, 3, 1)
        grad_w = grad_w.reshape(group, 3 * deep, lanes)
        gain_both = jnp.concatenate([gain_main + gain_shared, gain_two]).reshape(-1, lanes)
        gain_rows = gain_both.shape[0]
        tail = jnp.concatenate(in_pieces(gain_both), axis=0)
        tail = jnp.broadcast_to(tail[None], (group,) + tail.shape)
        grad_w = jnp.concatenate([grad_w, tail], axis=1)
        toks, tokm_got = after(toks, tokm_got)
        toks, toks_got = send_line(toks)
        grad_w, gfv = after(grad_w, gfv)
        grad_w = exchange(grad_w, layer)
        gfv, toks_got = after(gfv, toks_got)
        gfv, gfv_got = send_line(gfv)
        tail = grad_w[:, 3 * deep :].astype(F32).reshape(group, 3, gain_rows, lanes)
        tail = jnp.sum(tail, axis=(0, 1)).reshape(2, depth, -1, lanes).transpose(1, 0, 2, 3)
        tail = jnp.concatenate(in_pieces(tail.reshape(depth, -1, lanes)), axis=1)
        grad_w = grad_w[:, : 3 * deep].reshape(2, side, 3, deep, lanes)
        grad_w = grad_w.transpose(1, 2, 0, 3, 4).reshape(depth, 6 * deep, lanes)
        grad_w, w_got = send_line(jnp.concatenate([grad_w, tail], axis=1))
        out_tokens = from_layers(out[:, :length], out[:, length:])
        grads_b = join_line(grads_b, b_got)
        token_grads = from_layers(join_line(tokm, tokm_got), join_line(toks, toks_got))
        grad_out = jnp.sum(gout.astype(F32), axis=0)

        def untile(values):
            return values.reshape(-1, deep, lanes).transpose(1, 0, 2).reshape(deep, -1)

        gates, ups, downs = [], [], []
        for grads, tiles_in in ((grads_b, count - 2), (grads_a, 2)):
            part = jnp.sum(grads.astype(F32), axis=0)
            gates.append(untile(part[: tiles_in * deep]))
            ups.append(untile(part[tiles_in * deep : 2 * tiles_in * deep]))
            downs.append(part[2 * tiles_in * deep :])
        grad_gate = jnp.stack(
            [jnp.concatenate(g, axis=1)[:, :hidden] for g in (gates, ups)], axis=1
        )
        grad_down = jnp.concatenate(downs, axis=0)
        gfv_got, w_got, grad_gate, grad_down, grad_out, out_tokens, token_grads = after(
            gfv_got, w_got, grad_gate, grad_down, grad_out, out_tokens, token_grads
        )
        grad_w = join_line(grad_w, w_got)
        tail = jnp.sum(grad_w[:, 6 * deep :].astype(F32).reshape(depth, 3, 2, width), axis=(0, 1))
        grad_qkv = jnp.sum(grad_w[:, : 6 * deep].astype(F32), axis=0).reshape(3, 2, deep, lanes)
        grad_qkv = grad_qkv.transpose(2, 0, 1, 3).reshape(deep, 3, width)
        gfv = join_line(gfv, gfv_got)
        value_grads = from_layers(gfv[:, :length], gfv[:, length:])

        return (
            out_tokens,
            token_grads,
            value_grads,
            grad_qkv,
            grad_out,
            grad_gate,
            grad_down,
            tail[0],
            tail[1],
        )

    return run


def fits_layers(mesh, seqs, seq_len, full_width, heads):
    sizes = dict(mesh.shape)
    return (
        sizes["dp"] == 2
        and sizes["head"] == 4
        and sizes["ffn"] == 4
        and seqs == 12
        and seq_len % (512 * 4) == 0
        and full_width == 1024
        and heads == 16
    )


def solution(mesh):
    in_specs = (
        P("dp", "ffn", "head"),
        P("dp", "ffn", "head"),
        P("dp", None),
        P("dp", "ffn", "head"),
        P(("dp", "ffn"), None, "head"),
        P("head", ("dp", "ffn")),
        P(("dp", "ffn"), None, "head"),
        P("head", ("dp", "ffn")),
        P("head"),
        P("head"),
    )
    out_specs = (
        P("dp", "ffn", "head"),
        P("dp", "ffn", "head"),
        P("dp", "ffn", "head"),
        P(("dp", "ffn"), None, "head"),
        P("head", ("dp", "ffn")),
        P(("dp", "ffn"), None, "head"),
        P("head", ("dp", "ffn")),
        P("head"),
        P("head"),
    )

    def program(*args):
        seqs, seq_len, full_width = args[0].shape
        heads = args[5].shape[0] // HD
        fast = fits_layers(mesh, seqs, seq_len, full_width, heads)
        body = by_layers() if fast else per_device
        return jax.shard_map(
            body, mesh=mesh, in_specs=in_specs, out_specs=out_specs, check_vma=False
        )(*args)

    return program
```
